512 devices in a mesh: gx: 8 (over x, core), gy: 4 (over z_hi), gz: 16 (over z_lo, y).
Axes of the slice: x: 4, y: 8, z: 8 (z_hi: 4, z_lo: 2; z = z_hi * 2 + z_lo), core: 2. Of those that a mesh axis runs over, the one named last changes fastest.
Arguments:
- density: float32 [16, 32, 96, 1024], P('gz', 'gy', None, 'gx'), may hold values from 0.2 to 1
- bone: int32 [16, 32, 96, 1024], P('gz', 'gy', None, 'gx'), may hold values 0 or 1
- fixed: int32 [16, 32, 96, 1024], P('gz', 'gy', None, 'gx'), may hold values 0 or 1
- load: float32 [3, 16, 32, 96, 1024], P(None, 'gz', 'gy', None, 'gx'), may hold values from -6 to 6
Outputs:
- density_new: float32 [16, 32, 96, 1024], P('gz', 'gy', None, 'gx')
- displacement: float32 [3, 16, 32, 96, 1024], P(None, 'gz', 'gy', None, 'gx')
The draws below stay inside these ranges and needn't reach their ends.
All inputs are finite; a program needn't handle non-finite values. No bound on the sum of `bone` or of `fixed` on one device may be relied on, other than what follows from the above.
Results may differ from the reference program's by a relative error of at most 0.00024.
Values sent between devices are 32-bit elements; how exact they have to be, the bound alone decides.
A program may use at most 64 MiB of HBM per device.

```python
import math
import jax
import jax.numpy as jnp
import numpy as np
from jax import lax

ZB = 32
RAD = 24
ITERS = 2
NX = 1024
NY = 96
NZ = 512
N_GZ = 16


def draw_load(key, part):
    noise = jax.random.normal(key, (3, N_GZ, ZB, NY, NX), jnp.float32)
    traction = jnp.array([1.0, 0.0, 0.0], jnp.float32)
    return jnp.clip(noise + traction[:, None, None, None, None], -6.0, 6.0)


def plant(entries, own_key, smallest, top_value):
    extent = entries.shape
    spot = [jax.random.randint(jax.random.fold_in(own_key, axis), (), 0, extent[axis]) for axis in range(len(extent))]
    entries = entries.at[tuple(spot)].set(smallest)
    longest = extent.index(max(extent))
    spot[longest] = (spot[longest] + 1) % extent[longest]
    return entries.at[tuple(spot)].set(top_value)


def block_scale(rng, dims, split, least, high):
    gain, own = 1.0, jax.random.fold_in(rng, 6)
    for position, shards_of in split:
        heights = jnp.exp(jax.random.uniform(jax.random.fold_in(own, position), (shards_of,), jnp.float32, least / len(split), high / len(split)))
        gain = gain * jnp.repeat(heights, dims[position] // shards_of).reshape([-1 if axis == position else 1 for axis in range(len(dims))])
    return gain


def setup_inputs(seed: int = 0) -> dict:
    seeds = jax.random.split(jax.random.key(seed), 5)
    density = jnp.clip(0.2 + 0.8 * jax.random.uniform(seeds[0], (N_GZ, ZB, NY, NX), jnp.float32) ** block_scale(seeds[0], (N_GZ, ZB, NY, NX), ((0, 16), (1, 4), (3, 8)), -0.2, 0.2), 0.2, 1.0)
    bone = plant((jax.random.randint(seeds[1], (N_GZ, ZB, NY, NX), 0, 5) < 3).astype(jnp.int32), jax.random.fold_in(seeds[1], 1), 0, 1)
    fixed = plant((jax.random.randint(seeds[2], (N_GZ, ZB, NY, NX), 0, 16) < 1).astype(jnp.int32), jax.random.fold_in(seeds[2], 1), 0, 1)
    load = draw_load(jax.random.fold_in(seeds[4], 71), 0)
    return {"density": density, "bone": bone, "fixed": fixed, "load": load}


MARROW = 0.1
REMODEL = 0.25
FLOOR = 0.2
CEILING = 1.0
EPSILON = 1e-06

def element_stiffness():
    poisson = 0.3
    lame = poisson / ((1.0 + poisson) * (1.0 - 2.0 * poisson))
    shear = 0.5 / (1.0 + poisson)
    elastic = np.zeros((6, 6))
    elastic[:3, :3] = lame
    for index in range(3):
        elastic[index, index] += 2.0 * shear
        elastic[index + 3, index + 3] = shear
    points = [0.5 - 0.5 / math.sqrt(3.0), 0.5 + 0.5 / math.sqrt(3.0)]
    matrix = np.zeros((24, 24))
    for point_z in points:
        for point_y in points:
            for point_x in points:
                strain = np.zeros((6, 24))
                for corner_z in range(2):
                    for corner_y in range(2):
                        for corner_x in range(2):
                            node = 4 * corner_z + 2 * corner_y + corner_x
                            shape_x = point_x if corner_x else 1.0 - point_x
                            shape_y = point_y if corner_y else 1.0 - point_y
                            shape_z = point_z if corner_z else 1.0 - point_z
                            slope_x = 1.0 if corner_x else -1.0
                            slope_y = 1.0 if corner_y else -1.0
                            slope_z = 1.0 if corner_z else -1.0
                            along_x = slope_x * shape_y * shape_z
                            along_y = shape_x * slope_y * shape_z
                            along_z = shape_x * shape_y * slope_z
                            strain[0, node] = along_x
                            strain[1, 8 + node] = along_y
                            strain[2, 16 + node] = along_z
                            strain[3, node] = along_y
                            strain[3, 8 + node] = along_x
                            strain[4, 8 + node] = along_z
                            strain[4, 16 + node] = along_y
                            strain[5, node] = along_z
                            strain[5, 16 + node] = along_x
                matrix = matrix + strain.T @ elastic @ strain / 8.0
    return matrix

def corners():
    return [(corner_z, corner_y, corner_x) for corner_z in range(2) for corner_y in range(2) for corner_x in range(2)]

def gathered_forces(nodes, moduli, stiffness):
    depth, rows, width = moduli.shape
    height = rows - 1
    columns = jnp.stack([nodes[:, cz:cz + depth, cy:cy + rows, cx:cx + width] for cz, cy, cx in corners()], axis=1)
    product = jnp.dot(stiffness, columns.reshape(24, -1), precision=lax.Precision.HIGHEST)
    product = product.reshape(3, 8, depth, rows, width) * moduli
    product = jnp.pad(product, ((0, 0), (0, 0), (1, 1), (0, 0), (1, 1)))
    total = jnp.zeros((3, depth + 1, height, width + 1), jnp.float32)
    for node, (cz, cy, cx) in enumerate(corners()):
        total = total + product[:, node, 1 - cz:2 - cz + depth, 1 - cy:1 - cy + height, 1 - cx:2 - cx + width]
    return total

def element_energy(nodes, moduli, stiffness):
    depth, height, width = moduli.shape
    columns = jnp.stack([nodes[:, cz:cz + depth, cy:cy + height, cx:cx + width] for cz, cy, cx in corners()], axis=1)
    columns = columns.reshape(24, -1)
    product = jnp.dot(stiffness, columns, precision=lax.Precision.HIGHEST)
    return 0.5 * moduli * lax.optimization_barrier(jnp.sum(columns * product, axis=0)).reshape(depth, height, width)

def stiffness_diagonal(moduli_ext, stiffness, depth, height, width):
    main = jnp.diagonal(stiffness).reshape(3, 8)
    total = jnp.zeros((3, depth, height, width), jnp.float32)
    for node, (cz, cy, cx) in enumerate(corners()):
        piece = moduli_ext[1 - cz:1 - cz + depth, 1 - cy:1 - cy + height, 1 - cx:1 - cx + width]
        total = total + main[:, node][:, None, None, None] * piece[None]
    return total

def taps(radius):
    offsets = jnp.arange(2 * radius + 1).astype(jnp.float32) - radius
    raw = jnp.exp(-jnp.abs(offsets) / (0.5 * radius))
    return raw / jnp.sum(raw)

def smooth_reference(values, axis):
    weights = taps(RAD)
    length = values.shape[axis]
    widths = [(0, 0), (0, 0), (0, 0)]
    widths[axis] = (RAD, RAD)
    padded = jnp.pad(values, widths)
    total = jnp.zeros(values.shape, jnp.float32)
    for index in range(2 * RAD + 1):
        total = total + weights[index] * lax.slice_in_dim(padded, index, index + length, axis=axis)
    return total

def reference(density, bone, fixed, load):
    stiffness = jnp.asarray(element_stiffness(), jnp.float32)
    grid_density = density.reshape(NZ, NY, NX)
    bone_share = bone.reshape(NZ, NY, NX).astype(jnp.float32)
    free_nodes = 1.0 - fixed.reshape(NZ, NY, NX).astype(jnp.float32)
    modulus = bone_share * grid_density * grid_density + (1.0 - bone_share) * MARROW
    moduli_padded = jnp.pad(modulus, ((0, 0), (1, 0), (0, 0)))
    diagonal_full = stiffness_diagonal(jnp.pad(modulus, ((1, 0), (1, 0), (1, 0))), stiffness, NZ, NY, NX)
    precondition = free_nodes / diagonal_full
    starts = jnp.arange(N_GZ).astype(jnp.int32) * ZB

    def operate(field):
        nodes = jnp.pad(free_nodes * field, ((0, 0), (0, 1), (1, 1), (0, 1)))

        def one_block(start):
            block_nodes = lax.dynamic_slice_in_dim(nodes, start, ZB + 1, 1)
            block_moduli = lax.dynamic_slice_in_dim(moduli_padded, start, ZB, 0)
            return gathered_forces(block_nodes, block_moduli, stiffness)
        blocks = lax.map(one_block, starts)
        own = blocks[:, :, :ZB, :, :NX]
        tops = blocks[:, :, ZB:, :, :NX]
        carried = jnp.concatenate([jnp.zeros_like(tops[:1]), tops[:-1]], axis=0)
        own = jnp.concatenate([own[:, :, :1] + carried, own[:, :, 1:]], axis=2)
        return free_nodes * jnp.moveaxis(own, 0, 1).reshape(3, NZ, NY, NX)
    residual = free_nodes * load.reshape(3, NZ, NY, NX)
    solution = jnp.zeros_like(residual)
    search = precondition * residual
    gamma = jnp.sum(residual * search)
    for count in range(ITERS):
        image = operate(search)
        alpha = gamma / jnp.sum(search * image)
        solution = solution + alpha * search
        residual = residual - alpha * image
        scaled = precondition * residual
        gamma_next = jnp.sum(residual * scaled)
        search = scaled + gamma_next / gamma * search
        gamma = gamma_next
    nodes = jnp.pad(solution, ((0, 0), (0, 1), (0, 1), (0, 1)))

    def energy_block(start):
        block_nodes = lax.dynamic_slice_in_dim(nodes, start, ZB + 1, 1)
        block_moduli = lax.dynamic_slice_in_dim(modulus, start, ZB, 0)
        return element_energy(block_nodes, block_moduli, stiffness)
    energy = lax.map(energy_block, starts).reshape(NZ, NY, NX)
    specific = energy / grid_density
    stimulus = smooth_reference(smooth_reference(smooth_reference(specific, 2), 1), 0)
    mean = jnp.sum(stimulus) / (NX * NY * NZ)
    updated = grid_density + REMODEL * bone_share * (stimulus / (mean + EPSILON) - 1.0)
    updated = jnp.clip(updated, FLOOR, CEILING)
    return (updated.reshape(N_GZ, ZB, NY, NX), solution.reshape(3, N_GZ, ZB, NY, NX))
```

```python
import functools
import math

import jax
import jax.numpy as jnp
import numpy as np
from jax import lax
from jax.experimental import pallas as pl
from jax.experimental.pallas import tpu as pltpu
from jax.sharding import PartitionSpec as P

MESH = pl.DeviceIdType.MESH
RAD = 24
MARROW = 0.1
REMODEL = 0.25
FLOOR = 0.2
CEILING = 1.0
EPSILON = 1e-06
DEP = 8
HEI = 96
WID = 128
F32 = jnp.float32
BF16 = jnp.bfloat16


def element_stiffness():
    poisson = 0.3
    lame = poisson / ((1.0 + poisson) * (1.0 - 2.0 * poisson))
    shear = 0.5 / (1.0 + poisson)
    elastic = np.zeros((6, 6))
    elastic[:3, :3] = lame
    for index in range(3):
        elastic[index, index] += 2.0 * shear
        elastic[index + 3, index + 3] = shear
    points = [0.5 - 0.5 / math.sqrt(3.0), 0.5 + 0.5 / math.sqrt(3.0)]
    matrix = np.zeros((24, 24))
    for point_z in points:
        for point_y in points:
            for point_x in points:
                strain = np.zeros((6, 24))
                for corner_z in range(2):
                    for corner_y in range(2):
                        for corner_x in range(2):
                            node = 4 * corner_z + 2 * corner_y + corner_x
                            shape_x = point_x if corner_x else 1.0 - point_x
                            shape_y = point_y if corner_y else 1.0 - point_y
                            shape_z = point_z if corner_z else 1.0 - point_z
                            slope_x = 1.0 if corner_x else -1.0
                            slope_y = 1.0 if corner_y else -1.0
                            slope_z = 1.0 if corner_z else -1.0
                            along_x = slope_x * shape_y * shape_z
                            along_y = shape_x * slope_y * shape_z
                            along_z = shape_x * shape_y * slope_z
                            strain[0, node] = along_x
                            strain[1, 8 + node] = along_y
                            strain[2, 16 + node] = along_z
                            strain[3, node] = along_y
                            strain[3, 8 + node] = along_x
                            strain[4, 8 + node] = along_z
                            strain[4, 16 + node] = along_y
                            strain[5, node] = along_z
                            strain[5, 16 + node] = along_x
                matrix = matrix + strain.T @ elastic @ strain / 8.0
    return matrix


KE = element_stiffness()
HAAR1 = np.array([[1.0, 1.0], [-1.0, 1.0]])
HAAR = np.kron(np.eye(3), np.kron(HAAR1, np.kron(HAAR1, HAAR1)))
KH = HAAR @ KE @ HAAR.T / 64.0
DIAG = float(KE[0, 0])
GROUPS = ((1, 10, 20), (2, 9), (4, 17), (12, 18), (3, 22), (5, 14), (11, 21), (6, 13, 19), (7,), (15,), (23,))
LAMBDA = math.exp(-1.0 / 12.0)
NORMAL = 1.0 / (1.0 + 2.0 * sum(LAMBDA**d for d in range(1, RAD + 1)))


def stress(m):
    out = [None] * 24
    for group in GROUPS:
        first = group[0]
        diag = float(KH[first, first])
        if len(group) == 1:
            out[first] = diag * m[first]
            continue
        off = float(KH[first, group[1]])
        total = m[first]
        for k in group[1:]:
            total = total + m[k]
        common = off * total
        for k in group:
            out[k] = common if abs(diag - off) < 1e-12 else common + (diag - off) * m[k]
    return out


def bilinear(m, f):
    total = None
    for k in range(24):
        if f[k] is not None:
            total = m[k] * f[k] if total is None else total + m[k] * f[k]
    return total


def zmodes(lo, hi):
    m = [None] * 24
    for c in range(3):
        for p in range(4):
            m[c * 8 + p] = hi[c * 4 + p] + lo[c * 4 + p]
            m[c * 8 + 4 + p] = hi[c * 4 + p] - lo[c * 4 + p]
    return m


def minus(a, b):
    return -b if a is None else a - b


def plus(a, b):
    return b if a is None else a + b


def split(value):
    hi = value.astype(BF16)
    return hi, (value - hi.astype(F32)).astype(BF16)


def dot(a, b):
    return jnp.dot(a, b, preferred_element_type=F32)


def body(sizes, dens, bone, fixed, load, out_d, out_u, s):
    GX, GY, GZ = sizes
    S = GY * GZ
    gx, gy, gz = lax.axis_index("gx"), lax.axis_index("gy"), lax.axis_index("gz")
    slab = gz * GY + gy
    lane = lax.broadcasted_iota(jnp.int32, (HEI, WID), 1)
    rowi = lax.broadcasted_iota(jnp.int32, (HEI, WID), 0)

    def device(dx=0, ds=0):
        t = lax.rem(slab + ds + S, S)
        return (lax.rem(gx + dx + GX, GX), lax.rem(t, GY), lax.div(t, GY))

    def flag(cond):
        return jnp.where(cond, 1.0, 0.0).astype(F32)

    has_left, has_right = flag(gx > 0), flag(gx < GX - 1)
    has_down, has_up = flag(slab > 0), flag(slab < S - 1)

    count = [0]
    sends = []

    def remote(src, dst, target):
        k = count[0]
        count[0] += 1
        copy = pltpu.make_async_remote_copy(
            src_ref=src, dst_ref=dst, send_sem=s["send"].at[k], recv_sem=s["recv"].at[k],
            device_id=target, device_id_type=MESH)
        copy.start()
        sends.append(copy)
        return copy

    barrier = pltpu.get_barrier_semaphore()
    peers = [device(-1), device(1), device(0, 1), device(0, -1), device(0, 3), device(0, -3),
             device(1, 1), device(-1, -1), device(-1, 1), device(1, -1)]
    for k in range(1, GX):
        peers.append((lax.rem(gx + k, GX), gy, gz))
    for k in range(1, GY):
        peers.append((gx, lax.rem(gy + k, GY), gz))
    for k in range(1, GZ):
        peers.append((gx, gy, lax.rem(gz + k, GZ)))
    for peer in peers:
        pl.semaphore_signal(barrier, inc=1, device_id=peer, device_id_type=MESH)

    E, R = s["E"], s["R"]

    @pl.loop(0, DEP)
    def _(z):
        b = bone[0, z].astype(F32)
        d = dens[0, z]
        E[z + 1] = b * d * d + (1.0 - b) * MARROW
        f = 1.0 - fixed[0, z].astype(F32)
        for c in range(3):
            R[c, z] = f * load[c, 0, z]

    zero8 = jnp.zeros((8, WID), F32)

    @pl.loop(0, 10)
    def _(zz):
        for k in range(6):
            s["SDs"][k, zz, pl.ds(HEI, 8)] = zero8
            s["SDw"][k, zz, pl.ds(HEI, 8)] = zero8
            s["B"][k, zz, pl.ds(0, 8)] = zero8

    for k in range(6):
        s["XSD"][k, pl.ds(HEI, 8)] = zero8
    for k in range(3):
        s["XB"][k, pl.ds(0, 8)] = zero8

    def pack(get, slots, src):
        acc = jnp.zeros((HEI, WID), F32)
        for index, k in slots:
            acc = jnp.where(lane == k, pltpu.roll(get(index), (k - src) % WID, 1), acc)
        return acc

    def turned(acc):
        full = jnp.concatenate([acc, jnp.zeros((WID - HEI, WID), F32)], axis=0)
        return jnp.transpose(full)

    def unturned(ref, rows):
        got = ref[...]
        full = jnp.concatenate([got, jnp.zeros((WID - rows, WID), F32)], axis=0) if rows < WID else got
        return jnp.transpose(full)[:HEI]

    s["XEs"][...] = turned(pack(lambda z: E[z + 1], [(z, z) for z in range(DEP)], WID - 1))[:8]

    pl.semaphore_wait(barrier, len(peers))
    c_xe = remote(s["XEs"], s["XEr"], device(1))
    c_xd = remote(s["XEs"], s["XDr"], device(1, 1))
    c_r = remote(R.at[:, 0], s["R8"], device(0, -1))
    c_e = remote(E.at[DEP], E.at[0], device(0, 1))

    far_y = jnp.abs(lax.broadcasted_iota(jnp.int32, (HEI, HEI), 0) - lax.broadcasted_iota(jnp.int32, (HEI, HEI), 1))
    s["Wy"][0], s["Wy"][1] = split(tap(far_y))
    row = lax.broadcasted_iota(jnp.int32, (WID, WID), 0)
    col = lax.broadcasted_iota(jnp.int32, (WID, WID), 1)
    s["Wx"][0, 0], s["Wx"][0, 1] = split(tap(jnp.abs(row - col)))
    for j in range(4):
        inside = (row >= 32 * j) & (row < 32 * j + 32)
        right = jnp.where(inside, tap(jnp.abs(WID + row - 32 * j - col)), 0.0)
        left = jnp.where(inside, tap(jnp.abs(col + 32 - row + 32 * j)), 0.0)
        s["Wx"][1 + j, 0], s["Wx"][1 + j, 1] = split(left)
        s["Wx"][5 + j, 0], s["Wx"][5 + j, 1] = split(right)

    T = s["T"]

    def inplane(e, edge):
        ex = e + jnp.where(lane == 0, edge, pltpu.roll(e, 1, 1))
        return ex + jnp.where(rowi == 0, 0.0, pltpu.roll(ex, 1, 0))

    c_xe.wait_recv()
    s["XE"][...] = unturned(s["XEr"], 8) * has_left

    @pl.loop(0, DEP)
    def _(z):
        T[z + 1] = inplane(E[z + 1], pltpu.roll(s["XE"][...], lax.rem(WID - z, WID), 1))

    c_t = remote(T.at[1], T.at[DEP + 1], device(0, -1))
    s0, Q = s["s0"], s["Q"]

    def start(z):
        inv = 1.0 / (DIAG * (T[z] + T[z + 1]))
        Q[z] = (1.0 - fixed[0, z].astype(F32)) * inv
        for c in range(3):
            s0[c, z + 1] = R[c, z] * inv

    start(DEP - 1)
    c_s = remote(s0.at[:, DEP], s0.at[:, 0], device(0, 1))
    pl.loop(1, DEP - 1)(start)

    c_xd.wait_recv()
    c_e.wait_recv()
    E[0] = E[0] * has_down
    xd = unturned(s["XDr"], 8) * (has_left * has_down)
    T[0] = inplane(E[0], pltpu.roll(xd, WID - 7, 1))
    start(0)
    s["EX"][...] = jnp.where(lane == 0, pltpu.roll(xd, WID - 7, 1), pltpu.roll(s["XE"][...], 1, 1))

    c_r.wait_recv()
    c_t.wait_recv()
    inv8 = has_up / (DIAG * (T[DEP] + has_up * T[DEP + 1]))
    for c in range(3):
        s0[c, DEP + 1] = s["R8"][c] * inv8
    c_s.wait_recv()

    slots = [((c, zz), 16 * c + zz) for c in range(3) for zz in range(10)]
    first = pack(lambda i: s0[i[0], i[1]], slots, 0)
    last = pack(lambda i: s0[i[0], i[1]], slots, WID - 1)
    s["X0"][...] = first
    s["XLs"][...] = turned(first)[:48]
    s["XRs"][...] = turned(last)[:48]
    c_xl = remote(s["XLs"], s["XRr"], device(-1))
    c_xr = remote(s["XRs"], s["XLr"], device(1))
    c_xl.wait_recv()
    c_xr.wait_recv()
    s["XH"][...] = unturned(s["XRr"], 48) * has_right
    xl = unturned(s["XLr"], 48)
    for c in range(3):
        s["XSD"][2 * c, pl.ds(0, HEI)] = pltpu.roll(s["X0"][...] + xl, (WID - 16 * c) % WID, 1)
        s["XSD"][2 * c + 1, pl.ds(0, HEI)] = pltpu.roll(s["X0"][...] - xl, (WID - 16 * c) % WID, 1)

    def xstage(field, SD, halo, zz):
        for c in range(3):
            v = field[c, zz]
            h = pltpu.roll(halo[...], WID - 1 - 16 * c - zz, 1)
            v1 = jnp.where(lane == WID - 1, h, pltpu.roll(v, WID - 1, 1))
            SD[2 * c, zz, pl.ds(0, HEI)] = v1 + v
            SD[2 * c + 1, zz, pl.ds(0, HEI)] = v1 - v

    pl.loop(0, 10)(lambda zz: xstage(s0, s["SDs"], s["XH"], zz))

    def planar(SD, zz, y0):
        out = []
        for c in range(3):
            a0, a1 = SD[2 * c, zz, pl.ds(y0, 8)], SD[2 * c, zz, pl.ds(y0 + 1, 8)]
            b0, b1 = SD[2 * c + 1, zz, pl.ds(y0, 8)], SD[2 * c + 1, zz, pl.ds(y0 + 1, 8)]
            out += [a1 + a0, b1 + b0, a1 - a0, b1 - b0]
        return out

    A, B = s["A"], s["B"]

    @pl.loop(0, HEI // 8)
    def _(i):
        y0 = pl.multiple_of(i * 8, 8)

        def plane(zz, carry):
            lo, above = carry
            hi = planar(s["SDs"], zz + 1, y0)
            f = stress(zmodes(lo, hi))
            e = E[zz, pl.ds(y0, 8)]
            f = [None if v is None else v * e for v in f]
            up = [plus(f[c * 8 + p], f[c * 8 + 4 + p]) for c in range(3) for p in range(4)]
            down = [minus(f[c * 8 + p], f[c * 8 + 4 + p]) for c in range(3) for p in range(4)]
            g = [u + v for u, v in zip(above, down)]
            for c in range(3):
                for ix in range(2):
                    A[2 * c + ix, zz, pl.ds(y0, 8)] = g[4 * c + ix] - g[4 * c + 2 + ix]
                    B[2 * c + ix, zz, pl.ds(y0 + 8, 8)] = g[4 * c + ix] + g[4 * c + 2 + ix]
            return tuple(hi), tuple(up)

        z8 = jnp.zeros((8, WID), F32)
        lax.fori_loop(0, DEP + 1, plane, (tuple(planar(s["SDs"], 0, y0)), (z8,) * 12))
        lo = []
        for c in range(3):
            a0, a1 = s["XSD"][2 * c, pl.ds(y0, 8)], s["XSD"][2 * c, pl.ds(y0 + 1, 8)]
            b0, b1 = s["XSD"][2 * c + 1, pl.ds(y0, 8)], s["XSD"][2 * c + 1, pl.ds(y0 + 1, 8)]
            lo += [a1 + a0, b1 + b0, a1 - a0, b1 - b0]
        hi = [pltpu.roll(v, WID - 1, 1) for v in lo]
        f = stress(zmodes(lo, hi))
        e = s["EX"][pl.ds(y0, 8)]
        f = [None if v is None else v * e for v in f]
        for c in range(3):
            g = []
            for p in range(4):
                up = plus(f[c * 8 + p], f[c * 8 + 4 + p])
                down = minus(f[c * 8 + p], f[c * 8 + 4 + p])
                g.append(down + pltpu.roll(up, 1, 1))
            s["XA"][c, pl.ds(y0, 8)] = (g[0] - g[2]) + (g[1] - g[3])
            s["XB"][c, pl.ds(y0 + 8, 8)] = (g[0] + g[2]) + (g[1] + g[3])

    for c in range(3):
        s["XF"][c] = s["XA"][c] + s["XB"][c, pl.ds(7, HEI)]

    w0 = s["w0"]

    def image(z, sums):
        gamma, delta, eps = sums
        q = Q[z]
        for c in range(3):
            gs = A[2 * c, z + 1] + B[2 * c, z + 1, pl.ds(7, HEI)]
            gd = A[2 * c + 1, z + 1] + B[2 * c + 1, z + 1, pl.ds(7, HEI)]
            edge = pltpu.roll(s["XF"][c], WID - 1 - z, 1)
            im = (gs - gd) + jnp.where(lane == 0, edge, pltpu.roll(gs + gd, 1, 1))
            w = im * q
            w0[c, z] = w
            v = s0[c, z + 1]
            gamma = gamma + R[c, z] * v
            delta = delta + v * im
            eps = eps + w * im
        return gamma, delta, eps

    zp = jnp.zeros((HEI, WID), F32)
    sums = image(0, (zp, zp, zp))
    c_w = remote(w0.at[:, 0], w0.at[:, DEP], device(0, -1))
    sums = lax.fori_loop(1, DEP, image, sums)

    slots = [((c, z), 8 * z + c) for z in range(DEP) for c in range(3)]
    s["XWs"][...] = turned(pack(lambda i: w0[i[0], i[1]], slots, 0))[:64]
    c_xw = remote(s["XWs"], s["XWr"].at[pl.ds(0, 64)], device(-1))
    c_xc = remote(s["XWs"].at[pl.ds(0, 8)], s["XCr"], device(-1, -1))

    SDs, SDw, SE = s["SDs"], s["SDw"], s["SE"]

    def chunks(step):
        @pl.loop(0, HEI // 8)
        def _(i):
            step(pl.multiple_of(i * 8, 8))

    def self_energy(y0):
        def plane(z, lo):
            hi = planar(SDs, z + 2, y0)
            m = zmodes(lo, hi)
            SE[0, z, pl.ds(y0, 8)] = bilinear(m, stress(m))
            return tuple(hi)
        lax.fori_loop(0, DEP, plane, tuple(planar(SDs, 1, y0)))

    chunks(self_energy)

    c_xw.wait_recv()
    c_xc.wait_recv()
    s["XWr"][pl.ds(64, 8)] = s["XCr"][...] * has_up
    s["XH"][...] = unturned(s["XWr"], 72) * has_right
    c_w.wait_recv()
    for c in range(3):
        w0[c, DEP] = w0[c, DEP] * has_up

    @pl.loop(0, DEP + 1)
    def _(z):
        for c in range(3):
            v = w0[c, z]
            h = pltpu.roll(s["XH"][...], WID - 1 - 8 * z - c, 1)
            v1 = jnp.where(lane == WID - 1, h, pltpu.roll(v, WID - 1, 1))
            SDw[2 * c, z, pl.ds(0, HEI)] = v1 + v
            SDw[2 * c + 1, z, pl.ds(0, HEI)] = v1 - v

    def w_energy(i, zeta):
        y0 = pl.multiple_of(i * 8, 8)

        def plane(z, carry):
            lo, total = carry
            hi = planar(SDw, z + 1, y0)
            m = zmodes(lo, hi)
            q = bilinear(m, stress(m))
            SE[2, z, pl.ds(y0, 8)] = q
            return tuple(hi), total + q * E[z + 1, pl.ds(y0, 8)]
        return lax.fori_loop(0, DEP, plane, (tuple(planar(SDw, 0, y0)), zeta))[1]

    zeta = lax.fori_loop(0, HEI // 8, w_energy, jnp.zeros((8, WID), F32))

    def rows(value):
        return jnp.sum(value, axis=0, keepdims=True)

    def spread(which, axis, n, me, target):
        buf = s["red"].at[which]
        copies = []
        for k in range(1, n):
            peer = lax.rem(me + k, n)
            copies.append(remote(s["own"].at[which], buf.at[me], target(peer)))
        return copies

    def gather(which, n, me, copies):
        for copy in copies:
            copy.wait_recv()
        buf = s["red"]
        buf[which, me] = s["own"][which]
        total = buf[which, 0]
        for k in range(1, n):
            total = total + buf[which, k]
        return total

    axes = ((GX, gx, lambda p: (p, gy, gz)), (GY, gy, lambda p: (gx, p, gz)), (GZ, gz, lambda p: (gx, gy, p)))

    def reduce_start(base, stage):
        n, me, target = axes[stage]
        return spread(base + stage, None, n, me, target)

    def reduce_end(base, stage, copies):
        n, me, _ = axes[stage]
        return gather(base + stage, n, me, copies)

    gamma, delta, eps = sums
    pad = jnp.zeros((4, WID), F32)
    s["own"][0] = jnp.concatenate([rows(gamma), rows(delta), rows(eps), rows(zeta), pad], axis=0)
    copies = reduce_start(0, 0)

    def cross_energy(y0):
        def plane(z, carry):
            los, low = carry
            his, hiw = planar(SDs, z + 2, y0), planar(SDw, z + 1, y0)
            SE[1, z, pl.ds(y0, 8)] = bilinear(zmodes(low, hiw), stress(zmodes(los, his)))
            return tuple(his), tuple(hiw)
        lax.fori_loop(0, DEP, plane, (tuple(planar(SDs, 1, y0)), tuple(planar(SDw, 0, y0))))

    chunks(cross_energy)

    s["own"][1] = reduce_end(0, 0, copies)
    copies = reduce_start(0, 1)
    s["own"][2] = reduce_end(0, 1, copies)
    copies = reduce_start(0, 2)
    total = jnp.sum(reduce_end(0, 2, copies), axis=1, keepdims=True)
    g0, d0, ep, ze = total[0:1], total[1:2], total[2:3], total[3:4]
    alpha = g0 / d0
    g1 = g0 - 2.0 * alpha * d0 + alpha * alpha * ep
    beta = g1 / g0
    d1 = (1.0 + beta) * (1.0 + beta) * d0 - 2.0 * alpha * (1.0 + beta) * ep + alpha * alpha * ze
    alpha1 = g1 / d1
    ca = jnp.broadcast_to(alpha + alpha1 * (1.0 + beta), (HEI, WID))
    cb = jnp.broadcast_to(-(alpha1 * alpha), (HEI, WID))

    G = s["G"]

    @pl.loop(0, DEP)
    def _(z):
        form = ca * ca * SE[0, z] + 2.0 * (ca * cb) * SE[1, z] + cb * cb * SE[2, z]
        G[z] = form * (0.5 * E[z + 1]) / dens[0, z]

    for b in range(2):
        acc_l = acc_r = None
        for j in range(4):
            v = G[4 * b + j]
            mine = (lane >= 32 * j) & (lane < 32 * j + 32)
            to_l = pltpu.roll(v, 32 * j, 1) if j else v
            to_r = pltpu.roll(v, (32 * j - 96) % WID, 1) if (32 * j - 96) % WID else v
            acc_l = to_l if acc_l is None else jnp.where(mine, to_l, acc_l)
            acc_r = to_r if acc_r is None else jnp.where(mine, to_r, acc_r)
        s["HLs"][b] = acc_l
        s["HRs"][b] = acc_r
    c_hl = remote(s["HLs"], s["HRr"], device(-1))
    c_hr = remote(s["HRs"], s["HLr"], device(1))

    def smooth_y(v):
        hi, lo = split(v)
        return dot(s["Wy"][0], hi) + dot(s["Wy"][1], hi) + dot(s["Wy"][0], lo)

    def smooth_x(v, k):
        hi, lo = split(v)
        return dot(hi, s["Wx"][k, 0]) + dot(hi, s["Wx"][k, 1]) + dot(lo, s["Wx"][k, 0])

    @pl.loop(0, DEP)
    def _(z):
        G[z] = smooth_x(smooth_y(G[z]), 0)

    @pl.loop(0, DEP)
    def _(z):
        for c in range(3):
            out_u[c, 0, z] = ca * s0[c, z + 1] + cb * w0[c, z]

    c_hl.wait_recv()
    c_hr.wait_recv()
    for b in range(2):
        s["HLr"][b] = smooth_y(s["HLr"][b] * has_left)
        s["HRr"][b] = smooth_y(s["HRr"][b] * has_right)

    Gup, Gdn = s["Gup"], s["Gdn"]
    planes = [None] * DEP
    order = [0, 7, 1, 6, 2, 5, 3, 4]
    for z in order:
        b, j = z // 4, z % 4
        G[z] = G[z] + smooth_x(s["HLr"][b], 1 + j) + smooth_x(s["HRr"][b], 5 + j)
        planes[z] = (remote(G.at[z], Gup.at[z], device(0, -3)), remote(G.at[z], Gdn.at[z], device(0, 3)))

    low = G[0]
    high = G[DEP - 1]
    for k in range(1, DEP):
        low = low + (LAMBDA**k) * G[k]
        high = high + (LAMBDA**k) * G[DEP - 1 - k]
    s["RU"][0] = low
    s["RD"][0] = high
    c_u0 = remote(s["RU"].at[0], s["RU"].at[1], device(0, -1))
    c_d0 = remote(s["RD"].at[0], s["RD"].at[1], device(0, 1))

    share = jnp.zeros((HEI, WID), F32)
    one = jnp.ones((HEI, WID), F32)
    for z in range(DEP):
        below = jnp.minimum(slab * DEP + z, RAD)
        above = jnp.minimum(S * DEP - 1 - slab * DEP - z, RAD)
        tail = power(one * (below + 1).astype(F32)) + power(one * (above + 1).astype(F32))
        weight = NORMAL * (1.0 + (2.0 * LAMBDA - tail) * (1.0 / (1.0 - LAMBDA)))
        share = share + weight * G[z]
    s["own"][3] = jnp.concatenate([rows(share), jnp.zeros((7, WID), F32)], axis=0)
    copies = reduce_start(3, 0)

    c_u0.wait_recv()
    c_d0.wait_recv()
    at1, at2 = flag(slab + 1 < S), flag(slab + 2 < S)
    bt1, bt2 = flag(slab - 1 >= 0), flag(slab - 2 >= 0)
    at3, bt3 = flag(slab + 3 < S), flag(slab - 3 >= 0)
    s["RU"][2] = low + LAMBDA**DEP * (at1 * s["RU"][1])
    s["RD"][2] = high + LAMBDA**DEP * (bt1 * s["RD"][1])
    c_u1 = remote(s["RU"].at[2], s["RU"].at[3], device(0, -1))
    c_d1 = remote(s["RD"].at[2], s["RD"].at[3], device(0, 1))

    s["own"][4] = reduce_end(3, 0, copies)
    copies = reduce_start(3, 1)
    F = s["F"]
    acc = jnp.zeros((HEI, WID), F32)
    for z in range(DEP):
        acc = G[z] if z == 0 else LAMBDA * acc + G[z]
        F[z] = acc
    acc = jnp.zeros((HEI, WID), F32)
    for z in range(DEP - 2, -1, -1):
        acc = LAMBDA * (acc + G[z + 1])
        F[z] = F[z] + acc
    s["own"][5] = reduce_end(3, 1, copies)
    copies = reduce_start(3, 2)
    c_u1.wait_recv()
    c_d1.wait_recv()
    near_u, near_d = at1 * s["RU"][3], bt1 * s["RD"][3]
    for z in range(DEP):
        F[z] = F[z] + LAMBDA ** (DEP - z) * near_u + LAMBDA ** (z + 1) * near_d

    mean = jnp.sum(reduce_end(3, 2, copies)[0:1], axis=1, keepdims=True)
    mean = mean / float(S * DEP * HEI * WID * GX)
    scale = NORMAL * jnp.broadcast_to(1.0 / (mean + EPSILON), (HEI, WID))

    for z in order:
        planes[z][0].wait_recv()
        planes[z][1].wait_recv()
    run = None
    for z in range(DEP):
        g = (at3 * LAMBDA**RAD) * Gup[z]
        run = g if run is None else g + (1.0 / LAMBDA) * run
        F[z] = F[z] + run
    run = None
    for z in range(DEP - 1, -1, -1):
        g = (bt3 * LAMBDA**RAD) * Gdn[z]
        run = g if run is None else g + (1.0 / LAMBDA) * run
        b = bone[0, z].astype(F32)
        new = dens[0, z] + REMODEL * b * ((F[z] + run) * scale - 1.0)
        out_d[0, z] = jnp.clip(new, FLOOR, CEILING)

    for copy in sends:
        copy.wait_send()


def tap(distance):
    return jnp.where(distance <= RAD, NORMAL * jnp.exp(distance.astype(F32) * (-1.0 / 12.0)), 0.0)


def power(exponent):
    return jnp.exp(exponent * (-1.0 / 12.0))


def on_device(sizes, density, bone, fixed, load):
    GX, GY, GZ = sizes
    copies = 4 + 2 + 2 + 3 + 2 * (GX + GY + GZ - 3) + 2 + 16 + 4
    V = pltpu.VMEM
    big = max(sizes)
    scratch = {
        "send": pltpu.SemaphoreType.DMA((copies,)),
        "recv": pltpu.SemaphoreType.DMA((copies,)),
        "E": V((9, HEI, WID), F32), "R": V((3, DEP, HEI, WID), F32), "R8": V((3, HEI, WID), F32),
        "T": V((10, HEI, WID), F32), "Q": V((DEP, HEI, WID), F32),
        "s0": V((3, 10, HEI, WID), F32), "w0": V((3, 9, HEI, WID), F32),
        "SDs": V((6, 10, HEI + 8, WID), F32), "SDw": V((6, 10, HEI + 8, WID), F32),
        "A": V((6, 9, HEI, WID), F32), "B": V((6, 10, HEI + 8, WID), F32),
        "XSD": V((6, HEI + 8, WID), F32), "XA": V((3, HEI, WID), F32), "XB": V((3, HEI + 8, WID), F32),
        "XF": V((3, HEI, WID), F32), "EX": V((HEI, WID), F32), "XE": V((HEI, WID), F32),
        "X0": V((HEI, WID), F32), "XH": V((HEI, WID), F32),
        "XEs": V((8, WID), F32), "XEr": V((8, WID), F32), "XDr": V((8, WID), F32),
        "XLs": V((48, WID), F32), "XRs": V((48, WID), F32), "XLr": V((48, WID), F32), "XRr": V((48, WID), F32),
        "XWs": V((64, WID), F32), "XWr": V((72, WID), F32), "XCr": V((8, WID), F32),
        "SE": V((3, DEP, HEI, WID), F32), "own": V((6, 8, WID), F32), "red": V((6, big, 8, WID), F32),
        "Wy": V((2, HEI, HEI), BF16), "Wx": V((9, 2, WID, WID), BF16),
        "G": V((DEP, HEI, WID), F32), "Gup": V((DEP, HEI, WID), F32), "Gdn": V((DEP, HEI, WID), F32),
        "HLs": V((2, HEI, WID), F32), "HRs": V((2, HEI, WID), F32),
        "HLr": V((2, HEI, WID), F32), "HRr": V((2, HEI, WID), F32),
        "RU": V((4, HEI, WID), F32), "RD": V((4, HEI, WID), F32), "F": V((DEP, HEI, WID), F32),
    }
    names = list(scratch)

    def kernel(*refs):
        body(sizes, *refs[:6], dict(zip(names, refs[6:])))

    spec = pl.BlockSpec(memory_space=pltpu.VMEM)
    return pl.pallas_call(
        kernel,
        out_shape=(jax.ShapeDtypeStruct(density.shape, F32), jax.ShapeDtypeStruct(load.shape, F32)),
        in_specs=[spec] * 4,
        out_specs=(spec, spec),
        scratch_shapes=[scratch[n] for n in names],
        compiler_params=pltpu.CompilerParams(
            collective_id=0, has_side_effects=True, vmem_limit_bytes=52 * 1024 * 1024),
    )(density, bone, fixed, load)


def solution(mesh):
    sizes = tuple(mesh.shape[name] for name in ("gx", "gy", "gz"))
    placed = (P("gz", "gy", None, "gx"),) * 3 + (P(None, "gz", "gy", None, "gx"),)
    return jax.shard_map(
        functools.partial(on_device, sizes),
        mesh=mesh,
        in_specs=placed,
        out_specs=(P("gz", "gy", None, "gx"), P(None, "gz", "gy", None, "gx")),
        check_vma=False,
    )
```

```python
import functools
import math

import jax
import jax.numpy as jnp
import numpy as np
from jax import lax
from jax.experimental import pallas as pl
from jax.experimental.pallas import tpu as pltpu
from jax.sharding import PartitionSpec as P

MESH = pl.DeviceIdType.MESH
RAD = 24
MARROW = 0.1
REMODEL = 0.25
FLOOR = 0.2
CEILING = 1.0
EPSILON = 1e-06
DEP = 8
HEI = 96
WID = 128
F32 = jnp.float32
BF16 = jnp.bfloat16


def element_stiffness():
    poisson = 0.3
    lame = poisson / ((1.0 + poisson) * (1.0 - 2.0 * poisson))
    shear = 0.5 / (1.0 + poisson)
    elastic = np.zeros((6, 6))
    elastic[:3, :3] = lame
    for index in range(3):
        elastic[index, index] += 2.0 * shear
        elastic[index + 3, index + 3] = shear
    points = [0.5 - 0.5 / math.sqrt(3.0), 0.5 + 0.5 / math.sqrt(3.0)]
    matrix = np.zeros((24, 24))
    for point_z in points:
        for point_y in points:
            for point_x in points:
                strain = np.zeros((6, 24))
                for corner_z in range(2):
                    for corner_y in range(2):
                        for corner_x in range(2):
                            node = 4 * corner_z + 2 * corner_y + corner_x
                            shape_x = point_x if corner_x else 1.0 - point_x
                            shape_y = point_y if corner_y else 1.0 - point_y
                            shape_z = point_z if corner_z else 1.0 - point_z
                            slope_x = 1.0 if corner_x else -1.0
                            slope_y = 1.0 if corner_y else -1.0
                            slope_z = 1.0 if corner_z else -1.0
                            along_x = slope_x * shape_y * shape_z
                            along_y = shape_x * slope_y * shape_z
                            along_z = shape_x * shape_y * slope_z
                            strain[0, node] = along_x
                            strain[1, 8 + node] = along_y
                            strain[2, 16 + node] = along_z
                            strain[3, node] = along_y
                            strain[3, 8 + node] = along_x
                            strain[4, 8 + node] = along_z
                            strain[4, 16 + node] = along_y
                            strain[5, node] = along_z
                            strain[5, 16 + node] = along_x
                matrix = matrix + strain.T @ elastic @ strain / 8.0
    return matrix


KE = element_stiffness()
HAAR1 = np.array([[1.0, 1.0], [-1.0, 1.0]])
HAAR = np.kron(np.eye(3), np.kron(HAAR1, np.kron(HAAR1, HAAR1)))
KH = HAAR @ KE @ HAAR.T / 64.0
DIAG = float(KE[0, 0])
GROUPS = ((1, 10, 20), (2, 9), (4, 17), (12, 18), (3, 22), (5, 14), (11, 21), (6, 13, 19), (7,), (15,), (23,))
LAMBDA = math.exp(-1.0 / 12.0)
NORMAL = 1.0 / (1.0 + 2.0 * sum(LAMBDA**d for d in range(1, RAD + 1)))


def stress(m):
    out = [None] * 24
    for group in GROUPS:
        first = group[0]
        diag = float(KH[first, first])
        if len(group) == 1:
            out[first] = diag * m[first]
            continue
        off = float(KH[first, group[1]])
        total = m[first]
        for k in group[1:]:
            total = total + m[k]
        common = off * total
        for k in group:
            out[k] = common if abs(diag - off) < 1e-12 else common + (diag - off) * m[k]
    return out


def bilinear(m, f):
    total = None
    for k in range(24):
        if f[k] is not None:
            total = m[k] * f[k] if total is None else total + m[k] * f[k]
    return total


def zmodes(lo, hi):
    m = [None] * 24
    for c in range(3):
        for p in range(4):
            m[c * 8 + p] = hi[c * 4 + p] + lo[c * 4 + p]
            m[c * 8 + 4 + p] = hi[c * 4 + p] - lo[c * 4 + p]
    return m


def minus(a, b):
    return -b if a is None else a - b


def plus(a, b):
    return b if a is None else a + b


def split(value):
    hi = value.astype(BF16)
    return hi, (value - hi.astype(F32)).astype(BF16)


def dot(a, b):
    return jnp.dot(a, b, preferred_element_type=F32)


def tap(distance):
    return jnp.where(distance <= RAD, NORMAL * jnp.exp(distance.astype(F32) * (-1.0 / 12.0)), 0.0)


def power(exponent):
    return jnp.exp(exponent.astype(F32) * (-1.0 / 12.0))


def kept(index, size):
    ends = power(jnp.minimum(index, RAD) + 1) + power(jnp.minimum(size - 1 - index, RAD) + 1)
    return NORMAL * (1.0 + (2.0 * LAMBDA - ends) * (1.0 / (1.0 - LAMBDA)))


def fold(value):
    return jnp.sum(value.reshape(HEI // 8, 8, WID), axis=0)


def rows(value):
    return jnp.sum(value, axis=0, keepdims=True)


def body(sizes, dens_h, bone_h, fixed_h, load_h, out_d, out_u, s):
    GX, GY, GZ = sizes
    S = GY * GZ
    gx, gy, gz = lax.axis_index("gx"), lax.axis_index("gy"), lax.axis_index("gz")
    slab = gz * GY + gy
    lane = lax.broadcasted_iota(jnp.int32, (HEI, WID), 1)
    rowi = lax.broadcasted_iota(jnp.int32, (HEI, WID), 0)

    def device(dx=0, ds=0):
        t = lax.rem(slab + ds + S, S)
        return (lax.rem(gx + dx + GX, GX), lax.rem(t, GY), lax.div(t, GY))

    def flag(cond):
        return jnp.where(cond, 1.0, 0.0).astype(F32)

    has_left, has_right = flag(gx > 0), flag(gx < GX - 1)
    has_down, has_up = flag(slab > 0), flag(slab < S - 1)

    count = [0]
    sends = []

    def remote(src, dst, target):
        k = count[0]
        count[0] += 1
        copy = pltpu.make_async_remote_copy(
            src_ref=src, dst_ref=dst, send_sem=s["send"].at[k], recv_sem=s["recv"].at[k],
            device_id=target, device_id_type=MESH)
        copy.start()
        sends.append(copy)
        return copy

    dens, bone, fixed, load = s["dens"], s["bone"], s["fixed"], s["load"]
    loads = []
    for k, (src, dst) in enumerate(((dens_h, dens), (bone_h, bone), (fixed_h, fixed), (load_h, load))):
        copy = pltpu.make_async_copy(src, dst, s["local"].at[k])
        copy.start()
        loads.append(copy)

    barrier = pltpu.get_barrier_semaphore()
    peers = [device(-1), device(1), device(0, 1), device(0, -1), device(1, 1), device(-1, -1),
             device(0, 3), device(0, -3)]
    for k in range(2, GX - 1):
        peers.append((lax.rem(gx + k, GX), gy, gz))
    for k in range(1, GY):
        peers.append((gx, lax.rem(gy + k, GY), gz))
    for k in range(1, GZ):
        peers.append((gx, gy, lax.rem(gz + k, GZ)))
    for peer in peers:
        pl.semaphore_signal(barrier, inc=1, device_id=peer, device_id_type=MESH)

    zero8 = jnp.zeros((8, WID), F32)

    @pl.loop(0, 10)
    def _(zz):
        for k in range(6):
            s["SDs"][k, zz, pl.ds(HEI, 8)] = zero8
            s["SDw"][k, zz, pl.ds(HEI, 8)] = zero8
            s["B"][k, zz, pl.ds(0, 8)] = zero8

    for k in range(6):
        s["XSD"][k, pl.ds(HEI, 8)] = zero8
    for k in range(3):
        s["XB"][k, pl.ds(0, 8)] = zero8

    E, R = s["E"], s["R"]
    loads[0].wait()
    loads[1].wait()

    @pl.loop(0, DEP)
    def _(z):
        b = bone[0, z].astype(F32)
        d = dens[0, z]
        E[z + 1] = b * d * d + (1.0 - b) * MARROW

    def pack(get, slots, src):
        acc = jnp.zeros((HEI, WID), F32)
        for index, k in slots:
            acc = jnp.where(lane == k, pltpu.roll(get(index), (k - src) % WID, 1), acc)
        return acc

    def turned(acc):
        full = jnp.concatenate([acc, jnp.zeros((WID - HEI, WID), F32)], axis=0)
        return jnp.transpose(full)

    def unturned(ref, number):
        got = ref[...]
        full = jnp.concatenate([got, jnp.zeros((WID - number, WID), F32)], axis=0)
        return jnp.transpose(full)[:HEI]

    s["XEs"][...] = turned(pack(lambda z: E[z + 1], [(z, z) for z in range(DEP)], WID - 1))[:8]
    loads[2].wait()
    loads[3].wait()

    @pl.loop(0, DEP)
    def _(z):
        f = 1.0 - fixed[0, z].astype(F32)
        for c in range(3):
            R[c, z] = f * load[c, 0, z]

    pl.semaphore_wait(barrier, len(peers))
    c_xe = remote(s["XEs"], s["XEr"], device(1))
    c_e = remote(E.at[DEP], E.at[0], device(0, 1))
    c_r = remote(R.at[:, 0], s["R8"], device(0, -1))
    c_xd = remote(s["XEs"], s["XDr"], device(1, 1))

    T = s["T"]
    s0, Q = s["s0"], s["Q"]

    def inplane(e, edge):
        ex = e + jnp.where(lane == 0, edge, pltpu.roll(e, 1, 1))
        return ex + jnp.where(rowi == 0, 0.0, pltpu.roll(ex, 1, 0))

    def flat(z):
        T[z + 1] = inplane(E[z + 1], pltpu.roll(s["XE"][...], lax.rem(WID - z, WID), 1))

    def start(z):
        inv = 1.0 / (DIAG * (T[z] + T[z + 1]))
        Q[z] = (1.0 - fixed[0, z].astype(F32)) * inv
        for c in range(3):
            s0[c, z + 1] = R[c, z] * inv

    c_xe.wait_recv()
    s["XE"][...] = unturned(s["XEr"], 8) * has_left
    flat(DEP - 1)
    flat(DEP - 2)
    start(DEP - 1)
    c_s = remote(s0.at[:, DEP], s0.at[:, 0], device(0, 1))
    flat(0)
    c_t = remote(T.at[1], T.at[DEP + 1], device(0, -1))
    pl.loop(1, DEP - 2)(flat)
    pl.loop(1, DEP - 1)(start)

    def columns(planes, name):
        slots = [((c, zz), 16 * c + zz) for c in range(3) for zz in planes]
        first = pack(lambda i: s0[i[0], i[1]], slots, 0)
        last = pack(lambda i: s0[i[0], i[1]], slots, WID - 1)
        s["XLs" + name][...] = turned(first)[:48]
        s["XRs" + name][...] = turned(last)[:48]
        return first, (remote(s["XLs" + name], s["XRr" + name], device(-1)),
                       remote(s["XRs" + name], s["XLr" + name], device(1)))

    first, pair = columns(range(2, 9), "1")
    s["X0"][...] = first

    far_y = jnp.abs(lax.broadcasted_iota(jnp.int32, (HEI, HEI), 0) - lax.broadcasted_iota(jnp.int32, (HEI, HEI), 1))
    s["Wy"][0], s["Wy"][1] = split(tap(far_y))
    row = lax.broadcasted_iota(jnp.int32, (WID, WID), 0)
    col = lax.broadcasted_iota(jnp.int32, (WID, WID), 1)
    s["Wx"][0, 0], s["Wx"][0, 1] = split(tap(jnp.abs(row - col)))
    for j in range(4):
        inside = (row >= 32 * j) & (row < 32 * j + 32)
        right = jnp.where(inside, tap(jnp.abs(WID + row - 32 * j - col)), 0.0)
        left = jnp.where(inside, tap(jnp.abs(col + 32 - row + 32 * j)), 0.0)
        s["Wx"][1 + j, 0], s["Wx"][1 + j, 1] = split(left)
        s["Wx"][5 + j, 0], s["Wx"][5 + j, 1] = split(right)
    s["W2"][...] = kept(gx * WID + lane, GX * WID) * kept(rowi, HEI)

    def edges(got):
        for c in range(3):
            s["XSD"][2 * c, pl.ds(0, HEI)] = pltpu.roll(s["X0"][...] + got, (WID - 16 * c) % WID, 1)
            s["XSD"][2 * c + 1, pl.ds(0, HEI)] = pltpu.roll(s["X0"][...] - got, (WID - 16 * c) % WID, 1)

    def arrive(pair, name):
        for copy in pair:
            copy.wait_recv()
        s["XH"][...] = unturned(s["XRr" + name], 48) * has_right
        return unturned(s["XLr" + name], 48)

    def xstage(field, SD, shift, zz):
        for c in range(3):
            v = field[c, zz]
            h = pltpu.roll(s["XH"][...], shift(c, zz), 1)
            v1 = jnp.where(lane == WID - 1, h, pltpu.roll(v, WID - 1, 1))
            SD[2 * c, zz, pl.ds(0, HEI)] = v1 + v
            SD[2 * c + 1, zz, pl.ds(0, HEI)] = v1 - v

    def place_s(c, zz):
        return WID - 1 - 16 * c - zz

    def place_w(c, z):
        return WID - 1 - 8 * z - c

    def planar(SD, zz, y0):
        out = []
        for c in range(3):
            a0, a1 = SD[2 * c, zz, pl.ds(y0, 8)], SD[2 * c, zz, pl.ds(y0 + 1, 8)]
            b0, b1 = SD[2 * c + 1, zz, pl.ds(y0, 8)], SD[2 * c + 1, zz, pl.ds(y0 + 1, 8)]
            out += [a1 + a0, b1 + b0, a1 - a0, b1 - b0]
        return out

    A, B = s["A"], s["B"]

    def element(lo, hi, zz, y0):
        f = stress(zmodes(lo, hi))
        e = E[zz, pl.ds(y0, 8)]
        f = [None if v is None else v * e for v in f]
        up = [plus(f[c * 8 + p], f[c * 8 + 4 + p]) for c in range(3) for p in range(4)]
        down = [minus(f[c * 8 + p], f[c * 8 + 4 + p]) for c in range(3) for p in range(4)]
        return down, up

    def put(g, zz, y0, more=False):
        for c in range(3):
            for ix in range(2):
                a = g[4 * c + ix] - g[4 * c + 2 + ix]
                b = g[4 * c + ix] + g[4 * c + 2 + ix]
                if more:
                    a = a + A[2 * c + ix, zz, pl.ds(y0, 8)]
                    b = b + B[2 * c + ix, zz, pl.ds(y0 + 8, 8)]
                A[2 * c + ix, zz, pl.ds(y0, 8)] = a
                B[2 * c + ix, zz, pl.ds(y0 + 8, 8)] = b

    def both(g, h):
        return [u + v for u, v in zip(g, h)]

    def edge_elements(y0):
        lo = []
        for c in range(3):
            a0, a1 = s["XSD"][2 * c, pl.ds(y0, 8)], s["XSD"][2 * c, pl.ds(y0 + 1, 8)]
            b0, b1 = s["XSD"][2 * c + 1, pl.ds(y0, 8)], s["XSD"][2 * c + 1, pl.ds(y0 + 1, 8)]
            lo += [a1 + a0, b1 + b0, a1 - a0, b1 - b0]
        hi = [pltpu.roll(v, WID - 1, 1) for v in lo]
        f = stress(zmodes(lo, hi))
        e = s["EX"][pl.ds(y0, 8)]
        f = [None if v is None else v * e for v in f]
        for c in range(3):
            g = []
            for p in range(4):
                up = plus(f[c * 8 + p], f[c * 8 + 4 + p])
                down = minus(f[c * 8 + p], f[c * 8 + 4 + p])
                g.append(down + pltpu.roll(up, 1, 1))
            s["XA"][c, pl.ds(y0, 8)] = (g[0] - g[2]) + (g[1] - g[3])
            s["XB"][c, pl.ds(y0 + 8, 8)] = (g[0] + g[2]) + (g[1] + g[3])

    def chunks(step):
        @pl.loop(0, HEI // 8)
        def _(i):
            step(pl.multiple_of(i * 8, 8))

    w0 = s["w0"]

    def image(z, sums):
        gamma, delta, eps = sums
        q = Q[z]
        for c in range(3):
            gs = A[2 * c, z + 1] + B[2 * c, z + 1, pl.ds(7, HEI)]
            gd = A[2 * c + 1, z + 1] + B[2 * c + 1, z + 1, pl.ds(7, HEI)]
            edge = pltpu.roll(s["XA"][c] + s["XB"][c, pl.ds(7, HEI)], WID - 1 - z, 1)
            im = (gs - gd) + jnp.where(lane == 0, edge, pltpu.roll(gs + gd, 1, 1))
            w = im * q
            w0[c, z] = w
            v = s0[c, z + 1]
            gamma = gamma + fold(R[c, z] * v)
            delta = delta + fold(v * im)
            eps = eps + fold(w * im)
        return gamma, delta, eps

    s["EX"][...] = pltpu.roll(s["XE"][...], 1, 1)
    s["XL1"][...] = arrive(pair, "1")
    edges(s["XL1"][...])
    pl.loop(2, 9)(lambda zz: xstage(s0, s["SDs"], place_s, zz))

    def early(y0):
        def plane(zz, carry):
            lo, above = carry
            hi = planar(s["SDs"], zz + 1, y0)
            down, up = element(lo, hi, zz, y0)
            put(both(above, down), zz, y0)
            return tuple(hi), tuple(up)

        top = lax.fori_loop(2, DEP, plane, (tuple(planar(s["SDs"], 2, y0)), (zero8,) * 12))[1]
        put(top, DEP, y0)
        edge_elements(y0)

    chunks(early)
    sums = lax.fori_loop(2, DEP - 1, image, (zero8, zero8, zero8))

    c_xd.wait_recv()
    c_e.wait_recv()
    E[0] = E[0] * has_down
    corner = pltpu.roll(unturned(s["XDr"], 8) * (has_left * has_down), WID - 7, 1)
    T[0] = inplane(E[0], corner)
    start(0)
    s["EX"][...] = jnp.where(lane == 0, corner, s["EX"][...])
    c_r.wait_recv()
    c_t.wait_recv()
    inv8 = has_up / (DIAG * (T[DEP] + has_up * T[DEP + 1]))
    for c in range(3):
        s0[c, DEP + 1] = s["R8"][c] * inv8
    c_s.wait_recv()

    first, pair = columns((0, 1, 9), "2")
    s["X0"][...] = s["X0"][...] + first
    edges(s["XL1"][...] + arrive(pair, "2"))
    for zz in (0, 1, 9):
        xstage(s0, s["SDs"], place_s, zz)

    def late(y0):
        SD = s["SDs"]
        n0, n1, n2 = planar(SD, 0, y0), planar(SD, 1, y0), planar(SD, 2, y0)
        up = element(n0, n1, 0, y0)[1]
        down, above = element(n1, n2, 1, y0)
        put(both(up, down), 1, y0)
        put(above, 2, y0, more=True)
        put(element(planar(SD, 8, y0), planar(SD, 9, y0), DEP, y0)[0], DEP, y0, more=True)
        edge_elements(y0)

    chunks(late)
    sums = image(0, sums)
    c_w = remote(w0.at[:, 0], w0.at[:, DEP], device(0, -1))
    sums = image(1, sums)
    gamma, delta, eps = image(DEP - 1, sums)

    slots = [((c, z), 8 * z + c) for z in range(DEP) for c in range(3)]
    s["XWs"][...] = turned(pack(lambda i: w0[i[0], i[1]], slots, 0))[:64]
    c_xw = remote(s["XWs"], s["XWr"].at[pl.ds(0, 64)], device(-1))
    c_xc = remote(s["XWs"].at[pl.ds(0, 8)], s["XCr"], device(-1, -1))

    SDs, SDw, SE = s["SDs"], s["SDw"], s["SE"]

    def self_energy(y0):
        def plane(z, lo):
            hi = planar(SDs, z + 2, y0)
            m = zmodes(lo, hi)
            SE[0, z, pl.ds(y0, 8)] = bilinear(m, stress(m))
            return tuple(hi)
        lax.fori_loop(0, DEP, plane, tuple(planar(SDs, 1, y0)))

    def w_energy(low, high):
        def step(y0):
            def plane(z, lo):
                hi = planar(SDw, z + 1, y0)
                m = zmodes(lo, hi)
                SE[2, z, pl.ds(y0, 8)] = bilinear(m, stress(m))
                return tuple(hi)
            lax.fori_loop(low, high, plane, tuple(planar(SDw, low, y0)))
        return step

    def cross_energy(low, high):
        def step(y0):
            def plane(z, carry):
                los, lows = carry
                his, hiw = planar(SDs, z + 2, y0), planar(SDw, z + 1, y0)
                SE[1, z, pl.ds(y0, 8)] = bilinear(zmodes(lows, hiw), stress(zmodes(los, his)))
                return tuple(his), tuple(hiw)
            lax.fori_loop(low, high, plane, (tuple(planar(SDs, low + 1, y0)), tuple(planar(SDw, low, y0))))
        return step

    def per_density(z, sums):
        zeta, m0, m1, m2 = sums
        e = E[z + 1]
        g = 0.5 * e / dens[0, z]
        weight = s["W2"][...] * kept(jnp.full((HEI, WID), slab * DEP + z, jnp.int32), S * DEP)
        zeta = zeta + fold(SE[2, z] * e)
        out = []
        for i, m in enumerate((m0, m1, m2)):
            v = SE[i, z] * g
            SE[i, z] = v
            out.append(m + fold(v * weight))
        return (zeta, *out)

    HLs, HRs, HLr, HRr = s["HLs"], s["HRs"], s["HLr"], s["HRr"]

    def send_sides(b):
        @pl.loop(0, 3)
        def _(i):
            acc_l = acc_r = None
            for j in range(4):
                v = SE[i, 4 * b + j]
                mine = (lane >= 32 * j) & (lane < 32 * j + 32)
                to_l = pltpu.roll(v, 32 * j, 1) if j else v
                to_r = pltpu.roll(v, (32 * j - 96) % WID, 1) if (32 * j - 96) % WID else v
                acc_l = to_l if acc_l is None else jnp.where(mine, to_l, acc_l)
                acc_r = to_r if acc_r is None else jnp.where(mine, to_r, acc_r)
            HLs[b, i] = acc_l
            HRs[b, i] = acc_r
        return remote(HLs.at[b], HRr.at[b], device(-1)), remote(HRs.at[b], HLr.at[b], device(1))

    chunks(self_energy)
    c_xw.wait_recv()
    s["XH"][...] = unturned(s["XWr"], 72) * has_right
    pl.loop(0, DEP)(lambda z: xstage(w0, SDw, place_w, z))
    chunks(w_energy(0, DEP - 1))
    chunks(cross_energy(0, DEP - 1))
    forms = lax.fori_loop(0, DEP - 1, per_density, (zero8,) * 4)
    sides = [send_sides(0)]

    c_xc.wait_recv()
    c_w.wait_recv()
    s["XWr"][pl.ds(64, 8)] = s["XCr"][...] * has_up
    s["XH"][...] = unturned(s["XWr"], 72) * has_right
    for c in range(3):
        w0[c, DEP] = w0[c, DEP] * has_up
    xstage(w0, SDw, place_w, DEP)
    chunks(w_energy(DEP - 1, DEP))
    chunks(cross_energy(DEP - 1, DEP))
    forms = per_density(DEP - 1, forms)

    axes = ((GX, gx, lambda p: (p, gy, gz)), (GY, gy, lambda p: (gx, p, gz)), (GZ, gz, lambda p: (gx, gy, p)))
    own, red = s["own"], s["red"]

    def reduce_start(stage):
        n, me, target = axes[stage]
        return [remote(own.at[stage], red.at[stage, me], target(lax.rem(me + k, n))) for k in range(1, n)]

    def reduce_end(stage, copies):
        n, me, _ = axes[stage]
        for copy in copies:
            copy.wait_recv()
        red[stage, me] = own[stage]
        total = red[stage, 0]
        for k in range(1, n):
            total = total + red[stage, k]
        return total

    own[0] = jnp.concatenate([rows(v) for v in (gamma, delta, eps, *forms)] + [jnp.zeros((1, WID), F32)], axis=0)
    copies = reduce_start(0)
    sides.append(send_sides(1))

    def smooth_y(v):
        hi, lo = split(v)
        return dot(s["Wy"][0], hi) + dot(s["Wy"][1], hi) + dot(s["Wy"][0], lo)

    def smooth_x(v, k):
        hi, lo = split(v)
        return dot(hi, s["Wx"][k, 0]) + dot(hi, s["Wx"][k, 1]) + dot(lo, s["Wx"][k, 0])

    @pl.loop(0, DEP)
    def _(z):
        for i in range(3):
            SE[i, z] = smooth_y(SE[i, z])

    own[1] = reduce_end(0, copies)
    copies = reduce_start(1)

    for pair in sides:
        for copy in pair:
            copy.wait_recv()
    for b in range(2):
        @pl.loop(0, 3)
        def _(i, b=b):
            HLr[b, i] = smooth_y(HLr[b, i] * has_left)
            HRr[b, i] = smooth_y(HRr[b, i] * has_right)

    own[2] = reduce_end(1, copies)
    copies = reduce_start(2)

    for b in range(2):
        @pl.loop(0, 4)
        def _(j, b=b):
            for i in range(3):
                SE[i, 4 * b + j] = (smooth_x(SE[i, 4 * b + j], 0) + smooth_x(HLr[b, i], 1 + j)
                                    + smooth_x(HRr[b, i], 5 + j))

    total = jnp.sum(reduce_end(2, copies), axis=1, keepdims=True)
    g0, d0, ep, ze = total[0:1], total[1:2], total[2:3], total[3:4]
    alpha = g0 / d0
    g1 = g0 - 2.0 * alpha * d0 + alpha * alpha * ep
    beta = g1 / g0
    d1 = (1.0 + beta) * (1.0 + beta) * d0 - 2.0 * alpha * (1.0 + beta) * ep + alpha * alpha * ze
    alpha1 = g1 / d1
    a1 = alpha + alpha1 * (1.0 + beta)
    b1 = -(alpha1 * alpha)
    ca = jnp.broadcast_to(a1, (HEI, WID))
    cb = jnp.broadcast_to(b1, (HEI, WID))
    caa, cab, cbb = a1 * a1, 2.0 * (a1 * b1), b1 * b1
    mean = (caa * total[4:5] + cab * total[5:6] + cbb * total[6:7]) / float(S * DEP * HEI * WID * GX)
    scale = NORMAL * jnp.broadcast_to(1.0 / (mean + EPSILON), (HEI, WID))
    caa, cab, cbb = (jnp.broadcast_to(v, (HEI, WID)) for v in (caa, cab, cbb))

    G, Gup, Gdn, F = s["G"], s["Gup"], s["Gdn"], s["F"]

    @pl.loop(0, DEP)
    def _(z):
        G[z] = caa * SE[0, z] + cab * SE[1, z] + cbb * SE[2, z]

    low = G[DEP - 1]
    high = G[0]
    for k in range(1, DEP):
        low = LAMBDA * low + G[DEP - 1 - k]
        high = LAMBDA * high + G[k]
    RU, RD = s["RU"], s["RD"]
    RU[0] = low
    RD[0] = high
    c_u0 = remote(RU.at[0], RU.at[1], device(0, -1))
    c_d0 = remote(RD.at[0], RD.at[1], device(0, 1))

    def planes(k):
        z = DEP - 1 - k
        return remote(G.at[k], Gup.at[k], device(0, -3)), remote(G.at[z], Gdn.at[z], device(0, 3))

    far = [planes(k) for k in range(4)]

    acc = None
    for z in range(DEP):
        acc = G[z] if z == 0 else LAMBDA * acc + G[z]
        F[z] = acc
    acc = jnp.zeros((HEI, WID), F32)
    for z in range(DEP - 2, -1, -1):
        acc = LAMBDA * (acc + G[z + 1])
        F[z] = F[z] + acc

    at1, at3 = flag(slab + 1 < S), flag(slab + 3 < S)
    bt1, bt3 = flag(slab >= 1), flag(slab >= 3)
    c_u0.wait_recv()
    c_d0.wait_recv()
    RU[2] = RU[0] + (LAMBDA**DEP * at1) * RU[1]
    RD[2] = RD[0] + (LAMBDA**DEP * bt1) * RD[1]
    c_u1 = remote(RU.at[2], RU.at[3], device(0, -1))
    c_d1 = remote(RD.at[2], RD.at[3], device(0, 1))
    far += [planes(k) for k in range(4, DEP)]

    @pl.loop(0, DEP)
    def _(z):
        for c in range(3):
            s["U"][c, 0, z] = ca * s0[c, z + 1] + cb * w0[c, z]

    stores = [pltpu.make_async_copy(s["U"], out_u, s["local"].at[4])]
    stores[0].start()

    c_u1.wait_recv()
    c_d1.wait_recv()
    near_u, near_d = at1 * RU[3], bt1 * RD[3]
    for z in range(DEP):
        F[z] = F[z] + LAMBDA ** (DEP - z) * near_u + LAMBDA ** (z + 1) * near_d

    up_scale, dn_scale = at3 * LAMBDA**RAD, bt3 * LAMBDA**RAD
    RR = s["RR"]

    def finish_plane(z, value):
        b = bone[0, z].astype(F32)
        new = dens[0, z] + REMODEL * b * (value * scale - 1.0)
        s["D"][0, z] = jnp.clip(new, FLOOR, CEILING)
        copy = pltpu.make_async_copy(s["D"].at[0, z], out_d.at[0, z], s["local"].at[5 + z])
        copy.start()
        stores.append(copy)

    for k in range(DEP):
        z = DEP - 1 - k
        far[k][0].wait_recv()
        far[k][1].wait_recv()
        up = up_scale * Gup[k]
        down = dn_scale * Gdn[z]
        if k:
            up = up + (1.0 / LAMBDA) * RR[0]
            down = down + (1.0 / LAMBDA) * RR[1]
        RR[0] = up
        RR[1] = down
        if k < DEP // 2:
            F[k] = F[k] + up
            F[z] = F[z] + down
        else:
            finish_plane(k, F[k] + up)
            finish_plane(z, F[z] + down)

    for copy in stores:
        copy.wait()
    for copy in sends:
        copy.wait_send()


def on_device(sizes, density, bone, fixed, load):
    GX, GY, GZ = sizes
    copies = 4 + 2 + 4 + 3 + 4 + (GX + GY + GZ - 3) + 4 + 16
    V = pltpu.VMEM
    plane, tall, thin = (HEI, WID), (HEI + 8, WID), (48, WID)
    scratch = {
        "send": pltpu.SemaphoreType.DMA((copies,)),
        "recv": pltpu.SemaphoreType.DMA((copies,)),
        "local": pltpu.SemaphoreType.DMA((13,)),
        "U": V(load.shape, F32), "D": V(density.shape, F32),
        "dens": V(density.shape, F32), "bone": V(bone.shape, jnp.int32), "fixed": V(fixed.shape, jnp.int32),
        "load": V(load.shape, F32),
        "E": V((9, *plane), F32), "R": V((3, DEP, *plane), F32), "R8": V((3, *plane), F32),
        "T": V((10, *plane), F32), "Q": V((DEP, *plane), F32),
        "s0": V((3, 10, *plane), F32), "w0": V((3, 9, *plane), F32),
        "SDs": V((6, 10, *tall), F32), "SDw": V((6, 10, *tall), F32),
        "A": V((6, 9, *plane), F32), "B": V((6, 10, *tall), F32),
        "XSD": V((6, *tall), F32), "XA": V((3, *plane), F32), "XB": V((3, *tall), F32),
        "EX": V(plane, F32), "XE": V(plane, F32), "X0": V(plane, F32), "XH": V(plane, F32), "XL1": V(plane, F32),
        "XEs": V((8, WID), F32), "XEr": V((8, WID), F32), "XDr": V((8, WID), F32),
        "XLs1": V(thin, F32), "XRs1": V(thin, F32), "XLr1": V(thin, F32), "XRr1": V(thin, F32),
        "XLs2": V(thin, F32), "XRs2": V(thin, F32), "XLr2": V(thin, F32), "XRr2": V(thin, F32),
        "XWs": V((64, WID), F32), "XWr": V((72, WID), F32), "XCr": V((8, WID), F32),
        "SE": V((3, DEP, *plane), F32), "own": V((3, 8, WID), F32), "red": V((3, max(sizes), 8, WID), F32),
        "Wy": V((2, HEI, HEI), BF16), "Wx": V((9, 2, WID, WID), BF16), "W2": V(plane, F32),
        "G": V((DEP, *plane), F32), "Gup": V((DEP, *plane), F32), "Gdn": V((DEP, *plane), F32),
        "HLs": V((2, 3, *plane), F32), "HRs": V((2, 3, *plane), F32),
        "HLr": V((2, 3, *plane), F32), "HRr": V((2, 3, *plane), F32),
        "RU": V((4, *plane), F32), "RD": V((4, *plane), F32), "F": V((DEP, *plane), F32), "RR": V((2, *plane), F32),
    }
    names = list(scratch)

    def kernel(*refs):
        body(sizes, *refs[:6], dict(zip(names, refs[6:])))

    outer = pl.BlockSpec(memory_space=pltpu.HBM)
    return pl.pallas_call(
        kernel,
        out_shape=(jax.ShapeDtypeStruct(density.shape, F32), jax.ShapeDtypeStruct(load.shape, F32)),
        in_specs=[outer] * 4,
        out_specs=(outer, outer),
        scratch_shapes=[scratch[n] for n in names],
        compiler_params=pltpu.CompilerParams(
            collective_id=0, has_side_effects=True, vmem_limit_bytes=56 * 1024 * 1024),
    )(density, bone, fixed, load)


def solution(mesh):
    sizes = tuple(mesh.shape[name] for name in ("gx", "gy", "gz"))
    placed = (P("gz", "gy", None, "gx"),) * 3 + (P(None, "gz", "gy", None, "gx"),)
    return jax.shard_map(
        functools.partial(on_device, sizes),
        mesh=mesh,
        in_specs=placed,
        out_specs=(P("gz", "gy", None, "gx"), P(None, "gz", "gy", None, "gx")),
        check_vma=False,
    )
```

```python
import functools
import math

import jax
import jax.numpy as jnp
import numpy as np
from jax import lax
from jax.experimental import pallas as pl
from jax.experimental.pallas import tpu as pltpu
from jax.sharding import PartitionSpec as P

MESH = pl.DeviceIdType.MESH
RAD = 24
MARROW = 0.1
REMODEL = 0.25
FLOOR = 0.2
CEILING = 1.0
EPSILON = 1e-06
DEP = 8
HEI = 96
WID = 128
F32 = jnp.float32
BF16 = jnp.bfloat16


def element_stiffness():
    poisson = 0.3
    lame = poisson / ((1.0 + poisson) * (1.0 - 2.0 * poisson))
    shear = 0.5 / (1.0 + poisson)
    elastic = np.zeros((6, 6))
    elastic[:3, :3] = lame
    for index in range(3):
        elastic[index, index] += 2.0 * shear
        elastic[index + 3, index + 3] = shear
    points = [0.5 - 0.5 / math.sqrt(3.0), 0.5 + 0.5 / math.sqrt(3.0)]
    matrix = np.zeros((24, 24))
    for point_z in points:
        for point_y in points:
            for point_x in points:
                strain = np.zeros((6, 24))
                for corner_z in range(2):
                    for corner_y in range(2):
                        for corner_x in range(2):
                            node = 4 * corner_z + 2 * corner_y + corner_x
                            shape_x = point_x if corner_x else 1.0 - point_x
                            shape_y = point_y if corner_y else 1.0 - point_y
                            shape_z = point_z if corner_z else 1.0 - point_z
                            slope_x = 1.0 if corner_x else -1.0
                            slope_y = 1.0 if corner_y else -1.0
                            slope_z = 1.0 if corner_z else -1.0
                            along_x = slope_x * shape_y * shape_z
                            along_y = shape_x * slope_y * shape_z
                            along_z = shape_x * shape_y * slope_z
                            strain[0, node] = along_x
                            strain[1, 8 + node] = along_y
                            strain[2, 16 + node] = along_z
                            strain[3, node] = along_y
                            strain[3, 8 + node] = along_x
                            strain[4, 8 + node] = along_z
                            strain[4, 16 + node] = along_y
                            strain[5, node] = along_z
                            strain[5, 16 + node] = along_x
                matrix = matrix + strain.T @ elastic @ strain / 8.0
    return matrix


KE = element_stiffness()
HAAR1 = np.array([[1.0, 1.0], [-1.0, 1.0]])
HAAR = np.kron(np.eye(3), np.kron(HAAR1, np.kron(HAAR1, HAAR1)))
KH = HAAR @ KE @ HAAR.T / 64.0
DIAG = float(KE[0, 0])
GROUPS = ((1, 10, 20), (2, 9), (4, 17), (12, 18), (3, 22), (5, 14), (11, 21), (6, 13, 19), (7,), (15,), (23,))
LAMBDA = math.exp(-1.0 / 12.0)
NORMAL = 1.0 / (1.0 + 2.0 * sum(LAMBDA**d for d in range(1, RAD + 1)))


def stress(m):
    out = [None] * 24
    for group in GROUPS:
        first = group[0]
        diag = float(KH[first, first])
        if len(group) == 1:
            out[first] = diag * m[first]
            continue
        off = float(KH[first, group[1]])
        total = m[first]
        for k in group[1:]:
            total = total + m[k]
        common = off * total
        for k in group:
            out[k] = common if abs(diag - off) < 1e-12 else common + (diag - off) * m[k]
    return out


def bilinear(m, f):
    total = None
    for k in range(24):
        if f[k] is not None:
            total = m[k] * f[k] if total is None else total + m[k] * f[k]
    return total


def zmodes(lo, hi):
    m = [None] * 24
    for c in range(3):
        for p in range(4):
            m[c * 8 + p] = hi[c * 4 + p] + lo[c * 4 + p]
            m[c * 8 + 4 + p] = hi[c * 4 + p] - lo[c * 4 + p]
    return m


def minus(a, b):
    return -b if a is None else a - b


def plus(a, b):
    return b if a is None else a + b


def split(value):
    hi = value.astype(BF16)
    return hi, (value - hi.astype(F32)).astype(BF16)


def dot(a, b):
    return jnp.dot(a, b, preferred_element_type=F32)


def tap(distance):
    return jnp.where(distance <= RAD, NORMAL * jnp.exp(distance.astype(F32) * (-1.0 / 12.0)), 0.0)


def power(exponent):
    return jnp.exp(exponent.astype(F32) * (-1.0 / 12.0))


def kept(index, size):
    ends = power(jnp.minimum(index, RAD) + 1) + power(jnp.minimum(size - 1 - index, RAD) + 1)
    return NORMAL * (1.0 + (2.0 * LAMBDA - ends) * (1.0 / (1.0 - LAMBDA)))


def fold(value):
    return jnp.sum(value.reshape(HEI // 8, 8, WID), axis=0)


def rows(value):
    return jnp.sum(value, axis=0, keepdims=True)


def body(sizes, dens_h, bone_h, fixed_h, load_h, out_d, out_u, s):
    GX, GY, GZ = sizes
    S = GY * GZ
    gx, gy, gz = lax.axis_index("gx"), lax.axis_index("gy"), lax.axis_index("gz")
    slab = gz * GY + gy
    lane = lax.broadcasted_iota(jnp.int32, (HEI, WID), 1)
    rowi = lax.broadcasted_iota(jnp.int32, (HEI, WID), 0)

    def device(dx=0, ds=0):
        t = lax.rem(slab + ds + S, S)
        return (lax.rem(gx + dx + GX, GX), lax.rem(t, GY), lax.div(t, GY))

    def flag(cond):
        return jnp.where(cond, 1.0, 0.0).astype(F32)

    has_left, has_right = flag(gx > 0), flag(gx < GX - 1)
    has_down, has_up = flag(slab > 0), flag(slab < S - 1)

    count = [0]
    sends = []

    def remote(src, dst, target):
        k = count[0]
        count[0] += 1
        copy = pltpu.make_async_remote_copy(
            src_ref=src, dst_ref=dst, send_sem=s["send"].at[k], recv_sem=s["recv"].at[k],
            device_id=target, device_id_type=MESH)
        copy.start()
        sends.append(copy)
        return copy

    dens, bone, fixed, load = s["dens"], s["bone"], s["fixed"], s["load"]
    loads = []
    for k, (src, dst) in enumerate(((dens_h, dens), (bone_h, bone), (fixed_h, fixed), (load_h, load))):
        copy = pltpu.make_async_copy(src, dst, s["local"].at[k])
        copy.start()
        loads.append(copy)

    barrier = pltpu.get_barrier_semaphore()
    peers = [device(-1), device(1), device(0, 1), device(0, -1), device(1, 1), device(-1, -1),
             device(0, 3), device(0, -3), device(0, 2), device(0, -2)]
    for k in range(2, GX - 1):
        peers.append((lax.rem(gx + k, GX), gy, gz))
    for k in range(1, GY):
        peers.append((gx, lax.rem(gy + k, GY), gz))
    for k in range(1, GZ):
        peers.append((gx, gy, lax.rem(gz + k, GZ)))
    for peer in peers:
        pl.semaphore_signal(barrier, inc=1, device_id=peer, device_id_type=MESH)

    zero8 = jnp.zeros((8, WID), F32)

    @pl.loop(0, 10)
    def _(zz):
        for k in range(6):
            s["SDs"][k, zz, pl.ds(HEI, 8)] = zero8
            s["SDw"][k, zz, pl.ds(HEI, 8)] = zero8
            s["B"][k, zz, pl.ds(0, 8)] = zero8

    for k in range(6):
        s["XSD"][k, pl.ds(HEI, 8)] = zero8
    for k in range(3):
        s["XB"][k, pl.ds(0, 8)] = zero8

    far_y = jnp.abs(lax.broadcasted_iota(jnp.int32, (HEI, HEI), 0) - lax.broadcasted_iota(jnp.int32, (HEI, HEI), 1))
    s["Wy"][0], s["Wy"][1] = split(tap(far_y))
    row = lax.broadcasted_iota(jnp.int32, (WID, WID), 0)
    col = lax.broadcasted_iota(jnp.int32, (WID, WID), 1)
    s["Wx"][0, 0], s["Wx"][0, 1] = split(tap(jnp.abs(row - col)))
    for j in range(4):
        inside = (row >= 32 * j) & (row < 32 * j + 32)
        right = jnp.where(inside, tap(jnp.abs(WID + row - 32 * j - col)), 0.0)
        left = jnp.where(inside, tap(jnp.abs(col + 32 - row + 32 * j)), 0.0)
        s["Wx"][1 + j, 0], s["Wx"][1 + j, 1] = split(left)
        s["Wx"][5 + j, 0], s["Wx"][5 + j, 1] = split(right)
    s["W2"][...] = kept(gx * WID + lane, GX * WID) * kept(rowi, HEI)

    s["WZ"][...] = kept(slab * DEP + lax.broadcasted_iota(jnp.int32, (DEP, WID), 0), S * DEP)

    E, R = s["E"], s["R"]
    loads[0].wait()
    loads[1].wait()

    @pl.loop(0, DEP)
    def _(z):
        b = bone[0, z].astype(F32)
        d = dens[0, z]
        E[z + 1] = b * d * d + (1.0 - b) * MARROW

    def pack(get, slots, src):
        acc = jnp.zeros((HEI, WID), F32)
        for index, k in slots:
            acc = jnp.where(lane == k, pltpu.roll(get(index), (k - src) % WID, 1), acc)
        return acc

    def turned(acc):
        full = jnp.concatenate([acc, jnp.zeros((WID - HEI, WID), F32)], axis=0)
        return jnp.transpose(full)

    def unturned(ref, number):
        got = ref[...]
        full = jnp.concatenate([got, jnp.zeros((WID - number, WID), F32)], axis=0)
        return jnp.transpose(full)[:HEI]

    s["XEs"][...] = turned(pack(lambda z: E[z + 1], [(z, z) for z in range(DEP)], WID - 1))[:8]
    loads[2].wait()
    loads[3].wait()

    @pl.loop(0, DEP)
    def _(z):
        f = 1.0 - fixed[0, z].astype(F32)
        for c in range(3):
            R[c, z] = f * load[c, 0, z]
        s["GD"][z] = 0.5 * E[z + 1] / dens[0, z]

    pl.semaphore_wait(barrier, len(peers))
    c_xe = remote(s["XEs"], s["XEr"], device(1))
    c_e = remote(E.at[DEP], E.at[0], device(0, 1))
    c_r = remote(R.at[:, 0], s["R8"], device(0, -1))
    c_xd = remote(s["XEs"], s["XDr"], device(1, 1))

    T = s["T"]
    s0, Q = s["s0"], s["Q"]

    def inplane(e, edge):
        ex = e + jnp.where(lane == 0, edge, pltpu.roll(e, 1, 1))
        return ex + jnp.where(rowi == 0, 0.0, pltpu.roll(ex, 1, 0))

    def flat(z):
        T[z + 1] = inplane(E[z + 1], pltpu.roll(s["XE"][...], lax.rem(WID - z, WID), 1))

    def start(z):
        inv = 1.0 / (DIAG * (T[z] + T[z + 1]))
        Q[z] = (1.0 - fixed[0, z].astype(F32)) * inv
        for c in range(3):
            s0[c, z + 1] = R[c, z] * inv

    c_xe.wait_recv()
    s["XE"][...] = unturned(s["XEr"], 8) * has_left
    flat(DEP - 1)
    flat(DEP - 2)
    start(DEP - 1)
    c_s = remote(s0.at[:, DEP], s0.at[:, 0], device(0, 1))
    flat(0)
    c_t = remote(T.at[1], T.at[DEP + 1], device(0, -1))
    pl.loop(1, DEP - 2)(flat)
    pl.loop(1, DEP - 1)(start)

    def columns(planes, name):
        slots = [((c, zz), 16 * c + zz) for c in range(3) for zz in planes]
        first = pack(lambda i: s0[i[0], i[1]], slots, 0)
        last = pack(lambda i: s0[i[0], i[1]], slots, WID - 1)
        s["XLs" + name][...] = turned(first)[:48]
        s["XRs" + name][...] = turned(last)[:48]
        return first, (remote(s["XLs" + name], s["XRr" + name], device(-1)),
                       remote(s["XRs" + name], s["XLr" + name], device(1)))

    first, pair = columns(range(2, 9), "1")
    s["X0"][...] = first

    def edges(got):
        for c in range(3):
            s["XSD"][2 * c, pl.ds(0, HEI)] = pltpu.roll(s["X0"][...] + got, (WID - 16 * c) % WID, 1)
            s["XSD"][2 * c + 1, pl.ds(0, HEI)] = pltpu.roll(s["X0"][...] - got, (WID - 16 * c) % WID, 1)

    def arrive(pair, name):
        for copy in pair:
            copy.wait_recv()
        s["XH"][...] = unturned(s["XRr" + name], 48) * has_right
        return unturned(s["XLr" + name], 48)

    def xstage(field, SD, shift, zz):
        for c in range(3):
            v = field[c, zz]
            h = pltpu.roll(s["XH"][...], shift(c, zz), 1)
            v1 = jnp.where(lane == WID - 1, h, pltpu.roll(v, WID - 1, 1))
            SD[2 * c, zz, pl.ds(0, HEI)] = v1 + v
            SD[2 * c + 1, zz, pl.ds(0, HEI)] = v1 - v

    def place_s(c, zz):
        return WID - 1 - 16 * c - zz

    def place_w(c, z):
        return WID - 1 - 8 * z - c

    def planar(SD, zz, y0):
        out = []
        for c in range(3):
            a0, a1 = SD[2 * c, zz, pl.ds(y0, 8)], SD[2 * c, zz, pl.ds(y0 + 1, 8)]
            b0, b1 = SD[2 * c + 1, zz, pl.ds(y0, 8)], SD[2 * c + 1, zz, pl.ds(y0 + 1, 8)]
            out += [a1 + a0, b1 + b0, a1 - a0, b1 - b0]
        return out

    A, B = s["A"], s["B"]

    def element(lo, hi, zz, y0):
        f = stress(zmodes(lo, hi))
        e = E[zz, pl.ds(y0, 8)]
        f = [None if v is None else v * e for v in f]
        up = [plus(f[c * 8 + p], f[c * 8 + 4 + p]) for c in range(3) for p in range(4)]
        down = [minus(f[c * 8 + p], f[c * 8 + 4 + p]) for c in range(3) for p in range(4)]
        return down, up

    def put(g, zz, y0, more=False):
        for c in range(3):
            for ix in range(2):
                a = g[4 * c + ix] - g[4 * c + 2 + ix]
                b = g[4 * c + ix] + g[4 * c + 2 + ix]
                if more:
                    a = a + A[2 * c + ix, zz, pl.ds(y0, 8)]
                    b = b + B[2 * c + ix, zz, pl.ds(y0 + 8, 8)]
                A[2 * c + ix, zz, pl.ds(y0, 8)] = a
                B[2 * c + ix, zz, pl.ds(y0 + 8, 8)] = b

    def both(g, h):
        return [u + v for u, v in zip(g, h)]

    def edge_elements(y0):
        lo = []
        for c in range(3):
            a0, a1 = s["XSD"][2 * c, pl.ds(y0, 8)], s["XSD"][2 * c, pl.ds(y0 + 1, 8)]
            b0, b1 = s["XSD"][2 * c + 1, pl.ds(y0, 8)], s["XSD"][2 * c + 1, pl.ds(y0 + 1, 8)]
            lo += [a1 + a0, b1 + b0, a1 - a0, b1 - b0]
        hi = [pltpu.roll(v, WID - 1, 1) for v in lo]
        f = stress(zmodes(lo, hi))
        e = s["EX"][pl.ds(y0, 8)]
        f = [None if v is None else v * e for v in f]
        for c in range(3):
            g = []
            for p in range(4):
                up = plus(f[c * 8 + p], f[c * 8 + 4 + p])
                down = minus(f[c * 8 + p], f[c * 8 + 4 + p])
                g.append(down + pltpu.roll(up, 1, 1))
            s["XA"][c, pl.ds(y0, 8)] = (g[0] - g[2]) + (g[1] - g[3])
            s["XB"][c, pl.ds(y0 + 8, 8)] = (g[0] + g[2]) + (g[1] + g[3])

    def chunks(step):
        @pl.loop(0, HEI // 8)
        def _(i):
            step(pl.multiple_of(i * 8, 8))

    w0 = s["w0"]

    def image(z, sums):
        gamma, delta, eps = sums
        q = Q[z]
        for c in range(3):
            gs = A[2 * c, z + 1] + B[2 * c, z + 1, pl.ds(7, HEI)]
            gd = A[2 * c + 1, z + 1] + B[2 * c + 1, z + 1, pl.ds(7, HEI)]
            edge = pltpu.roll(s["XA"][c] + s["XB"][c, pl.ds(7, HEI)], WID - 1 - z, 1)
            im = (gs - gd) + jnp.where(lane == 0, edge, pltpu.roll(gs + gd, 1, 1))
            w = im * q
            w0[c, z] = w
            v = s0[c, z + 1]
            gamma = gamma + fold(R[c, z] * v)
            delta = delta + fold(v * im)
            eps = eps + fold(w * im)
        return gamma, delta, eps

    s["EX"][...] = pltpu.roll(s["XE"][...], 1, 1)
    s["XL1"][...] = arrive(pair, "1")
    edges(s["XL1"][...])
    pl.loop(2, 9)(lambda zz: xstage(s0, s["SDs"], place_s, zz))

    def early(y0):
        def plane(zz, carry):
            lo, above = carry
            hi = planar(s["SDs"], zz + 1, y0)
            down, up = element(lo, hi, zz, y0)
            put(both(above, down), zz, y0)
            return tuple(hi), tuple(up)

        top = lax.fori_loop(2, DEP, plane, (tuple(planar(s["SDs"], 2, y0)), (zero8,) * 12))[1]
        put(top, DEP, y0)
        edge_elements(y0)

    chunks(early)
    sums = lax.fori_loop(2, DEP - 1, image, (zero8, zero8, zero8))

    c_xd.wait_recv()
    c_e.wait_recv()
    E[0] = E[0] * has_down
    corner = pltpu.roll(unturned(s["XDr"], 8) * (has_left * has_down), WID - 7, 1)
    T[0] = inplane(E[0], corner)
    start(0)
    s["EX"][...] = jnp.where(lane == 0, corner, s["EX"][...])
    c_r.wait_recv()
    c_t.wait_recv()
    inv8 = has_up / (DIAG * (T[DEP] + has_up * T[DEP + 1]))
    for c in range(3):
        s0[c, DEP + 1] = s["R8"][c] * inv8
    c_s.wait_recv()

    SDs, SDw, SE = s["SDs"], s["SDw"], s["SE"]

    def self_energy(low, high):
        def step(y0):
            def plane(z, lo):
                hi = planar(SDs, z + 2, y0)
                m = zmodes(lo, hi)
                SE[0, z, pl.ds(y0, 8)] = bilinear(m, stress(m))
                return tuple(hi)
            lax.fori_loop(low, high, plane, tuple(planar(SDs, low + 1, y0)))
        return step

    first, pair = columns((0, 1, 9), "2")
    chunks(self_energy(1, DEP - 1))
    s["X0"][...] = s["X0"][...] + first
    edges(s["XL1"][...] + arrive(pair, "2"))
    for zz in (0, 1, 9):
        xstage(s0, s["SDs"], place_s, zz)

    def late(y0):
        SD = s["SDs"]
        n0, n1, n2 = planar(SD, 0, y0), planar(SD, 1, y0), planar(SD, 2, y0)
        up = element(n0, n1, 0, y0)[1]
        down, above = element(n1, n2, 1, y0)
        put(both(up, down), 1, y0)
        put(above, 2, y0, more=True)
        put(element(planar(SD, 8, y0), planar(SD, 9, y0), DEP, y0)[0], DEP, y0, more=True)
        edge_elements(y0)

    chunks(late)
    sums = image(0, sums)
    c_w = remote(w0.at[:, 0], w0.at[:, DEP], device(0, -1))
    sums = image(1, sums)
    gamma, delta, eps = image(DEP - 1, sums)

    slots = [((c, z), 8 * z + c) for z in range(DEP) for c in range(3)]
    s["XWs"][...] = turned(pack(lambda i: w0[i[0], i[1]], slots, 0))[:64]
    c_xw = remote(s["XWs"], s["XWr"].at[pl.ds(0, 64)], device(-1))
    c_xc = remote(s["XWs"].at[pl.ds(0, 8)], s["XCr"], device(-1, -1))

    def energies(low, high):
        def step(y0):
            def plane(z, carry):
                los, lows = carry
                his, hiw = planar(SDs, z + 2, y0), planar(SDw, z + 1, y0)
                m = zmodes(lows, hiw)
                f = stress(m)
                SE[2, z, pl.ds(y0, 8)] = bilinear(m, f)
                SE[1, z, pl.ds(y0, 8)] = bilinear(zmodes(los, his), f)
                return tuple(his), tuple(hiw)
            lax.fori_loop(low, high, plane, (tuple(planar(SDs, low + 1, y0)), tuple(planar(SDw, low, y0))))
        return step

    def per_density(z, sums):
        zeta, m0, m1, m2 = sums
        g = s["GD"][z]
        zeta = zeta + fold(SE[2, z] * E[z + 1])
        share = s["WZ"][pl.ds(z, 1)]
        out = []
        for i, m in enumerate((m0, m1, m2)):
            v = SE[i, z] * g
            SE[i, z] = v
            out.append(m + share * fold(v * s["W2"][...]))
        return (zeta, *out)

    HLs, HRs, HLr, HRr = s["HLs"], s["HRs"], s["HLr"], s["HRr"]

    def send_sides(b):
        @pl.loop(0, 3)
        def _(i):
            acc_l = acc_r = None
            for j in range(4):
                v = SE[i, 4 * b + j]
                mine = (lane >= 32 * j) & (lane < 32 * j + 32)
                to_l = pltpu.roll(v, 32 * j, 1) if j else v
                to_r = pltpu.roll(v, (32 * j - 96) % WID, 1) if (32 * j - 96) % WID else v
                acc_l = to_l if acc_l is None else jnp.where(mine, to_l, acc_l)
                acc_r = to_r if acc_r is None else jnp.where(mine, to_r, acc_r)
            HLs[b, i] = acc_l
            HRs[b, i] = acc_r
        return remote(HLs.at[b], HRr.at[b], device(-1)), remote(HRs.at[b], HLr.at[b], device(1))

    @pl.loop(0, HEI // 8)
    def _(i):
        y0 = pl.multiple_of(i * 8, 8)
        self_energy(0, 1)(y0)
        self_energy(DEP - 1, DEP)(y0)

    c_xw.wait_recv()
    s["XH"][...] = unturned(s["XWr"], 72) * has_right
    pl.loop(0, DEP)(lambda z: xstage(w0, SDw, place_w, z))
    chunks(energies(0, DEP - 1))
    forms = lax.fori_loop(0, DEP - 1, per_density, (zero8,) * 4)
    sides = [send_sides(0)]

    c_xc.wait_recv()
    c_w.wait_recv()
    s["XWr"][pl.ds(64, 8)] = s["XCr"][...] * has_up
    s["XH"][...] = unturned(s["XWr"], 72) * has_right
    for c in range(3):
        w0[c, DEP] = w0[c, DEP] * has_up
    xstage(w0, SDw, place_w, DEP)
    chunks(energies(DEP - 1, DEP))
    forms = per_density(DEP - 1, forms)

    axes = ((GX, gx, lambda p: (p, gy, gz)), (GY, gy, lambda p: (gx, p, gz)), (GZ, gz, lambda p: (gx, gy, p)))
    own, red = s["own"], s["red"]

    def reduce_start(stage):
        n, me, target = axes[stage]
        return [remote(own.at[stage], red.at[stage, me], target(lax.rem(me + k, n))) for k in range(1, n)]

    def reduce_end(stage, copies):
        n, me, _ = axes[stage]
        for copy in copies:
            copy.wait_recv()
        red[stage, me] = own[stage]
        total = red[stage, 0]
        for k in range(1, n):
            total = total + red[stage, k]
        return total

    own[0] = jnp.concatenate([rows(v) for v in (gamma, delta, eps, *forms)] + [jnp.zeros((1, WID), F32)], axis=0)
    copies = reduce_start(0)
    sides.append(send_sides(1))

    def smooth_y(v):
        hi, lo = split(v)
        return dot(s["Wy"][0], hi) + dot(s["Wy"][1], hi) + dot(s["Wy"][0], lo)

    def smooth_x(v, k):
        hi, lo = split(v)
        return dot(hi, s["Wx"][k, 0]) + dot(hi, s["Wx"][k, 1]) + dot(lo, s["Wx"][k, 0])

    @pl.loop(0, DEP)
    def _(z):
        for i in range(3):
            SE[i, z] = smooth_y(SE[i, z])

    own[1] = reduce_end(0, copies)
    copies = reduce_start(1)

    for pair in sides:
        for copy in pair:
            copy.wait_recv()
    for b in range(2):
        @pl.loop(0, 3)
        def _(i, b=b):
            HLr[b, i] = smooth_y(HLr[b, i] * has_left)
            HRr[b, i] = smooth_y(HRr[b, i] * has_right)

    own[2] = reduce_end(1, copies)
    copies = reduce_start(2)

    for b in range(2):
        @pl.loop(0, 4)
        def _(j, b=b):
            for i in range(3):
                SE[i, 4 * b + j] = (smooth_x(SE[i, 4 * b + j], 0) + smooth_x(HLr[b, i], 1 + j)
                                    + smooth_x(HRr[b, i], 5 + j))

    total = jnp.sum(reduce_end(2, copies), axis=1, keepdims=True)
    g0, d0, ep, ze = total[0:1], total[1:2], total[2:3], total[3:4]
    alpha = g0 / d0
    g1 = g0 - 2.0 * alpha * d0 + alpha * alpha * ep
    beta = g1 / g0
    d1 = (1.0 + beta) * (1.0 + beta) * d0 - 2.0 * alpha * (1.0 + beta) * ep + alpha * alpha * ze
    alpha1 = g1 / d1
    a1 = alpha + alpha1 * (1.0 + beta)
    b1 = -(alpha1 * alpha)
    ca = jnp.broadcast_to(a1, (HEI, WID))
    cb = jnp.broadcast_to(b1, (HEI, WID))
    caa, cab, cbb = a1 * a1, 2.0 * (a1 * b1), b1 * b1
    mean = (caa * total[4:5] + cab * total[5:6] + cbb * total[6:7]) / float(S * DEP * HEI * WID * GX)
    scale = NORMAL * jnp.broadcast_to(1.0 / (mean + EPSILON), (HEI, WID))
    caa, cab, cbb = (jnp.broadcast_to(v, (HEI, WID)) for v in (caa, cab, cbb))

    G, Gup, Gdn, F = s["G"], s["Gup"], s["Gdn"], s["F"]

    @pl.loop(0, DEP)
    def _(z):
        G[z] = caa * SE[0, z] + cab * SE[1, z] + cbb * SE[2, z]

    low = G[DEP - 1]
    high = G[0]
    for k in range(1, DEP):
        low = LAMBDA * low + G[DEP - 1 - k]
        high = LAMBDA * high + G[k]
    RU, RD = s["RU"], s["RD"]
    RU[0] = low
    RD[0] = high
    near = [remote(RU.at[0], RU.at[1], device(0, -1)), remote(RD.at[0], RD.at[1], device(0, 1)),
            remote(RU.at[0], RU.at[2], device(0, -2)), remote(RD.at[0], RD.at[2], device(0, 2))]

    def planes(k):
        z = DEP - 1 - k
        return remote(G.at[k], Gup.at[k], device(0, -3)), remote(G.at[z], Gdn.at[z], device(0, 3))

    far = [planes(k) for k in range(DEP)]

    acc = None
    for z in range(DEP):
        acc = G[z] if z == 0 else LAMBDA * acc + G[z]
        F[z] = acc
    acc = jnp.zeros((HEI, WID), F32)
    for z in range(DEP - 2, -1, -1):
        acc = LAMBDA * (acc + G[z + 1])
        F[z] = F[z] + acc

    at1, at2, at3 = flag(slab + 1 < S), flag(slab + 2 < S), flag(slab + 3 < S)
    bt1, bt2, bt3 = flag(slab >= 1), flag(slab >= 2), flag(slab >= 3)

    @pl.loop(0, DEP)
    def _(z):
        for c in range(3):
            s["U"][c, 0, z] = ca * s0[c, z + 1] + cb * w0[c, z]

    stores = [pltpu.make_async_copy(s["U"], out_u, s["local"].at[4])]
    stores[0].start()

    for copy in near:
        copy.wait_recv()
    near_u = at1 * RU[1] + (LAMBDA**DEP * at2) * RU[2]
    near_d = bt1 * RD[1] + (LAMBDA**DEP * bt2) * RD[2]
    for z in range(DEP):
        F[z] = F[z] + LAMBDA ** (DEP - z) * near_u + LAMBDA ** (z + 1) * near_d

    up_scale, dn_scale = at3 * LAMBDA**RAD, bt3 * LAMBDA**RAD
    RR = s["RR"]

    def finish_plane(z, value):
        b = bone[0, z].astype(F32)
        new = dens[0, z] + REMODEL * b * (value * scale - 1.0)
        s["D"][0, z] = jnp.clip(new, FLOOR, CEILING)
        copy = pltpu.make_async_copy(s["D"].at[0, z], out_d.at[0, z], s["local"].at[5 + z])
        copy.start()
        stores.append(copy)

    for k in range(DEP):
        z = DEP - 1 - k
        far[k][0].wait_recv()
        far[k][1].wait_recv()
        up = up_scale * Gup[k]
        down = dn_scale * Gdn[z]
        if k:
            up = up + (1.0 / LAMBDA) * RR[0]
            down = down + (1.0 / LAMBDA) * RR[1]
        RR[0] = up
        RR[1] = down
        if k < DEP // 2:
            F[k] = F[k] + up
            F[z] = F[z] + down
        else:
            finish_plane(k, F[k] + up)
            finish_plane(z, F[z] + down)

    for copy in stores:
        copy.wait()
    for copy in sends:
        copy.wait_send()


def on_device(sizes, density, bone, fixed, load):
    GX, GY, GZ = sizes
    copies = 4 + 2 + 4 + 3 + 4 + (GX + GY + GZ - 3) + 4 + 16
    V = pltpu.VMEM
    plane, tall, thin = (HEI, WID), (HEI + 8, WID), (48, WID)
    scratch = {
        "send": pltpu.SemaphoreType.DMA((copies,)),
        "recv": pltpu.SemaphoreType.DMA((copies,)),
        "local": pltpu.SemaphoreType.DMA((13,)),
        "U": V(load.shape, F32), "D": V(density.shape, F32),
        "dens": V(density.shape, F32), "bone": V(bone.shape, jnp.int32), "fixed": V(fixed.shape, jnp.int32),
        "load": V(load.shape, F32),
        "E": V((9, *plane), F32), "R": V((3, DEP, *plane), F32), "R8": V((3, *plane), F32),
        "T": V((10, *plane), F32), "Q": V((DEP, *plane), F32),
        "s0": V((3, 10, *plane), F32), "w0": V((3, 9, *plane), F32),
        "SDs": V((6, 10, *tall), F32), "SDw": V((6, 10, *tall), F32),
        "A": V((6, 9, *plane), F32), "B": V((6, 10, *tall), F32),
        "XSD": V((6, *tall), F32), "XA": V((3, *plane), F32), "XB": V((3, *tall), F32),
        "EX": V(plane, F32), "XE": V(plane, F32), "X0": V(plane, F32), "XH": V(plane, F32), "XL1": V(plane, F32),
        "XEs": V((8, WID), F32), "XEr": V((8, WID), F32), "XDr": V((8, WID), F32),
        "XLs1": V(thin, F32), "XRs1": V(thin, F32), "XLr1": V(thin, F32), "XRr1": V(thin, F32),
        "XLs2": V(thin, F32), "XRs2": V(thin, F32), "XLr2": V(thin, F32), "XRr2": V(thin, F32),
        "XWs": V((64, WID), F32), "XWr": V((72, WID), F32), "XCr": V((8, WID), F32),
        "SE": V((3, DEP, *plane), F32), "own": V((3, 8, WID), F32), "red": V((3, max(sizes), 8, WID), F32),
        "Wy": V((2, HEI, HEI), BF16), "Wx": V((9, 2, WID, WID), BF16), "W2": V(plane, F32), "WZ": V((DEP, WID), F32), "GD": V((DEP, *plane), F32),
        "G": V((DEP, *plane), F32), "Gup": V((DEP, *plane), F32), "Gdn": V((DEP, *plane), F32),
        "HLs": V((2, 3, *plane), F32), "HRs": V((2, 3, *plane), F32),
        "HLr": V((2, 3, *plane), F32), "HRr": V((2, 3, *plane), F32),
        "RU": V((3, *plane), F32), "RD": V((3, *plane), F32), "F": V((DEP, *plane), F32), "RR": V((2, *plane), F32),
    }
    names = list(scratch)

    def kernel(*refs):
        body(sizes, *refs[:6], dict(zip(names, refs[6:])))

    outer = pl.BlockSpec(memory_space=pltpu.HBM)
    return pl.pallas_call(
        kernel,
        out_shape=(jax.ShapeDtypeStruct(density.shape, F32), jax.ShapeDtypeStruct(load.shape, F32)),
        in_specs=[outer] * 4,
        out_specs=(outer, outer),
        scratch_shapes=[scratch[n] for n in names],
        compiler_params=pltpu.CompilerParams(
            collective_id=0, has_side_effects=True, vmem_limit_bytes=56 * 1024 * 1024),
    )(density, bone, fixed, load)


def solution(mesh):
    sizes = tuple(mesh.shape[name] for name in ("gx", "gy", "gz"))
    placed = (P("gz", "gy", None, "gx"),) * 3 + (P(None, "gz", "gy", None, "gx"),)
    return jax.shard_map(
        functools.partial(on_device, sizes),
        mesh=mesh,
        in_specs=placed,
        out_specs=(P("gz", "gy", None, "gx"), P(None, "gz", "gy", None, "gx")),
        check_vma=False,
    )
```

```python
import functools
import math

import jax
import jax.numpy as jnp
import numpy as np
from jax import lax
from jax.experimental import pallas as pl
from jax.experimental.pallas import tpu as pltpu
from jax.sharding import PartitionSpec as P

MESH = pl.DeviceIdType.MESH
RAD = 24
MARROW = 0.1
REMODEL = 0.25
FLOOR = 0.2
CEILING = 1.0
EPSILON = 1e-06
DEP = 8
HEI = 96
WID = 128
F32 = jnp.float32
BF16 = jnp.bfloat16


def element_stiffness():
    poisson = 0.3
    lame = poisson / ((1.0 + poisson) * (1.0 - 2.0 * poisson))
    shear = 0.5 / (1.0 + poisson)
    elastic = np.zeros((6, 6))
    elastic[:3, :3] = lame
    for index in range(3):
        elastic[index, index] += 2.0 * shear
        elastic[index + 3, index + 3] = shear
    points = [0.5 - 0.5 / math.sqrt(3.0), 0.5 + 0.5 / math.sqrt(3.0)]
    matrix = np.zeros((24, 24))
    for point_z in points:
        for point_y in points:
            for point_x in points:
                strain = np.zeros((6, 24))
                for corner_z in range(2):
                    for corner_y in range(2):
                        for corner_x in range(2):
                            node = 4 * corner_z + 2 * corner_y + corner_x
                            shape_x = point_x if corner_x else 1.0 - point_x
                            shape_y = point_y if corner_y else 1.0 - point_y
                            shape_z = point_z if corner_z else 1.0 - point_z
                            slope_x = 1.0 if corner_x else -1.0
                            slope_y = 1.0 if corner_y else -1.0
                            slope_z = 1.0 if corner_z else -1.0
                            along_x = slope_x * shape_y * shape_z
                            along_y = shape_x * slope_y * shape_z
                            along_z = shape_x * shape_y * slope_z
                            strain[0, node] = along_x
                            strain[1, 8 + node] = along_y
                            strain[2, 16 + node] = along_z
                            strain[3, node] = along_y
                            strain[3, 8 + node] = along_x
                            strain[4, 8 + node] = along_z
                            strain[4, 16 + node] = along_y
                            strain[5, node] = along_z
                            strain[5, 16 + node] = along_x
                matrix = matrix + strain.T @ elastic @ strain / 8.0
    return matrix


KE = element_stiffness()
HAAR1 = np.array([[1.0, 1.0], [-1.0, 1.0]])
HAAR = np.kron(np.eye(3), np.kron(HAAR1, np.kron(HAAR1, HAAR1)))
KH = HAAR @ KE @ HAAR.T / 64.0
DIAG = float(KE[0, 0])
GROUPS = ((1, 10, 20), (2, 9), (4, 17), (12, 18), (3, 22), (5, 14), (11, 21), (6, 13, 19), (7,), (15,), (23,))
LAMBDA = math.exp(-1.0 / 12.0)
NORMAL = 1.0 / (1.0 + 2.0 * sum(LAMBDA**d for d in range(1, RAD + 1)))


def stress(m):
    out = [None] * 24
    for group in GROUPS:
        first = group[0]
        diag = float(KH[first, first])
        if len(group) == 1:
            out[first] = diag * m[first]
            continue
        off = float(KH[first, group[1]])
        total = m[first]
        for k in group[1:]:
            total = total + m[k]
        common = off * total
        for k in group:
            out[k] = common if abs(diag - off) < 1e-12 else common + (diag - off) * m[k]
    return out


def bilinear(m, f):
    total = None
    for k in range(24):
        if f[k] is not None:
            total = m[k] * f[k] if total is None else total + m[k] * f[k]
    return total


def zmodes(lo, hi):
    m = [None] * 24
    for c in range(3):
        for p in range(4):
            m[c * 8 + p] = hi[c * 4 + p] + lo[c * 4 + p]
            m[c * 8 + 4 + p] = hi[c * 4 + p] - lo[c * 4 + p]
    return m


def minus(a, b):
    return -b if a is None else a - b


def plus(a, b):
    return b if a is None else a + b


def split(value):
    hi = value.astype(BF16)
    return hi, (value - hi.astype(F32)).astype(BF16)


def dot(a, b):
    return jnp.dot(a, b, preferred_element_type=F32)


def tap(distance):
    return jnp.where(distance <= RAD, NORMAL * jnp.exp(distance.astype(F32) * (-1.0 / 12.0)), 0.0)


def power(exponent):
    return jnp.exp(exponent.astype(F32) * (-1.0 / 12.0))


def kept(index, size):
    ends = power(jnp.minimum(index, RAD) + 1) + power(jnp.minimum(size - 1 - index, RAD) + 1)
    return NORMAL * (1.0 + (2.0 * LAMBDA - ends) * (1.0 / (1.0 - LAMBDA)))


def fold(value):
    return jnp.sum(value.reshape(HEI // 8, 8, WID), axis=0)


def rows(value):
    return jnp.sum(value, axis=0, keepdims=True)


def body(sizes, dens_h, bone_h, fixed_h, load_h, out_d, out_u, s):
    GX, GY, GZ = sizes
    S = GY * GZ
    gx, gy, gz = lax.axis_index("gx"), lax.axis_index("gy"), lax.axis_index("gz")
    slab = gz * GY + gy
    lane = lax.broadcasted_iota(jnp.int32, (HEI, WID), 1)
    rowi = lax.broadcasted_iota(jnp.int32, (HEI, WID), 0)

    def device(dx=0, ds=0):
        t = lax.rem(slab + ds + S, S)
        return (lax.rem(gx + dx + GX, GX), lax.rem(t, GY), lax.div(t, GY))

    def flag(cond):
        return jnp.where(cond, 1.0, 0.0).astype(F32)

    has_left, has_right = flag(gx > 0), flag(gx < GX - 1)
    has_down, has_up = flag(slab > 0), flag(slab < S - 1)

    count = [0]
    sends = []

    def remote(src, dst, target):
        k = count[0]
        count[0] += 1
        copy = pltpu.make_async_remote_copy(
            src_ref=src, dst_ref=dst, send_sem=s["send"].at[k], recv_sem=s["recv"].at[k],
            device_id=target, device_id_type=MESH)
        copy.start()
        sends.append(copy)
        return copy

    dens, bone, fixed, load = s["dens"], s["bone"], s["fixed"], s["load"]
    loads = []
    for k, (src, dst) in enumerate(((dens_h, dens), (bone_h, bone), (fixed_h, fixed), (load_h, load))):
        copy = pltpu.make_async_copy(src, dst, s["local"].at[k])
        copy.start()
        loads.append(copy)

    barrier = pltpu.get_barrier_semaphore()
    peers = [device(-1), device(1), device(0, 1), device(0, -1), device(1, 1), device(-1, -1),
             device(0, 3), device(0, -3), device(0, 2), device(0, -2)]
    NY = GZ // 2
    lo, iy = lax.div(gz, NY), lax.rem(gz, NY)
    axes = ((GX, gx, lambda p: (p, gy, gz)),
            (2 * GY, 2 * gy + lo, lambda p: (gx, lax.div(p, 2), lax.rem(p, 2) * NY + iy)),
            (NY, iy, lambda p: (gx, gy, lo * NY + p)))
    for number, me, target in axes:
        for k in range(1, number):
            if me is not gx or 1 < k < GX - 1:
                peers.append(target(lax.rem(me + k, number)))
    for peer in peers:
        pl.semaphore_signal(barrier, inc=1, device_id=peer, device_id_type=MESH)

    zero8 = jnp.zeros((8, WID), F32)

    @pl.loop(0, 10)
    def _(zz):
        for k in range(6):
            s["SDs"][k, zz, pl.ds(HEI, 8)] = zero8
            s["SDw"][k, zz, pl.ds(HEI, 8)] = zero8
            s["B"][k, zz, pl.ds(0, 8)] = zero8

    for k in range(6):
        s["XSD"][k, pl.ds(HEI, 8)] = zero8
    for k in range(3):
        s["XB"][k, pl.ds(0, 8)] = zero8

    far_y = jnp.abs(lax.broadcasted_iota(jnp.int32, (HEI, HEI), 0) - lax.broadcasted_iota(jnp.int32, (HEI, HEI), 1))
    s["Wy"][0], s["Wy"][1] = split(tap(far_y))
    row = lax.broadcasted_iota(jnp.int32, (WID, WID), 0)
    col = lax.broadcasted_iota(jnp.int32, (WID, WID), 1)
    s["Wx"][0, 0], s["Wx"][0, 1] = split(tap(jnp.abs(row - col)))
    for j in range(4):
        inside = (row >= 32 * j) & (row < 32 * j + 32)
        right = jnp.where(inside, tap(jnp.abs(WID + row - 32 * j - col)), 0.0)
        left = jnp.where(inside, tap(jnp.abs(col + 32 - row + 32 * j)), 0.0)
        s["Wx"][1 + j, 0], s["Wx"][1 + j, 1] = split(left)
        s["Wx"][5 + j, 0], s["Wx"][5 + j, 1] = split(right)
    s["W2"][...] = kept(gx * WID + lane, GX * WID) * kept(rowi, HEI)

    s["WZ"][...] = kept(slab * DEP + lax.broadcasted_iota(jnp.int32, (DEP, WID), 0), S * DEP)

    E, R = s["E"], s["R"]
    loads[0].wait()
    loads[1].wait()

    @pl.loop(0, DEP)
    def _(z):
        b = bone[0, z].astype(F32)
        d = dens[0, z]
        E[z + 1] = b * d * d + (1.0 - b) * MARROW

    def pack(get, slots, src):
        acc = jnp.zeros((HEI, WID), F32)
        for index, k in slots:
            acc = jnp.where(lane == k, pltpu.roll(get(index), (k - src) % WID, 1), acc)
        return acc

    def turned(acc):
        full = jnp.concatenate([acc, jnp.zeros((WID - HEI, WID), F32)], axis=0)
        return jnp.transpose(full)

    def unturned(ref, number):
        got = ref[...]
        full = jnp.concatenate([got, jnp.zeros((WID - number, WID), F32)], axis=0)
        return jnp.transpose(full)[:HEI]

    s["XEs"][...] = turned(pack(lambda z: E[z + 1], [(z, z) for z in range(DEP)], WID - 1))[:8]
    loads[2].wait()
    loads[3].wait()

    @pl.loop(0, DEP)
    def _(z):
        f = 1.0 - fixed[0, z].astype(F32)
        for c in range(3):
            R[c, z] = f * load[c, 0, z]
        s["GD"][z] = 0.5 * E[z + 1] / dens[0, z]

    pl.semaphore_wait(barrier, len(peers))
    c_xe = remote(s["XEs"], s["XEr"], device(1))
    c_e = remote(E.at[DEP], E.at[0], device(0, 1))
    c_r = remote(R.at[:, 0], s["R8"], device(0, -1))
    c_xd = remote(s["XEs"], s["XDr"], device(1, 1))

    T = s["T"]
    s0, Q = s["s0"], s["Q"]

    def inplane(e, edge):
        ex = e + jnp.where(lane == 0, edge, pltpu.roll(e, 1, 1))
        return ex + jnp.where(rowi == 0, 0.0, pltpu.roll(ex, 1, 0))

    def flat(z):
        T[z + 1] = inplane(E[z + 1], pltpu.roll(s["XE"][...], lax.rem(WID - z, WID), 1))

    def start(z):
        inv = 1.0 / (DIAG * (T[z] + T[z + 1]))
        Q[z] = (1.0 - fixed[0, z].astype(F32)) * inv
        for c in range(3):
            s0[c, z + 1] = R[c, z] * inv

    c_xe.wait_recv()
    s["XE"][...] = unturned(s["XEr"], 8) * has_left
    flat(DEP - 1)
    flat(DEP - 2)
    start(DEP - 1)
    c_s = remote(s0.at[:, DEP], s0.at[:, 0], device(0, 1))
    flat(0)
    c_t = remote(T.at[1], T.at[DEP + 1], device(0, -1))
    pl.loop(1, DEP - 2)(flat)
    pl.loop(1, DEP - 1)(start)

    def columns(planes, name):
        slots = [((c, zz), 16 * c + zz) for c in range(3) for zz in planes]
        first = pack(lambda i: s0[i[0], i[1]], slots, 0)
        last = pack(lambda i: s0[i[0], i[1]], slots, WID - 1)
        s["XLs" + name][...] = turned(first)[:48]
        s["XRs" + name][...] = turned(last)[:48]
        return first, (remote(s["XLs" + name], s["XRr" + name], device(-1)),
                       remote(s["XRs" + name], s["XLr" + name], device(1)))

    first, pair = columns(range(2, 9), "1")
    s["X0"][...] = first

    def edges(got):
        for c in range(3):
            s["XSD"][2 * c, pl.ds(0, HEI)] = pltpu.roll(s["X0"][...] + got, (WID - 16 * c) % WID, 1)
            s["XSD"][2 * c + 1, pl.ds(0, HEI)] = pltpu.roll(s["X0"][...] - got, (WID - 16 * c) % WID, 1)

    def arrive(pair, name):
        for copy in pair:
            copy.wait_recv()
        s["XH"][...] = unturned(s["XRr" + name], 48) * has_right
        return unturned(s["XLr" + name], 48)

    def xstage(field, SD, shift, zz):
        for c in range(3):
            v = field[c, zz]
            h = pltpu.roll(s["XH"][...], shift(c, zz), 1)
            v1 = jnp.where(lane == WID - 1, h, pltpu.roll(v, WID - 1, 1))
            SD[2 * c, zz, pl.ds(0, HEI)] = v1 + v
            SD[2 * c + 1, zz, pl.ds(0, HEI)] = v1 - v

    def place_s(c, zz):
        return WID - 1 - 16 * c - zz

    def place_w(c, z):
        return WID - 1 - 8 * z - c

    def planar(SD, zz, y0):
        out = []
        for c in range(3):
            a0, a1 = SD[2 * c, zz, pl.ds(y0, 8)], SD[2 * c, zz, pl.ds(y0 + 1, 8)]
            b0, b1 = SD[2 * c + 1, zz, pl.ds(y0, 8)], SD[2 * c + 1, zz, pl.ds(y0 + 1, 8)]
            out += [a1 + a0, b1 + b0, a1 - a0, b1 - b0]
        return out

    A, B = s["A"], s["B"]

    def element(lo, hi, zz, y0):
        f = stress(zmodes(lo, hi))
        e = E[zz, pl.ds(y0, 8)]
        f = [None if v is None else v * e for v in f]
        up = [plus(f[c * 8 + p], f[c * 8 + 4 + p]) for c in range(3) for p in range(4)]
        down = [minus(f[c * 8 + p], f[c * 8 + 4 + p]) for c in range(3) for p in range(4)]
        return down, up

    def put(g, zz, y0, more=False):
        for c in range(3):
            for ix in range(2):
                a = g[4 * c + ix] - g[4 * c + 2 + ix]
                b = g[4 * c + ix] + g[4 * c + 2 + ix]
                if more:
                    a = a + A[2 * c + ix, zz, pl.ds(y0, 8)]
                    b = b + B[2 * c + ix, zz, pl.ds(y0 + 8, 8)]
                A[2 * c + ix, zz, pl.ds(y0, 8)] = a
                B[2 * c + ix, zz, pl.ds(y0 + 8, 8)] = b

    def both(g, h):
        return [u + v for u, v in zip(g, h)]

    def edge_elements(y0):
        lo = []
        for c in range(3):
            a0, a1 = s["XSD"][2 * c, pl.ds(y0, 8)], s["XSD"][2 * c, pl.ds(y0 + 1, 8)]
            b0, b1 = s["XSD"][2 * c + 1, pl.ds(y0, 8)], s["XSD"][2 * c + 1, pl.ds(y0 + 1, 8)]
            lo += [a1 + a0, b1 + b0, a1 - a0, b1 - b0]
        hi = [pltpu.roll(v, WID - 1, 1) for v in lo]
        f = stress(zmodes(lo, hi))
        e = s["EX"][pl.ds(y0, 8)]
        f = [None if v is None else v * e for v in f]
        for c in range(3):
            g = []
            for p in range(4):
                up = plus(f[c * 8 + p], f[c * 8 + 4 + p])
                down = minus(f[c * 8 + p], f[c * 8 + 4 + p])
                g.append(down + pltpu.roll(up, 1, 1))
            s["XA"][c, pl.ds(y0, 8)] = (g[0] - g[2]) + (g[1] - g[3])
            s["XB"][c, pl.ds(y0 + 8, 8)] = (g[0] + g[2]) + (g[1] + g[3])

    def chunks(step):
        @pl.loop(0, HEI // 8)
        def _(i):
            step(pl.multiple_of(i * 8, 8))

    w0 = s["w0"]

    def image(z, sums):
        gamma, delta, eps = sums
        q = Q[z]
        for c in range(3):
            gs = A[2 * c, z + 1] + B[2 * c, z + 1, pl.ds(7, HEI)]
            gd = A[2 * c + 1, z + 1] + B[2 * c + 1, z + 1, pl.ds(7, HEI)]
            edge = pltpu.roll(s["XA"][c] + s["XB"][c, pl.ds(7, HEI)], WID - 1 - z, 1)
            im = (gs - gd) + jnp.where(lane == 0, edge, pltpu.roll(gs + gd, 1, 1))
            w = im * q
            w0[c, z] = w
            v = s0[c, z + 1]
            gamma = gamma + fold(R[c, z] * v)
            delta = delta + fold(v * im)
            eps = eps + fold(w * im)
        return gamma, delta, eps

    s["EX"][...] = pltpu.roll(s["XE"][...], 1, 1)
    s["XL1"][...] = arrive(pair, "1")
    edges(s["XL1"][...])
    pl.loop(2, 9)(lambda zz: xstage(s0, s["SDs"], place_s, zz))

    def early(y0):
        def plane(zz, carry):
            lo, above = carry
            hi = planar(s["SDs"], zz + 1, y0)
            down, up = element(lo, hi, zz, y0)
            put(both(above, down), zz, y0)
            return tuple(hi), tuple(up)

        top = lax.fori_loop(2, DEP, plane, (tuple(planar(s["SDs"], 2, y0)), (zero8,) * 12))[1]
        put(top, DEP, y0)
        edge_elements(y0)

    chunks(early)
    sums = lax.fori_loop(2, DEP - 1, image, (zero8, zero8, zero8))

    c_xd.wait_recv()
    c_e.wait_recv()
    E[0] = E[0] * has_down
    corner = pltpu.roll(unturned(s["XDr"], 8) * (has_left * has_down), WID - 7, 1)
    T[0] = inplane(E[0], corner)
    start(0)
    s["EX"][...] = jnp.where(lane == 0, corner, s["EX"][...])
    c_r.wait_recv()
    c_t.wait_recv()
    inv8 = has_up / (DIAG * (T[DEP] + has_up * T[DEP + 1]))
    for c in range(3):
        s0[c, DEP + 1] = s["R8"][c] * inv8
    c_s.wait_recv()

    SDs, SDw, SE = s["SDs"], s["SDw"], s["SE"]

    def self_energy(low, high):
        def step(y0):
            def plane(z, lo):
                hi = planar(SDs, z + 2, y0)
                m = zmodes(lo, hi)
                SE[0, z, pl.ds(y0, 8)] = bilinear(m, stress(m))
                return tuple(hi)
            lax.fori_loop(low, high, plane, tuple(planar(SDs, low + 1, y0)))
        return step

    first, pair = columns((0, 1, 9), "2")
    chunks(self_energy(1, DEP - 1))
    s["X0"][...] = s["X0"][...] + first
    edges(s["XL1"][...] + arrive(pair, "2"))
    for zz in (0, 1, 9):
        xstage(s0, s["SDs"], place_s, zz)

    def late(y0):
        SD = s["SDs"]
        n0, n1, n2 = planar(SD, 0, y0), planar(SD, 1, y0), planar(SD, 2, y0)
        up = element(n0, n1, 0, y0)[1]
        down, above = element(n1, n2, 1, y0)
        put(both(up, down), 1, y0)
        put(above, 2, y0, more=True)
        put(element(planar(SD, 8, y0), planar(SD, 9, y0), DEP, y0)[0], DEP, y0, more=True)
        edge_elements(y0)

    chunks(late)
    sums = image(0, sums)
    c_w = remote(w0.at[:, 0], w0.at[:, DEP], device(0, -1))
    sums = image(1, sums)
    gamma, delta, eps = image(DEP - 1, sums)

    slots = [((c, z), 8 * z + c) for z in range(DEP) for c in range(3)]
    s["XWs"][...] = turned(pack(lambda i: w0[i[0], i[1]], slots, 0))[:64]
    c_xw = remote(s["XWs"], s["XWr"].at[pl.ds(0, 64)], device(-1))
    c_xc = remote(s["XWs"].at[pl.ds(0, 8)], s["XCr"], device(-1, -1))

    def energies(low, high):
        def step(y0):
            def plane(z, carry):
                los, lows = carry
                his, hiw = planar(SDs, z + 2, y0), planar(SDw, z + 1, y0)
                m = zmodes(lows, hiw)
                f = stress(m)
                SE[2, z, pl.ds(y0, 8)] = bilinear(m, f)
                SE[1, z, pl.ds(y0, 8)] = bilinear(zmodes(los, his), f)
                return tuple(his), tuple(hiw)
            lax.fori_loop(low, high, plane, (tuple(planar(SDs, low + 1, y0)), tuple(planar(SDw, low, y0))))
        return step

    def per_density(z, sums):
        zeta, m0, m1, m2 = sums
        g = s["GD"][z]
        zeta = zeta + fold(SE[2, z] * E[z + 1])
        share = s["WZ"][pl.ds(z, 1)]
        out = []
        for i, m in enumerate((m0, m1, m2)):
            v = SE[i, z] * g
            SE[i, z] = v
            out.append(m + share * fold(v * s["W2"][...]))
        return (zeta, *out)

    HLs, HRs, HLr, HRr = s["HLs"], s["HRs"], s["HLr"], s["HRr"]

    def send_sides(b):
        @pl.loop(0, 3)
        def _(i):
            acc_l = acc_r = None
            for j in range(4):
                v = SE[i, 4 * b + j]
                mine = (lane >= 32 * j) & (lane < 32 * j + 32)
                to_l = pltpu.roll(v, 32 * j, 1) if j else v
                to_r = pltpu.roll(v, (32 * j - 96) % WID, 1) if (32 * j - 96) % WID else v
                acc_l = to_l if acc_l is None else jnp.where(mine, to_l, acc_l)
                acc_r = to_r if acc_r is None else jnp.where(mine, to_r, acc_r)
            HLs[b, i] = acc_l
            HRs[b, i] = acc_r
        return remote(HLs.at[b], HRr.at[b], device(-1)), remote(HRs.at[b], HLr.at[b], device(1))

    @pl.loop(0, HEI // 8)
    def _(i):
        y0 = pl.multiple_of(i * 8, 8)
        self_energy(0, 1)(y0)
        self_energy(DEP - 1, DEP)(y0)

    c_xw.wait_recv()
    s["XH"][...] = unturned(s["XWr"], 72) * has_right
    pl.loop(0, DEP)(lambda z: xstage(w0, SDw, place_w, z))
    chunks(energies(0, DEP - 1))
    forms = lax.fori_loop(0, DEP - 1, per_density, (zero8,) * 4)
    sides = [send_sides(0)]

    c_xc.wait_recv()
    c_w.wait_recv()
    s["XWr"][pl.ds(64, 8)] = s["XCr"][...] * has_up
    s["XH"][...] = unturned(s["XWr"], 72) * has_right
    for c in range(3):
        w0[c, DEP] = w0[c, DEP] * has_up
    xstage(w0, SDw, place_w, DEP)
    chunks(energies(DEP - 1, DEP))
    forms = per_density(DEP - 1, forms)

    own, red = s["own"], s["red"]

    def reduce_start(stage, row):
        own[stage, pl.ds(0, 1)] = row
        n, me, target = axes[stage]
        return [remote(own.at[stage, pl.ds(0, 1)], red.at[stage, me, pl.ds(0, 1)], target(lax.rem(me + k, n)))
                for k in range(1, n)]

    def reduce_end(stage, copies):
        n, me, _ = axes[stage]
        for copy in copies:
            copy.wait_recv()
        red[stage, me, pl.ds(0, 1)] = own[stage, pl.ds(0, 1)]
        total = red[stage, 0, pl.ds(0, 1)]
        for k in range(1, n):
            total = total + red[stage, k, pl.ds(0, 1)]
        return total

    lane1 = lax.broadcasted_iota(jnp.int32, (1, WID), 1)
    mine = jnp.zeros((1, WID), F32)
    for k, v in enumerate((gamma, delta, eps, *forms)):
        mine = jnp.where(lane1 == k, jnp.sum(rows(v), axis=1, keepdims=True), mine)
    copies = reduce_start(0, mine)
    sides.append(send_sides(1))

    def smooth_y(v):
        hi, lo = split(v)
        return dot(s["Wy"][0], hi) + dot(s["Wy"][1], hi) + dot(s["Wy"][0], lo)

    def smooth_x(v, k):
        hi, lo = split(v)
        return dot(hi, s["Wx"][k, 0]) + dot(hi, s["Wx"][k, 1]) + dot(lo, s["Wx"][k, 0])

    @pl.loop(0, DEP)
    def _(z):
        for i in range(3):
            SE[i, z] = smooth_y(SE[i, z])

    copies = reduce_start(1, reduce_end(0, copies))

    for pair in sides:
        for copy in pair:
            copy.wait_recv()
    for b in range(2):
        @pl.loop(0, 3)
        def _(i, b=b):
            HLr[b, i] = smooth_y(HLr[b, i] * has_left)
            HRr[b, i] = smooth_y(HRr[b, i] * has_right)

    copies = reduce_start(2, reduce_end(1, copies))

    for b in range(2):
        @pl.loop(0, 4)
        def _(j, b=b):
            for i in range(3):
                SE[i, 4 * b + j] = (smooth_x(SE[i, 4 * b + j], 0) + smooth_x(HLr[b, i], 1 + j)
                                    + smooth_x(HRr[b, i], 5 + j))

    total = reduce_end(2, copies)
    g0, d0, ep, ze, t0, t1, t2 = (total[:, k:k + 1] for k in range(7))
    alpha = g0 / d0
    g1 = g0 - 2.0 * alpha * d0 + alpha * alpha * ep
    beta = g1 / g0
    d1 = (1.0 + beta) * (1.0 + beta) * d0 - 2.0 * alpha * (1.0 + beta) * ep + alpha * alpha * ze
    alpha1 = g1 / d1
    a1 = alpha + alpha1 * (1.0 + beta)
    b1 = -(alpha1 * alpha)
    ca = jnp.broadcast_to(a1, (HEI, WID))
    cb = jnp.broadcast_to(b1, (HEI, WID))
    caa, cab, cbb = a1 * a1, 2.0 * (a1 * b1), b1 * b1
    mean = (caa * t0 + cab * t1 + cbb * t2) / float(S * DEP * HEI * WID * GX)
    scale = NORMAL * jnp.broadcast_to(1.0 / (mean + EPSILON), (HEI, WID))
    caa, cab, cbb = (jnp.broadcast_to(v, (HEI, WID)) for v in (caa, cab, cbb))

    G, Gup, Gdn, F = s["G"], s["Gup"], s["Gdn"], s["F"]

    def planes(k):
        z = DEP - 1 - k
        return remote(G.at[k], Gup.at[k], device(0, -3)), remote(G.at[z], Gdn.at[z], device(0, 3))

    def combine(z):
        G[z] = caa * SE[0, z] + cab * SE[1, z] + cbb * SE[2, z]

    far = []
    for k in range(DEP // 2):
        combine(k)
        combine(DEP - 1 - k)
        far.append(planes(k))

    low = G[DEP - 1]
    high = G[0]
    for k in range(1, DEP):
        low = LAMBDA * low + G[DEP - 1 - k]
        high = LAMBDA * high + G[k]
    RU, RD = s["RU"], s["RD"]
    RU[0] = low
    RD[0] = high
    near = [remote(RU.at[0], RU.at[1], device(0, -1)), remote(RD.at[0], RD.at[1], device(0, 1)),
            remote(RU.at[0], RU.at[2], device(0, -2)), remote(RD.at[0], RD.at[2], device(0, 2))]
    far += [planes(k) for k in range(DEP // 2, DEP)]

    acc = None
    for z in range(DEP):
        acc = G[z] if z == 0 else LAMBDA * acc + G[z]
        F[z] = acc
    acc = jnp.zeros((HEI, WID), F32)
    for z in range(DEP - 2, -1, -1):
        acc = LAMBDA * (acc + G[z + 1])
        F[z] = F[z] + acc

    at1, at2, at3 = flag(slab + 1 < S), flag(slab + 2 < S), flag(slab + 3 < S)
    bt1, bt2, bt3 = flag(slab >= 1), flag(slab >= 2), flag(slab >= 3)

    @pl.loop(0, DEP)
    def _(z):
        for c in range(3):
            s["U"][c, 0, z] = ca * s0[c, z + 1] + cb * w0[c, z]

    stores = [pltpu.make_async_copy(s["U"], out_u, s["local"].at[4])]
    stores[0].start()

    for copy in near:
        copy.wait_recv()
    near_u = at1 * RU[1] + (LAMBDA**DEP * at2) * RU[2]
    near_d = bt1 * RD[1] + (LAMBDA**DEP * bt2) * RD[2]
    for z in range(DEP):
        F[z] = F[z] + LAMBDA ** (DEP - z) * near_u + LAMBDA ** (z + 1) * near_d

    up_scale, dn_scale = at3 * LAMBDA**RAD, bt3 * LAMBDA**RAD
    RR = s["RR"]

    def finish_plane(z, value):
        b = bone[0, z].astype(F32)
        new = dens[0, z] + REMODEL * b * (value * scale - 1.0)
        s["D"][0, z] = jnp.clip(new, FLOOR, CEILING)
        copy = pltpu.make_async_copy(s["D"].at[0, z], out_d.at[0, z], s["local"].at[5 + z])
        copy.start()
        stores.append(copy)

    for k in range(DEP):
        z = DEP - 1 - k
        far[k][0].wait_recv()
        far[k][1].wait_recv()
        up = up_scale * Gup[k]
        down = dn_scale * Gdn[z]
        if k:
            up = up + (1.0 / LAMBDA) * RR[0]
            down = down + (1.0 / LAMBDA) * RR[1]
        RR[0] = up
        RR[1] = down
        if k < DEP // 2:
            F[k] = F[k] + up
            F[z] = F[z] + down
        else:
            finish_plane(k, F[k] + up)
            finish_plane(z, F[z] + down)

    for copy in stores:
        copy.wait()
    for copy in sends:
        copy.wait_send()


def on_device(sizes, density, bone, fixed, load):
    GX, GY, GZ = sizes
    copies = 4 + 2 + 4 + 3 + 4 + (GX + 2 * GY + GZ // 2 - 3) + 4 + 16
    V = pltpu.VMEM
    plane, tall, thin = (HEI, WID), (HEI + 8, WID), (48, WID)
    scratch = {
        "send": pltpu.SemaphoreType.DMA((copies,)),
        "recv": pltpu.SemaphoreType.DMA((copies,)),
        "local": pltpu.SemaphoreType.DMA((13,)),
        "U": V(load.shape, F32), "D": V(density.shape, F32),
        "dens": V(density.shape, F32), "bone": V(bone.shape, jnp.int32), "fixed": V(fixed.shape, jnp.int32),
        "load": V(load.shape, F32),
        "E": V((9, *plane), F32), "R": V((3, DEP, *plane), F32), "R8": V((3, *plane), F32),
        "T": V((10, *plane), F32), "Q": V((DEP, *plane), F32),
        "s0": V((3, 10, *plane), F32), "w0": V((3, 9, *plane), F32),
        "SDs": V((6, 10, *tall), F32), "SDw": V((6, 10, *tall), F32),
        "A": V((6, 9, *plane), F32), "B": V((6, 10, *tall), F32),
        "XSD": V((6, *tall), F32), "XA": V((3, *plane), F32), "XB": V((3, *tall), F32),
        "EX": V(plane, F32), "XE": V(plane, F32), "X0": V(plane, F32), "XH": V(plane, F32), "XL1": V(plane, F32),
        "XEs": V((8, WID), F32), "XEr": V((8, WID), F32), "XDr": V((8, WID), F32),
        "XLs1": V(thin, F32), "XRs1": V(thin, F32), "XLr1": V(thin, F32), "XRr1": V(thin, F32),
        "XLs2": V(thin, F32), "XRs2": V(thin, F32), "XLr2": V(thin, F32), "XRr2": V(thin, F32),
        "XWs": V((64, WID), F32), "XWr": V((72, WID), F32), "XCr": V((8, WID), F32),
        "SE": V((3, DEP, *plane), F32), "own": V((3, 8, WID), F32), "red": V((3, max(GX, 2 * GY, GZ // 2), 8, WID), F32),
        "Wy": V((2, HEI, HEI), BF16), "Wx": V((9, 2, WID, WID), BF16), "W2": V(plane, F32), "WZ": V((DEP, WID), F32), "GD": V((DEP, *plane), F32),
        "G": V((DEP, *plane), F32), "Gup": V((DEP, *plane), F32), "Gdn": V((DEP, *plane), F32),
        "HLs": V((2, 3, *plane), F32), "HRs": V((2, 3, *plane), F32),
        "HLr": V((2, 3, *plane), F32), "HRr": V((2, 3, *plane), F32),
        "RU": V((3, *plane), F32), "RD": V((3, *plane), F32), "F": V((DEP, *plane), F32), "RR": V((2, *plane), F32),
    }
    names = list(scratch)

    def kernel(*refs):
        body(sizes, *refs[:6], dict(zip(names, refs[6:])))

    outer = pl.BlockSpec(memory_space=pltpu.HBM)
    results = pl.pallas_call(
        kernel,
        out_shape=(jax.ShapeDtypeStruct(density.shape, F32), jax.ShapeDtypeStruct(load.shape, F32)),
        in_specs=[outer] * 4,
        out_specs=(outer, outer),
        scratch_shapes=[scratch[n] for n in names],
        compiler_params=pltpu.CompilerParams(
            collective_id=0, has_side_effects=True, vmem_limit_bytes=56 * 1024 * 1024),
    )(density, bone, fixed, load)

    def hand_over(d, u, out_d, out_u, sem):
        moves = [pltpu.make_async_copy(d.at[0, pl.ds(4 * k, 4)], out_d.at[0, pl.ds(4 * k, 4)], sem.at[k]) for k in range(2)]
        moves += [pltpu.make_async_copy(u.at[c, 0, pl.ds(4 * k, 4)], out_u.at[c, 0, pl.ds(4 * k, 4)], sem.at[2 + 2 * c + k])
                  for c in range(3) for k in range(2)]
        for move in moves:
            move.start()
        for move in moves:
            move.wait()

    return pl.pallas_call(
        hand_over,
        out_shape=tuple(jax.ShapeDtypeStruct(v.shape, F32) for v in results),
        in_specs=[outer] * 2,
        out_specs=(outer, outer),
        scratch_shapes=[pltpu.SemaphoreType.DMA((8,))],
    )(*results)


def solution(mesh):
    sizes = tuple(mesh.shape[name] for name in ("gx", "gy", "gz"))
    placed = (P("gz", "gy", None, "gx"),) * 3 + (P(None, "gz", "gy", None, "gx"),)
    return jax.shard_map(
        functools.partial(on_device, sizes),
        mesh=mesh,
        in_specs=placed,
        out_specs=(P("gz", "gy", None, "gx"), P(None, "gz", "gy", None, "gx")),
        check_vma=False,
    )
```

```python
import functools
import math

import jax
import jax.numpy as jnp
import numpy as np
from jax import lax
from jax.experimental import pallas as pl
from jax.experimental.pallas import tpu as pltpu
from jax.sharding import PartitionSpec as P

MESH = pl.DeviceIdType.MESH
RAD = 24
MARROW = 0.1
REMODEL = 0.25
FLOOR = 0.2
CEILING = 1.0
EPSILON = 1e-06
DEP = 8
HEI = 96
WID = 128
PIECES = 1
F32 = jnp.float32
BF16 = jnp.bfloat16


def element_stiffness():
    poisson = 0.3
    lame = poisson / ((1.0 + poisson) * (1.0 - 2.0 * poisson))
    shear = 0.5 / (1.0 + poisson)
    elastic = np.zeros((6, 6))
    elastic[:3, :3] = lame
    for index in range(3):
        elastic[index, index] += 2.0 * shear
        elastic[index + 3, index + 3] = shear
    points = [0.5 - 0.5 / math.sqrt(3.0), 0.5 + 0.5 / math.sqrt(3.0)]
    matrix = np.zeros((24, 24))
    for point_z in points:
        for point_y in points:
            for point_x in points:
                strain = np.zeros((6, 24))
                for corner_z in range(2):
                    for corner_y in range(2):
                        for corner_x in range(2):
                            node = 4 * corner_z + 2 * corner_y + corner_x
                            shape_x = point_x if corner_x else 1.0 - point_x
                            shape_y = point_y if corner_y else 1.0 - point_y
                            shape_z = point_z if corner_z else 1.0 - point_z
                            slope_x = 1.0 if corner_x else -1.0
                            slope_y = 1.0 if corner_y else -1.0
                            slope_z = 1.0 if corner_z else -1.0
                            along_x = slope_x * shape_y * shape_z
                            along_y = shape_x * slope_y * shape_z
                            along_z = shape_x * shape_y * slope_z
                            strain[0, node] = along_x
                            strain[1, 8 + node] = along_y
                            strain[2, 16 + node] = along_z
                            strain[3, node] = along_y
                            strain[3, 8 + node] = along_x
                            strain[4, 8 + node] = along_z
                            strain[4, 16 + node] = along_y
                            strain[5, node] = along_z
                            strain[5, 16 + node] = along_x
                matrix = matrix + strain.T @ elastic @ strain / 8.0
    return matrix


KE = element_stiffness()
HAAR1 = np.array([[1.0, 1.0], [-1.0, 1.0]])
HAAR = np.kron(np.eye(3), np.kron(HAAR1, np.kron(HAAR1, HAAR1)))
KH = HAAR @ KE @ HAAR.T / 64.0
DIAG = float(KE[0, 0])
GROUPS = ((1, 10, 20), (2, 9), (4, 17), (12, 18), (3, 22), (5, 14), (11, 21), (6, 13, 19), (7,), (15,), (23,))
LAMBDA = math.exp(-1.0 / 12.0)
NORMAL = 1.0 / (1.0 + 2.0 * sum(LAMBDA**d for d in range(1, RAD + 1)))


def stress(m):
    out = [None] * 24
    for group in GROUPS:
        first = group[0]
        diag = float(KH[first, first])
        if len(group) == 1:
            out[first] = diag * m[first]
            continue
        off = float(KH[first, group[1]])
        total = m[first]
        for k in group[1:]:
            total = total + m[k]
        common = off * total
        for k in group:
            out[k] = common if abs(diag - off) < 1e-12 else common + (diag - off) * m[k]
    return out


def bilinear(m, f):
    total = None
    for k in range(24):
        if f[k] is not None:
            total = m[k] * f[k] if total is None else total + m[k] * f[k]
    return total


def zmodes(lo, hi):
    m = [None] * 24
    for c in range(3):
        for p in range(4):
            m[c * 8 + p] = hi[c * 4 + p] + lo[c * 4 + p]
            m[c * 8 + 4 + p] = hi[c * 4 + p] - lo[c * 4 + p]
    return m


def minus(a, b):
    return -b if a is None else a - b


def plus(a, b):
    return b if a is None else a + b


def split(value):
    hi = value.astype(BF16)
    return hi, (value - hi.astype(F32)).astype(BF16)


def dot(a, b):
    return jnp.dot(a, b, preferred_element_type=F32)


def tap(distance):
    return jnp.where(distance <= RAD, NORMAL * jnp.exp(distance.astype(F32) * (-1.0 / 12.0)), 0.0)


def power(exponent):
    return jnp.exp(exponent.astype(F32) * (-1.0 / 12.0))


def kept(index, size):
    ends = power(jnp.minimum(index, RAD) + 1) + power(jnp.minimum(size - 1 - index, RAD) + 1)
    return NORMAL * (1.0 + (2.0 * LAMBDA - ends) * (1.0 / (1.0 - LAMBDA)))


def fold(value):
    return jnp.sum(value.reshape(HEI // 8, 8, WID), axis=0)


def rows(value):
    return jnp.sum(value, axis=0, keepdims=True)


def body(sizes, dens_h, bone_h, fixed_h, load_h, out_d, out_u, s):
    GX, GY, GZ = sizes
    S = GY * GZ
    gx, gy, gz = lax.axis_index("gx"), lax.axis_index("gy"), lax.axis_index("gz")
    slab = gz * GY + gy
    lane = lax.broadcasted_iota(jnp.int32, (HEI, WID), 1)
    rowi = lax.broadcasted_iota(jnp.int32, (HEI, WID), 0)

    def device(dx=0, ds=0):
        t = lax.rem(slab + ds + S, S)
        return (lax.rem(gx + dx + GX, GX), lax.rem(t, GY), lax.div(t, GY))

    def flag(cond):
        return jnp.where(cond, 1.0, 0.0).astype(F32)

    has_left, has_right = flag(gx > 0), flag(gx < GX - 1)
    has_down, has_up = flag(slab > 0), flag(slab < S - 1)

    count = [0]
    sends = []

    def remote(src, dst, target):
        k = count[0]
        count[0] += 1
        copy = pltpu.make_async_remote_copy(
            src_ref=src, dst_ref=dst, send_sem=s["send"].at[k], recv_sem=s["recv"].at[k],
            device_id=target, device_id_type=MESH)
        copy.start()
        sends.append(copy)
        return copy

    dens, bone, fixed, load = s["dens"], s["bone"], s["fixed"], s["load"]
    loads = []
    for k, (src, dst) in enumerate(((dens_h, dens), (bone_h, bone), (fixed_h, fixed), (load_h, load))):
        copy = pltpu.make_async_copy(src, dst, s["local"].at[k])
        copy.start()
        loads.append(copy)

    barrier = pltpu.get_barrier_semaphore()
    peers = [device(-1), device(1), device(0, 1), device(0, -1), device(1, 1), device(-1, -1),
             device(0, 3), device(0, -3), device(0, 2), device(0, -2)]
    NY = GZ // 2
    lo, iy = lax.div(gz, NY), lax.rem(gz, NY)
    axes = ((GX, gx, lambda p: (p, gy, gz)),
            (2 * GY, 2 * gy + lo, lambda p: (gx, lax.div(p, 2), lax.rem(p, 2) * NY + iy)),
            (NY, iy, lambda p: (gx, gy, lo * NY + p)))
    for number, me, target in axes:
        for k in range(1, number):
            if me is not gx or 1 < k < GX - 1:
                peers.append(target(lax.rem(me + k, number)))
    for peer in peers:
        pl.semaphore_signal(barrier, inc=1, device_id=peer, device_id_type=MESH)

    zero8 = jnp.zeros((8, WID), F32)

    @pl.loop(0, 10)
    def _(zz):
        for k in range(6):
            s["SDs"][k, zz, pl.ds(HEI, 8)] = zero8
            s["SDw"][k, zz, pl.ds(HEI, 8)] = zero8
            s["B"][k, zz, pl.ds(0, 8)] = zero8

    for k in range(6):
        s["XSD"][k, pl.ds(HEI, 8)] = zero8
    for k in range(3):
        s["XB"][k, pl.ds(0, 8)] = zero8

    far_y = jnp.abs(lax.broadcasted_iota(jnp.int32, (HEI, HEI), 0) - lax.broadcasted_iota(jnp.int32, (HEI, HEI), 1))
    s["Wy"][0], s["Wy"][1] = split(tap(far_y))
    row = lax.broadcasted_iota(jnp.int32, (WID, WID), 0)
    col = lax.broadcasted_iota(jnp.int32, (WID, WID), 1)
    s["Wx"][0, 0], s["Wx"][0, 1] = split(tap(jnp.abs(row - col)))
    for j in range(4):
        inside = (row >= 32 * j) & (row < 32 * j + 32)
        right = jnp.where(inside, tap(jnp.abs(WID + row - 32 * j - col)), 0.0)
        left = jnp.where(inside, tap(jnp.abs(col + 32 - row + 32 * j)), 0.0)
        s["Wx"][1 + j, 0], s["Wx"][1 + j, 1] = split(left)
        s["Wx"][5 + j, 0], s["Wx"][5 + j, 1] = split(right)
    s["W2"][...] = kept(gx * WID + lane, GX * WID) * kept(rowi, HEI)

    s["WZ"][...] = kept(slab * DEP + lax.broadcasted_iota(jnp.int32, (DEP, WID), 0), S * DEP)

    E, R = s["E"], s["R"]
    loads[0].wait()
    loads[1].wait()

    @pl.loop(0, DEP)
    def _(z):
        b = bone[0, z].astype(F32)
        d = dens[0, z]
        E[z + 1] = b * d * d + (1.0 - b) * MARROW

    def pack(get, slots, src):
        acc = jnp.zeros((HEI, WID), F32)
        for index, k in slots:
            acc = jnp.where(lane == k, pltpu.roll(get(index), (k - src) % WID, 1), acc)
        return acc

    def turned(acc):
        full = jnp.concatenate([acc, jnp.zeros((WID - HEI, WID), F32)], axis=0)
        return jnp.transpose(full)

    def unturned(ref, number):
        got = ref[...]
        full = jnp.concatenate([got, jnp.zeros((WID - number, WID), F32)], axis=0)
        return jnp.transpose(full)[:HEI]

    s["XEs"][...] = turned(pack(lambda z: E[z + 1], [(z, z) for z in range(DEP)], WID - 1))[:8]
    loads[2].wait()
    loads[3].wait()

    @pl.loop(0, DEP)
    def _(z):
        f = 1.0 - fixed[0, z].astype(F32)
        for c in range(3):
            R[c, z] = f * load[c, 0, z]
        s["GD"][z] = 0.5 * E[z + 1] / dens[0, z]

    pl.semaphore_wait(barrier, len(peers))
    c_xe = remote(s["XEs"], s["XEr"], device(1))
    c_e = remote(E.at[DEP], E.at[0], device(0, 1))
    c_r = remote(R.at[:, 0], s["R8"], device(0, -1))
    c_xd = remote(s["XEs"], s["XDr"], device(1, 1))

    T = s["T"]
    s0, Q = s["s0"], s["Q"]

    def inplane(e, edge):
        ex = e + jnp.where(lane == 0, edge, pltpu.roll(e, 1, 1))
        return ex + jnp.where(rowi == 0, 0.0, pltpu.roll(ex, 1, 0))

    def flat(z):
        T[z + 1] = inplane(E[z + 1], pltpu.roll(s["XE"][...], lax.rem(WID - z, WID), 1))

    def start(z):
        inv = 1.0 / (DIAG * (T[z] + T[z + 1]))
        Q[z] = (1.0 - fixed[0, z].astype(F32)) * inv
        for c in range(3):
            s0[c, z + 1] = R[c, z] * inv

    c_xe.wait_recv()
    s["XE"][...] = unturned(s["XEr"], 8) * has_left
    flat(DEP - 1)
    flat(DEP - 2)
    start(DEP - 1)
    c_s = remote(s0.at[:, DEP], s0.at[:, 0], device(0, 1))
    flat(0)
    c_t = remote(T.at[1], T.at[DEP + 1], device(0, -1))
    pl.loop(1, DEP - 2)(flat)
    pl.loop(1, DEP - 1)(start)

    def columns(planes, name):
        slots = [((c, zz), 16 * c + zz) for c in range(3) for zz in planes]
        first = pack(lambda i: s0[i[0], i[1]], slots, 0)
        last = pack(lambda i: s0[i[0], i[1]], slots, WID - 1)
        s["XLs" + name][...] = turned(first)[:48]
        s["XRs" + name][...] = turned(last)[:48]
        return first, (remote(s["XLs" + name], s["XRr" + name], device(-1)),
                       remote(s["XRs" + name], s["XLr" + name], device(1)))

    first, pair = columns(range(2, 9), "1")
    s["X0"][...] = first

    def edges(got):
        for c in range(3):
            s["XSD"][2 * c, pl.ds(0, HEI)] = pltpu.roll(s["X0"][...] + got, (WID - 16 * c) % WID, 1)
            s["XSD"][2 * c + 1, pl.ds(0, HEI)] = pltpu.roll(s["X0"][...] - got, (WID - 16 * c) % WID, 1)

    def arrive(pair, name):
        for copy in pair:
            copy.wait_recv()
        s["XH"][...] = unturned(s["XRr" + name], 48) * has_right
        return unturned(s["XLr" + name], 48)

    def xstage(field, SD, shift, zz):
        for c in range(3):
            v = field[c, zz]
            h = pltpu.roll(s["XH"][...], shift(c, zz), 1)
            v1 = jnp.where(lane == WID - 1, h, pltpu.roll(v, WID - 1, 1))
            SD[2 * c, zz, pl.ds(0, HEI)] = v1 + v
            SD[2 * c + 1, zz, pl.ds(0, HEI)] = v1 - v

    def place_s(c, zz):
        return WID - 1 - 16 * c - zz

    def place_w(c, z):
        return WID - 1 - 8 * z - c

    def planar(SD, zz, y0):
        out = []
        for c in range(3):
            a0, a1 = SD[2 * c, zz, pl.ds(y0, 8)], SD[2 * c, zz, pl.ds(y0 + 1, 8)]
            b0, b1 = SD[2 * c + 1, zz, pl.ds(y0, 8)], SD[2 * c + 1, zz, pl.ds(y0 + 1, 8)]
            out += [a1 + a0, b1 + b0, a1 - a0, b1 - b0]
        return out

    A, B = s["A"], s["B"]

    def element(lo, hi, zz, y0):
        f = stress(zmodes(lo, hi))
        e = E[zz, pl.ds(y0, 8)]
        f = [None if v is None else v * e for v in f]
        up = [plus(f[c * 8 + p], f[c * 8 + 4 + p]) for c in range(3) for p in range(4)]
        down = [minus(f[c * 8 + p], f[c * 8 + 4 + p]) for c in range(3) for p in range(4)]
        return down, up

    def put(g, zz, y0, more=False):
        for c in range(3):
            for ix in range(2):
                a = g[4 * c + ix] - g[4 * c + 2 + ix]
                b = g[4 * c + ix] + g[4 * c + 2 + ix]
                if more:
                    a = a + A[2 * c + ix, zz, pl.ds(y0, 8)]
                    b = b + B[2 * c + ix, zz, pl.ds(y0 + 8, 8)]
                A[2 * c + ix, zz, pl.ds(y0, 8)] = a
                B[2 * c + ix, zz, pl.ds(y0 + 8, 8)] = b

    def both(g, h):
        return [u + v for u, v in zip(g, h)]

    def edge_elements(y0):
        lo = []
        for c in range(3):
            a0, a1 = s["XSD"][2 * c, pl.ds(y0, 8)], s["XSD"][2 * c, pl.ds(y0 + 1, 8)]
            b0, b1 = s["XSD"][2 * c + 1, pl.ds(y0, 8)], s["XSD"][2 * c + 1, pl.ds(y0 + 1, 8)]
            lo += [a1 + a0, b1 + b0, a1 - a0, b1 - b0]
        hi = [pltpu.roll(v, WID - 1, 1) for v in lo]
        f = stress(zmodes(lo, hi))
        e = s["EX"][pl.ds(y0, 8)]
        f = [None if v is None else v * e for v in f]
        for c in range(3):
            g = []
            for p in range(4):
                up = plus(f[c * 8 + p], f[c * 8 + 4 + p])
                down = minus(f[c * 8 + p], f[c * 8 + 4 + p])
                g.append(down + pltpu.roll(up, 1, 1))
            s["XA"][c, pl.ds(y0, 8)] = (g[0] - g[2]) + (g[1] - g[3])
            s["XB"][c, pl.ds(y0 + 8, 8)] = (g[0] + g[2]) + (g[1] + g[3])

    def chunks(step):
        @pl.loop(0, HEI // 8)
        def _(i):
            step(pl.multiple_of(i * 8, 8))

    w0 = s["w0"]

    def image(z, sums):
        gamma, delta, eps = sums
        q = Q[z]
        for c in range(3):
            gs = A[2 * c, z + 1] + B[2 * c, z + 1, pl.ds(7, HEI)]
            gd = A[2 * c + 1, z + 1] + B[2 * c + 1, z + 1, pl.ds(7, HEI)]
            edge = pltpu.roll(s["XA"][c] + s["XB"][c, pl.ds(7, HEI)], WID - 1 - z, 1)
            im = (gs - gd) + jnp.where(lane == 0, edge, pltpu.roll(gs + gd, 1, 1))
            w = im * q
            w0[c, z] = w
            v = s0[c, z + 1]
            gamma = gamma + fold(R[c, z] * v)
            delta = delta + fold(v * im)
            eps = eps + fold(w * im)
        return gamma, delta, eps

    s["EX"][...] = pltpu.roll(s["XE"][...], 1, 1)
    s["XL1"][...] = arrive(pair, "1")
    edges(s["XL1"][...])
    pl.loop(2, 9)(lambda zz: xstage(s0, s["SDs"], place_s, zz))

    def early(y0):
        def plane(zz, carry):
            lo, above = carry
            hi = planar(s["SDs"], zz + 1, y0)
            down, up = element(lo, hi, zz, y0)
            put(both(above, down), zz, y0)
            return tuple(hi), tuple(up)

        top = lax.fori_loop(2, DEP, plane, (tuple(planar(s["SDs"], 2, y0)), (zero8,) * 12))[1]
        put(top, DEP, y0)
        edge_elements(y0)

    chunks(early)
    sums = lax.fori_loop(2, DEP - 1, image, (zero8, zero8, zero8))

    c_xd.wait_recv()
    c_e.wait_recv()
    E[0] = E[0] * has_down
    corner = pltpu.roll(unturned(s["XDr"], 8) * (has_left * has_down), WID - 7, 1)
    T[0] = inplane(E[0], corner)
    start(0)
    s["EX"][...] = jnp.where(lane == 0, corner, s["EX"][...])
    c_r.wait_recv()
    c_t.wait_recv()
    inv8 = has_up / (DIAG * (T[DEP] + has_up * T[DEP + 1]))
    for c in range(3):
        s0[c, DEP + 1] = s["R8"][c] * inv8
    c_s.wait_recv()

    SDs, SDw, SE = s["SDs"], s["SDw"], s["SE"]

    def self_energy(low, high):
        def step(y0):
            def plane(z, lo):
                hi = planar(SDs, z + 2, y0)
                m = zmodes(lo, hi)
                SE[0, z, pl.ds(y0, 8)] = bilinear(m, stress(m))
                return tuple(hi)
            lax.fori_loop(low, high, plane, tuple(planar(SDs, low + 1, y0)))
        return step

    first, pair = columns((0, 1, 9), "2")
    chunks(self_energy(1, DEP - 1))
    s["X0"][...] = s["X0"][...] + first
    edges(s["XL1"][...] + arrive(pair, "2"))
    for zz in (0, 1, 9):
        xstage(s0, s["SDs"], place_s, zz)

    def late(y0):
        SD = s["SDs"]
        n0, n1, n2 = planar(SD, 0, y0), planar(SD, 1, y0), planar(SD, 2, y0)
        up = element(n0, n1, 0, y0)[1]
        down, above = element(n1, n2, 1, y0)
        put(both(up, down), 1, y0)
        put(above, 2, y0, more=True)
        put(element(planar(SD, 8, y0), planar(SD, 9, y0), DEP, y0)[0], DEP, y0, more=True)
        edge_elements(y0)

    chunks(late)
    sums = image(0, sums)
    c_w = remote(w0.at[:, 0], w0.at[:, DEP], device(0, -1))
    sums = image(1, sums)
    gamma, delta, eps = image(DEP - 1, sums)

    slots = [((c, z), 8 * z + c) for z in range(DEP) for c in range(3)]
    s["XWs"][...] = turned(pack(lambda i: w0[i[0], i[1]], slots, 0))[:64]
    c_xw = remote(s["XWs"], s["XWr"].at[pl.ds(0, 64)], device(-1))
    c_xc = remote(s["XWs"].at[pl.ds(0, 8)], s["XCr"], device(-1, -1))

    def energies(low, high):
        def step(y0):
            def plane(z, carry):
                los, lows = carry
                his, hiw = planar(SDs, z + 2, y0), planar(SDw, z + 1, y0)
                m = zmodes(lows, hiw)
                f = stress(m)
                SE[2, z, pl.ds(y0, 8)] = bilinear(m, f)
                SE[1, z, pl.ds(y0, 8)] = bilinear(zmodes(los, his), f)
                return tuple(his), tuple(hiw)
            lax.fori_loop(low, high, plane, (tuple(planar(SDs, low + 1, y0)), tuple(planar(SDw, low, y0))))
        return step

    def per_density(z, sums):
        zeta, m0, m1, m2 = sums
        g = s["GD"][z]
        zeta = zeta + fold(SE[2, z] * E[z + 1])
        share = s["WZ"][pl.ds(z, 1)]
        out = []
        for i, m in enumerate((m0, m1, m2)):
            v = SE[i, z] * g
            SE[i, z] = v
            out.append(m + share * fold(v * s["W2"][...]))
        return (zeta, *out)

    HLs, HRs, HLr, HRr = s["HLs"], s["HRs"], s["HLr"], s["HRr"]

    def send_sides(b):
        @pl.loop(0, 3)
        def _(i):
            acc_l = acc_r = None
            for j in range(4):
                v = SE[i, 4 * b + j]
                mine = (lane >= 32 * j) & (lane < 32 * j + 32)
                to_l = pltpu.roll(v, 32 * j, 1) if j else v
                to_r = pltpu.roll(v, (32 * j - 96) % WID, 1) if (32 * j - 96) % WID else v
                acc_l = to_l if acc_l is None else jnp.where(mine, to_l, acc_l)
                acc_r = to_r if acc_r is None else jnp.where(mine, to_r, acc_r)
            HLs[b, i] = acc_l
            HRs[b, i] = acc_r
        return remote(HLs.at[b], HRr.at[b], device(-1)), remote(HRs.at[b], HLr.at[b], device(1))

    @pl.loop(0, HEI // 8)
    def _(i):
        y0 = pl.multiple_of(i * 8, 8)
        self_energy(0, 1)(y0)
        self_energy(DEP - 1, DEP)(y0)

    c_xw.wait_recv()
    s["XH"][...] = unturned(s["XWr"], 72) * has_right
    pl.loop(0, DEP)(lambda z: xstage(w0, SDw, place_w, z))
    chunks(energies(0, DEP - 1))
    forms = lax.fori_loop(0, DEP - 1, per_density, (zero8,) * 4)
    sides = [send_sides(0)]

    c_xc.wait_recv()
    c_w.wait_recv()
    s["XWr"][pl.ds(64, 8)] = s["XCr"][...] * has_up
    s["XH"][...] = unturned(s["XWr"], 72) * has_right
    for c in range(3):
        w0[c, DEP] = w0[c, DEP] * has_up
    xstage(w0, SDw, place_w, DEP)
    chunks(energies(DEP - 1, DEP))
    forms = per_density(DEP - 1, forms)

    own, red = s["own"], s["red"]

    def reduce_start(stage, row):
        own[stage, pl.ds(0, 1)] = row
        n, me, target = axes[stage]
        return [remote(own.at[stage, pl.ds(0, 1)], red.at[stage, me, pl.ds(0, 1)], target(lax.rem(me + k, n)))
                for k in range(1, n)]

    def reduce_end(stage, copies):
        n, me, _ = axes[stage]
        for copy in copies:
            copy.wait_recv()
        red[stage, me, pl.ds(0, 1)] = own[stage, pl.ds(0, 1)]
        total = red[stage, 0, pl.ds(0, 1)]
        for k in range(1, n):
            total = total + red[stage, k, pl.ds(0, 1)]
        return total

    lane1 = lax.broadcasted_iota(jnp.int32, (1, WID), 1)
    mine = jnp.zeros((1, WID), F32)
    for k, v in enumerate((gamma, delta, eps, *forms)):
        mine = jnp.where(lane1 == k, jnp.sum(rows(v), axis=1, keepdims=True), mine)
    copies = reduce_start(0, mine)
    sides.append(send_sides(1))

    def smooth_y(v):
        hi, lo = split(v)
        return dot(s["Wy"][0], hi) + dot(s["Wy"][1], hi) + dot(s["Wy"][0], lo)

    def smooth_x(v, k):
        hi, lo = split(v)
        return dot(hi, s["Wx"][k, 0]) + dot(hi, s["Wx"][k, 1]) + dot(lo, s["Wx"][k, 0])

    @pl.loop(0, DEP)
    def _(z):
        for i in range(3):
            SE[i, z] = smooth_y(SE[i, z])

    copies = reduce_start(1, reduce_end(0, copies))

    for pair in sides:
        for copy in pair:
            copy.wait_recv()
    for b in range(2):
        @pl.loop(0, 3)
        def _(i, b=b):
            HLr[b, i] = smooth_y(HLr[b, i] * has_left)
            HRr[b, i] = smooth_y(HRr[b, i] * has_right)

    copies = reduce_start(2, reduce_end(1, copies))

    for b in range(2):
        @pl.loop(0, 4)
        def _(j, b=b):
            for i in range(3):
                SE[i, 4 * b + j] = (smooth_x(SE[i, 4 * b + j], 0) + smooth_x(HLr[b, i], 1 + j)
                                    + smooth_x(HRr[b, i], 5 + j))

    total = reduce_end(2, copies)
    g0, d0, ep, ze, t0, t1, t2 = (total[:, k:k + 1] for k in range(7))
    alpha = g0 / d0
    g1 = g0 - 2.0 * alpha * d0 + alpha * alpha * ep
    beta = g1 / g0
    d1 = (1.0 + beta) * (1.0 + beta) * d0 - 2.0 * alpha * (1.0 + beta) * ep + alpha * alpha * ze
    alpha1 = g1 / d1
    a1 = alpha + alpha1 * (1.0 + beta)
    b1 = -(alpha1 * alpha)
    ca = jnp.broadcast_to(a1, (HEI, WID))
    cb = jnp.broadcast_to(b1, (HEI, WID))
    caa, cab, cbb = a1 * a1, 2.0 * (a1 * b1), b1 * b1
    mean = (caa * t0 + cab * t1 + cbb * t2) / float(S * DEP * HEI * WID * GX)
    scale = NORMAL * jnp.broadcast_to(1.0 / (mean + EPSILON), (HEI, WID))
    caa, cab, cbb = (jnp.broadcast_to(v, (HEI, WID)) for v in (caa, cab, cbb))

    G, Gup, Gdn, F = s["G"], s["Gup"], s["Gdn"], s["F"]

    def planes(k):
        z = DEP - 1 - k
        return remote(G.at[k], Gup.at[k], device(0, -3)), remote(G.at[z], Gdn.at[z], device(0, 3))

    def combine(z):
        G[z] = caa * SE[0, z] + cab * SE[1, z] + cbb * SE[2, z]

    far = []
    for k in range(DEP // 2):
        combine(k)
        combine(DEP - 1 - k)
        far.append(planes(k))

    low = G[DEP - 1]
    high = G[0]
    for k in range(1, DEP):
        low = LAMBDA * low + G[DEP - 1 - k]
        high = LAMBDA * high + G[k]
    RU, RD = s["RU"], s["RD"]
    RU[0] = low
    RD[0] = high
    near = [remote(RU.at[0], RU.at[1], device(0, -1)), remote(RD.at[0], RD.at[1], device(0, 1)),
            remote(RU.at[0], RU.at[2], device(0, -2)), remote(RD.at[0], RD.at[2], device(0, 2))]
    far += [planes(k) for k in range(DEP // 2, DEP)]

    acc = None
    for z in range(DEP):
        acc = G[z] if z == 0 else LAMBDA * acc + G[z]
        F[z] = acc
    acc = jnp.zeros((HEI, WID), F32)
    for z in range(DEP - 2, -1, -1):
        acc = LAMBDA * (acc + G[z + 1])
        F[z] = F[z] + acc

    at1, at2, at3 = flag(slab + 1 < S), flag(slab + 2 < S), flag(slab + 3 < S)
    bt1, bt2, bt3 = flag(slab >= 1), flag(slab >= 2), flag(slab >= 3)

    @pl.loop(0, DEP)
    def _(z):
        for c in range(3):
            s["U"][c, 0, z] = ca * s0[c, z + 1] + cb * w0[c, z]

    stores = [pltpu.make_async_copy(s["U"], out_u, s["local"].at[4])]
    stores[0].start()

    for copy in near:
        copy.wait_recv()
    near_u = at1 * RU[1] + (LAMBDA**DEP * at2) * RU[2]
    near_d = bt1 * RD[1] + (LAMBDA**DEP * bt2) * RD[2]
    for z in range(DEP):
        F[z] = F[z] + LAMBDA ** (DEP - z) * near_u + LAMBDA ** (z + 1) * near_d

    up_scale, dn_scale = at3 * LAMBDA**RAD, bt3 * LAMBDA**RAD
    RR = s["RR"]

    def finish_plane(z, value):
        b = bone[0, z].astype(F32)
        new = dens[0, z] + REMODEL * b * (value * scale - 1.0)
        s["D"][0, z] = jnp.clip(new, FLOOR, CEILING)
        copy = pltpu.make_async_copy(s["D"].at[0, z], out_d.at[0, z], s["local"].at[5 + z])
        copy.start()
        stores.append(copy)

    for k in range(DEP):
        z = DEP - 1 - k
        far[k][0].wait_recv()
        far[k][1].wait_recv()
        up = up_scale * Gup[k]
        down = dn_scale * Gdn[z]
        if k:
            up = up + (1.0 / LAMBDA) * RR[0]
            down = down + (1.0 / LAMBDA) * RR[1]
        RR[0] = up
        RR[1] = down
        if k < DEP // 2:
            F[k] = F[k] + up
            F[z] = F[z] + down
        else:
            finish_plane(k, F[k] + up)
            finish_plane(z, F[z] + down)

    for copy in stores:
        copy.wait()
    for copy in sends:
        copy.wait_send()


def on_device(sizes, density, bone, fixed, load):
    GX, GY, GZ = sizes
    copies = 4 + 2 + 4 + 3 + 4 + (GX + 2 * GY + GZ // 2 - 3) + 4 + 16
    V = pltpu.VMEM
    plane, tall, thin = (HEI, WID), (HEI + 8, WID), (48, WID)
    scratch = {
        "send": pltpu.SemaphoreType.DMA((copies,)),
        "recv": pltpu.SemaphoreType.DMA((copies,)),
        "local": pltpu.SemaphoreType.DMA((13,)),
        "U": V(load.shape, F32), "D": V(density.shape, F32),
        "dens": V(density.shape, F32), "bone": V(bone.shape, jnp.int32), "fixed": V(fixed.shape, jnp.int32),
        "load": V(load.shape, F32),
        "E": V((9, *plane), F32), "R": V((3, DEP, *plane), F32), "R8": V((3, *plane), F32),
        "T": V((10, *plane), F32), "Q": V((DEP, *plane), F32),
        "s0": V((3, 10, *plane), F32), "w0": V((3, 9, *plane), F32),
        "SDs": V((6, 10, *tall), F32), "SDw": V((6, 10, *tall), F32),
        "A": V((6, 9, *plane), F32), "B": V((6, 10, *tall), F32),
        "XSD": V((6, *tall), F32), "XA": V((3, *plane), F32), "XB": V((3, *tall), F32),
        "EX": V(plane, F32), "XE": V(plane, F32), "X0": V(plane, F32), "XH": V(plane, F32), "XL1": V(plane, F32),
        "XEs": V((8, WID), F32), "XEr": V((8, WID), F32), "XDr": V((8, WID), F32),
        "XLs1": V(thin, F32), "XRs1": V(thin, F32), "XLr1": V(thin, F32), "XRr1": V(thin, F32),
        "XLs2": V(thin, F32), "XRs2": V(thin, F32), "XLr2": V(thin, F32), "XRr2": V(thin, F32),
        "XWs": V((64, WID), F32), "XWr": V((72, WID), F32), "XCr": V((8, WID), F32),
        "SE": V((3, DEP, *plane), F32), "own": V((3, 8, WID), F32), "red": V((3, max(GX, 2 * GY, GZ // 2), 8, WID), F32),
        "Wy": V((2, HEI, HEI), BF16), "Wx": V((9, 2, WID, WID), BF16), "W2": V(plane, F32), "WZ": V((DEP, WID), F32), "GD": V((DEP, *plane), F32),
        "G": V((DEP, *plane), F32), "Gup": V((DEP, *plane), F32), "Gdn": V((DEP, *plane), F32),
        "HLs": V((2, 3, *plane), F32), "HRs": V((2, 3, *plane), F32),
        "HLr": V((2, 3, *plane), F32), "HRr": V((2, 3, *plane), F32),
        "RU": V((3, *plane), F32), "RD": V((3, *plane), F32), "F": V((DEP, *plane), F32), "RR": V((2, *plane), F32),
    }
    names = list(scratch)

    def kernel(*refs):
        body(sizes, *refs[:6], dict(zip(names, refs[6:])))

    outer = pl.BlockSpec(memory_space=pltpu.HBM)
    results = pl.pallas_call(
        kernel,
        out_shape=(jax.ShapeDtypeStruct(density.shape, F32), jax.ShapeDtypeStruct(load.shape, F32)),
        in_specs=[outer] * 4,
        out_specs=(outer, outer),
        scratch_shapes=[scratch[n] for n in names],
        compiler_params=pltpu.CompilerParams(
            collective_id=0, has_side_effects=True, vmem_limit_bytes=56 * 1024 * 1024),
    )(density, bone, fixed, load)

    def hand_over(d, u, out_d, out_u, mid_d, mid_u, into, out):
        parts = []
        for k in range(PIECES):
            rows_z = pl.ds(k * (DEP // PIECES), DEP // PIECES)
            parts.append((d.at[0, rows_z], mid_d.at[0, rows_z], out_d.at[0, rows_z]))
            parts += [(u.at[c, 0, rows_z], mid_u.at[c, 0, rows_z], out_u.at[c, 0, rows_z]) for c in range(3)]
        reads = [pltpu.make_async_copy(a, b, into.at[n]) for n, (a, b, _) in enumerate(parts)]
        writes = [pltpu.make_async_copy(b, c, out.at[n]) for n, (_, b, c) in enumerate(parts)]
        for read in reads:
            read.start()
        for read, write in zip(reads, writes):
            read.wait()
            write.start()
        for write in writes:
            write.wait()

    return pl.pallas_call(
        hand_over,
        out_shape=tuple(jax.ShapeDtypeStruct(v.shape, F32) for v in results),
        in_specs=[outer] * 2,
        out_specs=(outer, outer),
        scratch_shapes=[V(density.shape, F32), V(load.shape, F32), pltpu.SemaphoreType.DMA((4 * PIECES,)),
                        pltpu.SemaphoreType.DMA((4 * PIECES,))],
        compiler_params=pltpu.CompilerParams(vmem_limit_bytes=56 * 1024 * 1024),
    )(*results)


def solution(mesh):
    sizes = tuple(mesh.shape[name] for name in ("gx", "gy", "gz"))
    placed = (P("gz", "gy", None, "gx"),) * 3 + (P(None, "gz", "gy", None, "gx"),)
    return jax.shard_map(
        functools.partial(on_device, sizes),
        mesh=mesh,
        in_specs=placed,
        out_specs=(P("gz", "gy", None, "gx"), P(None, "gz", "gy", None, "gx")),
        check_vma=False,
    )
```

```python
import functools
import math

import jax
import jax.numpy as jnp
import numpy as np
from jax import lax
from jax.experimental import pallas as pl
from jax.experimental.pallas import tpu as pltpu
from jax.sharding import PartitionSpec as P

MESH = pl.DeviceIdType.MESH
RAD = 24
MARROW = 0.1
REMODEL = 0.25
FLOOR = 0.2
CEILING = 1.0
EPSILON = 1e-06
DEP = 8
HEI = 96
WID = 128
PIECES = 1
F32 = jnp.float32
BF16 = jnp.bfloat16


def element_stiffness():
    poisson = 0.3
    lame = poisson / ((1.0 + poisson) * (1.0 - 2.0 * poisson))
    shear = 0.5 / (1.0 + poisson)
    elastic = np.zeros((6, 6))
    elastic[:3, :3] = lame
    for index in range(3):
        elastic[index, index] += 2.0 * shear
        elastic[index + 3, index + 3] = shear
    points = [0.5 - 0.5 / math.sqrt(3.0), 0.5 + 0.5 / math.sqrt(3.0)]
    matrix = np.zeros((24, 24))
    for point_z in points:
        for point_y in points:
            for point_x in points:
                strain = np.zeros((6, 24))
                for corner_z in range(2):
                    for corner_y in range(2):
                        for corner_x in range(2):
                            node = 4 * corner_z + 2 * corner_y + corner_x
                            shape_x = point_x if corner_x else 1.0 - point_x
                            shape_y = point_y if corner_y else 1.0 - point_y
                            shape_z = point_z if corner_z else 1.0 - point_z
                            slope_x = 1.0 if corner_x else -1.0
                            slope_y = 1.0 if corner_y else -1.0
                            slope_z = 1.0 if corner_z else -1.0
                            along_x = slope_x * shape_y * shape_z
                            along_y = shape_x * slope_y * shape_z
                            along_z = shape_x * shape_y * slope_z
                            strain[0, node] = along_x
                            strain[1, 8 + node] = along_y
                            strain[2, 16 + node] = along_z
                            strain[3, node] = along_y
                            strain[3, 8 + node] = along_x
                            strain[4, 8 + node] = along_z
                            strain[4, 16 + node] = along_y
                            strain[5, node] = along_z
                            strain[5, 16 + node] = along_x
                matrix = matrix + strain.T @ elastic @ strain / 8.0
    return matrix


KE = element_stiffness()
HAAR1 = np.array([[1.0, 1.0], [-1.0, 1.0]])
HAAR = np.kron(np.eye(3), np.kron(HAAR1, np.kron(HAAR1, HAAR1)))
KH = HAAR @ KE @ HAAR.T / 64.0
DIAG = float(KE[0, 0])
GROUPS = ((1, 10, 20), (2, 9), (4, 17), (12, 18), (3, 22), (5, 14), (11, 21), (6, 13, 19), (7,), (15,), (23,))
LAMBDA = math.exp(-1.0 / 12.0)
NORMAL = 1.0 / (1.0 + 2.0 * sum(LAMBDA**d for d in range(1, RAD + 1)))


def stress(m):
    out = [None] * 24
    for group in GROUPS:
        first = group[0]
        diag = float(KH[first, first])
        if len(group) == 1:
            out[first] = diag * m[first]
            continue
        off = float(KH[first, group[1]])
        total = m[first]
        for k in group[1:]:
            total = total + m[k]
        common = off * total
        for k in group:
            out[k] = common if abs(diag - off) < 1e-12 else common + (diag - off) * m[k]
    return out


def bilinear(m, f):
    total = None
    for k in range(24):
        if f[k] is not None:
            total = m[k] * f[k] if total is None else total + m[k] * f[k]
    return total


def zmodes(lo, hi):
    m = [None] * 24
    for c in range(3):
        for p in range(4):
            m[c * 8 + p] = hi[c * 4 + p] + lo[c * 4 + p]
            m[c * 8 + 4 + p] = hi[c * 4 + p] - lo[c * 4 + p]
    return m


def minus(a, b):
    return -b if a is None else a - b


def plus(a, b):
    return b if a is None else a + b


def split(value):
    hi = value.astype(BF16)
    return hi, (value - hi.astype(F32)).astype(BF16)


def dot(a, b):
    return jnp.dot(a, b, preferred_element_type=F32)


def tap(distance):
    return jnp.where(distance <= RAD, NORMAL * jnp.exp(distance.astype(F32) * (-1.0 / 12.0)), 0.0)


def power(exponent):
    return jnp.exp(exponent.astype(F32) * (-1.0 / 12.0))


def kept(index, size):
    ends = power(jnp.minimum(index, RAD) + 1) + power(jnp.minimum(size - 1 - index, RAD) + 1)
    return NORMAL * (1.0 + (2.0 * LAMBDA - ends) * (1.0 / (1.0 - LAMBDA)))


def fold(value):
    return jnp.sum(value.reshape(HEI // 8, 8, WID), axis=0)


def rows(value):
    return jnp.sum(value, axis=0, keepdims=True)


def body(sizes, dens_h, bone_h, fixed_h, load_h, out_d, out_u, s):
    GX, GY, GZ = sizes
    S = GY * GZ
    gx, gy, gz = lax.axis_index("gx"), lax.axis_index("gy"), lax.axis_index("gz")
    slab = gz * GY + gy
    lane = lax.broadcasted_iota(jnp.int32, (HEI, WID), 1)
    rowi = lax.broadcasted_iota(jnp.int32, (HEI, WID), 0)

    def device(dx=0, ds=0):
        t = lax.rem(slab + ds + S, S)
        return (lax.rem(gx + dx + GX, GX), lax.rem(t, GY), lax.div(t, GY))

    def flag(cond):
        return jnp.where(cond, 1.0, 0.0).astype(F32)

    has_left, has_right = flag(gx > 0), flag(gx < GX - 1)
    has_down, has_up = flag(slab > 0), flag(slab < S - 1)

    count = [0]
    sends = []

    def remote(src, dst, target):
        k = count[0]
        count[0] += 1
        copy = pltpu.make_async_remote_copy(
            src_ref=src, dst_ref=dst, send_sem=s["send"].at[k], recv_sem=s["recv"].at[k],
            device_id=target, device_id_type=MESH)
        copy.start()
        sends.append(copy)
        return copy

    dens, bone, fixed, load = s["dens"], s["bone"], s["fixed"], s["load"]
    loads = []
    for k, (src, dst) in enumerate(((dens_h, dens), (bone_h, bone), (fixed_h, fixed), (load_h, load))):
        copy = pltpu.make_async_copy(src, dst, s["local"].at[k])
        copy.start()
        loads.append(copy)

    barrier = pltpu.get_barrier_semaphore()
    peers = [device(-1), device(1), device(0, 1), device(0, -1), device(1, 1), device(-1, -1),
             device(0, 3), device(0, -3), device(0, 2), device(0, -2)]
    NY = GZ // 2
    lo, iy = lax.div(gz, NY), lax.rem(gz, NY)
    axes = ((GX, gx, lambda p: (p, gy, gz)),
            (2 * GY, 2 * gy + lo, lambda p: (gx, lax.div(p, 2), lax.rem(p, 2) * NY + iy)),
            (NY, iy, lambda p: (gx, gy, lo * NY + p)))
    for number, me, target in axes:
        for k in range(1, number):
            if me is not gx or 1 < k < GX - 1:
                peers.append(target(lax.rem(me + k, number)))
    for peer in peers:
        pl.semaphore_signal(barrier, inc=1, device_id=peer, device_id_type=MESH)

    zero8 = jnp.zeros((8, WID), F32)

    @pl.loop(0, 10)
    def _(zz):
        for k in range(6):
            s["SDs"][k, zz, pl.ds(HEI, 8)] = zero8
            s["SDw"][k, zz, pl.ds(HEI, 8)] = zero8
            s["B"][k, zz, pl.ds(0, 8)] = zero8

    for k in range(6):
        s["XSD"][k, pl.ds(HEI, 8)] = zero8
    for k in range(3):
        s["XB"][k, pl.ds(0, 8)] = zero8

    far_y = jnp.abs(lax.broadcasted_iota(jnp.int32, (HEI, HEI), 0) - lax.broadcasted_iota(jnp.int32, (HEI, HEI), 1))
    s["Wy"][0], s["Wy"][1] = split(tap(far_y))
    row = lax.broadcasted_iota(jnp.int32, (WID, WID), 0)
    col = lax.broadcasted_iota(jnp.int32, (WID, WID), 1)
    s["Wx"][0, 0], s["Wx"][0, 1] = split(tap(jnp.abs(row - col)))
    for j in range(4):
        inside = (row >= 32 * j) & (row < 32 * j + 32)
        right = jnp.where(inside, tap(jnp.abs(WID + row - 32 * j - col)), 0.0)
        left = jnp.where(inside, tap(jnp.abs(col + 32 - row + 32 * j)), 0.0)
        s["Wx"][1 + j, 0], s["Wx"][1 + j, 1] = split(left)
        s["Wx"][5 + j, 0], s["Wx"][5 + j, 1] = split(right)
    s["W2"][...] = kept(gx * WID + lane, GX * WID) * kept(rowi, HEI)

    s["WZ"][...] = kept(slab * DEP + lax.broadcasted_iota(jnp.int32, (DEP, WID), 0), S * DEP)

    E, R = s["E"], s["R"]
    loads[0].wait()
    loads[1].wait()

    @pl.loop(0, DEP)
    def _(z):
        b = bone[0, z].astype(F32)
        d = dens[0, z]
        E[z + 1] = b * d * d + (1.0 - b) * MARROW

    def pack(get, slots, src):
        acc = jnp.zeros((HEI, WID), F32)
        for index, k in slots:
            acc = jnp.where(lane == k, pltpu.roll(get(index), (k - src) % WID, 1), acc)
        return acc

    def turned(acc):
        full = jnp.concatenate([acc, jnp.zeros((WID - HEI, WID), F32)], axis=0)
        return jnp.transpose(full)

    def unturned(ref, number):
        got = ref[...]
        full = jnp.concatenate([got, jnp.zeros((WID - number, WID), F32)], axis=0)
        return jnp.transpose(full)[:HEI]

    s["XEs"][...] = turned(pack(lambda z: E[z + 1], [(z, z) for z in range(DEP)], WID - 1))[:8]
    loads[2].wait()
    loads[3].wait()

    @pl.loop(0, DEP)
    def _(z):
        f = 1.0 - fixed[0, z].astype(F32)
        for c in range(3):
            R[c, z] = f * load[c, 0, z]
        s["GD"][z] = 0.5 * E[z + 1] / dens[0, z]

    pl.semaphore_wait(barrier, len(peers))
    c_xe = remote(s["XEs"], s["XEr"], device(1))
    c_e = remote(E.at[DEP], E.at[0], device(0, 1))
    c_r = remote(R.at[:, 0], s["R8"], device(0, -1))
    c_xd = remote(s["XEs"], s["XDr"], device(1, 1))

    T = s["T"]
    s0, Q = s["s0"], s["Q"]

    def inplane(e, edge):
        ex = e + jnp.where(lane == 0, edge, pltpu.roll(e, 1, 1))
        return ex + jnp.where(rowi == 0, 0.0, pltpu.roll(ex, 1, 0))

    def flat(z):
        T[z + 1] = inplane(E[z + 1], pltpu.roll(s["XE"][...], lax.rem(WID - z, WID), 1))

    def start(z):
        inv = 1.0 / (DIAG * (T[z] + T[z + 1]))
        Q[z] = (1.0 - fixed[0, z].astype(F32)) * inv
        for c in range(3):
            s0[c, z + 1] = R[c, z] * inv

    c_xe.wait_recv()
    s["XE"][...] = unturned(s["XEr"], 8) * has_left
    flat(DEP - 1)
    flat(DEP - 2)
    start(DEP - 1)
    c_s = remote(s0.at[:, DEP], s0.at[:, 0], device(0, 1))
    flat(0)
    c_t = remote(T.at[1], T.at[DEP + 1], device(0, -1))
    pl.loop(1, DEP - 2)(flat)
    pl.loop(1, DEP - 1)(start)

    def columns(planes, name):
        slots = [((c, zz), 16 * c + zz) for c in range(3) for zz in planes]
        first = pack(lambda i: s0[i[0], i[1]], slots, 0)
        last = pack(lambda i: s0[i[0], i[1]], slots, WID - 1)
        s["XLs" + name][...] = turned(first)[:48]
        s["XRs" + name][...] = turned(last)[:48]
        return first, (remote(s["XLs" + name], s["XRr" + name], device(-1)),
                       remote(s["XRs" + name], s["XLr" + name], device(1)))

    first, pair = columns(range(2, 9), "1")
    s["X0"][...] = first

    def edges(got):
        for c in range(3):
            s["XSD"][2 * c, pl.ds(0, HEI)] = pltpu.roll(s["X0"][...] + got, (WID - 16 * c) % WID, 1)
            s["XSD"][2 * c + 1, pl.ds(0, HEI)] = pltpu.roll(s["X0"][...] - got, (WID - 16 * c) % WID, 1)

    def arrive(pair, name):
        for copy in pair:
            copy.wait_recv()
        s["XH"][...] = unturned(s["XRr" + name], 48) * has_right
        return unturned(s["XLr" + name], 48)

    def xstage(field, SD, shift, zz):
        for c in range(3):
            v = field[c, zz]
            h = pltpu.roll(s["XH"][...], shift(c, zz), 1)
            v1 = jnp.where(lane == WID - 1, h, pltpu.roll(v, WID - 1, 1))
            SD[2 * c, zz, pl.ds(0, HEI)] = v1 + v
            SD[2 * c + 1, zz, pl.ds(0, HEI)] = v1 - v

    def place_s(c, zz):
        return WID - 1 - 16 * c - zz

    def place_w(c, z):
        return WID - 1 - 8 * z - c

    def planar(SD, zz, y0):
        out = []
        for c in range(3):
            a0, a1 = SD[2 * c, zz, pl.ds(y0, 8)], SD[2 * c, zz, pl.ds(y0 + 1, 8)]
            b0, b1 = SD[2 * c + 1, zz, pl.ds(y0, 8)], SD[2 * c + 1, zz, pl.ds(y0 + 1, 8)]
            out += [a1 + a0, b1 + b0, a1 - a0, b1 - b0]
        return out

    A, B = s["A"], s["B"]

    def element(lo, hi, zz, y0):
        f = stress(zmodes(lo, hi))
        e = E[zz, pl.ds(y0, 8)]
        f = [None if v is None else v * e for v in f]
        up = [plus(f[c * 8 + p], f[c * 8 + 4 + p]) for c in range(3) for p in range(4)]
        down = [minus(f[c * 8 + p], f[c * 8 + 4 + p]) for c in range(3) for p in range(4)]
        return down, up

    def put(g, zz, y0, more=False):
        for c in range(3):
            for ix in range(2):
                a = g[4 * c + ix] - g[4 * c + 2 + ix]
                b = g[4 * c + ix] + g[4 * c + 2 + ix]
                if more:
                    a = a + A[2 * c + ix, zz, pl.ds(y0, 8)]
                    b = b + B[2 * c + ix, zz, pl.ds(y0 + 8, 8)]
                A[2 * c + ix, zz, pl.ds(y0, 8)] = a
                B[2 * c + ix, zz, pl.ds(y0 + 8, 8)] = b

    def both(g, h):
        return [u + v for u, v in zip(g, h)]

    def edge_elements(y0):
        lo = []
        for c in range(3):
            a0, a1 = s["XSD"][2 * c, pl.ds(y0, 8)], s["XSD"][2 * c, pl.ds(y0 + 1, 8)]
            b0, b1 = s["XSD"][2 * c + 1, pl.ds(y0, 8)], s["XSD"][2 * c + 1, pl.ds(y0 + 1, 8)]
            lo += [a1 + a0, b1 + b0, a1 - a0, b1 - b0]
        hi = [pltpu.roll(v, WID - 1, 1) for v in lo]
        f = stress(zmodes(lo, hi))
        e = s["EX"][pl.ds(y0, 8)]
        f = [None if v is None else v * e for v in f]
        for c in range(3):
            g = []
            for p in range(4):
                up = plus(f[c * 8 + p], f[c * 8 + 4 + p])
                down = minus(f[c * 8 + p], f[c * 8 + 4 + p])
                g.append(down + pltpu.roll(up, 1, 1))
            s["XA"][c, pl.ds(y0, 8)] = (g[0] - g[2]) + (g[1] - g[3])
            s["XB"][c, pl.ds(y0 + 8, 8)] = (g[0] + g[2]) + (g[1] + g[3])

    def chunks(step):
        @pl.loop(0, HEI // 8)
        def _(i):
            step(pl.multiple_of(i * 8, 8))

    w0 = s["w0"]

    def image(z, sums):
        gamma, delta, eps = sums
        q = Q[z]
        for c in range(3):
            gs = A[2 * c, z + 1] + B[2 * c, z + 1, pl.ds(7, HEI)]
            gd = A[2 * c + 1, z + 1] + B[2 * c + 1, z + 1, pl.ds(7, HEI)]
            edge = pltpu.roll(s["XA"][c] + s["XB"][c, pl.ds(7, HEI)], WID - 1 - z, 1)
            im = (gs - gd) + jnp.where(lane == 0, edge, pltpu.roll(gs + gd, 1, 1))
            w = im * q
            w0[c, z] = w
            v = s0[c, z + 1]
            gamma = gamma + fold(R[c, z] * v)
            delta = delta + fold(v * im)
            eps = eps + fold(w * im)
        return gamma, delta, eps

    s["EX"][...] = pltpu.roll(s["XE"][...], 1, 1)
    s["XL1"][...] = arrive(pair, "1")
    edges(s["XL1"][...])
    pl.loop(2, 9)(lambda zz: xstage(s0, s["SDs"], place_s, zz))

    def early(y0):
        def plane(zz, carry):
            lo, above = carry
            hi = planar(s["SDs"], zz + 1, y0)
            down, up = element(lo, hi, zz, y0)
            put(both(above, down), zz, y0)
            return tuple(hi), tuple(up)

        top = lax.fori_loop(2, DEP, plane, (tuple(planar(s["SDs"], 2, y0)), (zero8,) * 12))[1]
        put(top, DEP, y0)
        edge_elements(y0)

    chunks(early)
    sums = lax.fori_loop(2, DEP - 1, image, (zero8, zero8, zero8))

    c_xd.wait_recv()
    c_e.wait_recv()
    E[0] = E[0] * has_down
    corner = pltpu.roll(unturned(s["XDr"], 8) * (has_left * has_down), WID - 7, 1)
    T[0] = inplane(E[0], corner)
    start(0)
    s["EX"][...] = jnp.where(lane == 0, corner, s["EX"][...])
    c_r.wait_recv()
    c_t.wait_recv()
    inv8 = has_up / (DIAG * (T[DEP] + has_up * T[DEP + 1]))
    for c in range(3):
        s0[c, DEP + 1] = s["R8"][c] * inv8
    c_s.wait_recv()

    SDs, SDw, SE = s["SDs"], s["SDw"], s["SE"]

    def self_energy(low, high):
        def step(y0):
            def plane(z, lo):
                hi = planar(SDs, z + 2, y0)
                m = zmodes(lo, hi)
                SE[0, z, pl.ds(y0, 8)] = bilinear(m, stress(m))
                return tuple(hi)
            lax.fori_loop(low, high, plane, tuple(planar(SDs, low + 1, y0)))
        return step

    first, pair = columns((0, 1, 9), "2")
    chunks(self_energy(1, DEP - 1))
    s["X0"][...] = s["X0"][...] + first
    edges(s["XL1"][...] + arrive(pair, "2"))
    for zz in (0, 1):
        xstage(s0, s["SDs"], place_s, zz)

    def late(y0):
        SD = s["SDs"]
        n0, n1, n2 = planar(SD, 0, y0), planar(SD, 1, y0), planar(SD, 2, y0)
        up = element(n0, n1, 0, y0)[1]
        down, above = element(n1, n2, 1, y0)
        put(both(up, down), 1, y0)
        put(above, 2, y0, more=True)
        edge_elements(y0)

    chunks(late)
    sums = image(0, sums)
    c_w = remote(w0.at[:, 0], w0.at[:, DEP], device(0, -1))
    xstage(s0, s["SDs"], place_s, DEP + 1)

    def last_element(y0):
        SD = s["SDs"]
        put(element(planar(SD, DEP, y0), planar(SD, DEP + 1, y0), DEP, y0)[0], DEP, y0, more=True)

    chunks(last_element)
    sums = image(1, sums)
    gamma, delta, eps = image(DEP - 1, sums)

    slots = [((c, z), 8 * z + c) for z in range(DEP) for c in range(3)]
    s["XWs"][...] = turned(pack(lambda i: w0[i[0], i[1]], slots, 0))[:64]
    c_xw = remote(s["XWs"], s["XWr"].at[pl.ds(0, 64)], device(-1))
    c_xc = remote(s["XWs"].at[pl.ds(0, 8)], s["XCr"], device(-1, -1))

    def energies(low, high):
        def step(y0):
            def plane(z, carry):
                los, lows = carry
                his, hiw = planar(SDs, z + 2, y0), planar(SDw, z + 1, y0)
                m = zmodes(lows, hiw)
                f = stress(m)
                SE[2, z, pl.ds(y0, 8)] = bilinear(m, f)
                SE[1, z, pl.ds(y0, 8)] = bilinear(zmodes(los, his), f)
                return tuple(his), tuple(hiw)
            lax.fori_loop(low, high, plane, (tuple(planar(SDs, low + 1, y0)), tuple(planar(SDw, low, y0))))
        return step

    def per_density(z, sums):
        zeta, m0, m1, m2 = sums
        g = s["GD"][z]
        zeta = zeta + fold(SE[2, z] * E[z + 1])
        share = s["WZ"][pl.ds(z, 1)]
        out = []
        for i, m in enumerate((m0, m1, m2)):
            v = SE[i, z] * g
            SE[i, z] = v
            out.append(m + share * fold(v * s["W2"][...]))
        return (zeta, *out)

    HLs, HRs, HLr, HRr = s["HLs"], s["HRs"], s["HLr"], s["HRr"]

    def send_sides(b):
        @pl.loop(0, 3)
        def _(i):
            acc_l = acc_r = None
            for j in range(4):
                v = SE[i, 4 * b + j]
                mine = (lane >= 32 * j) & (lane < 32 * j + 32)
                to_l = pltpu.roll(v, 32 * j, 1) if j else v
                to_r = pltpu.roll(v, (32 * j - 96) % WID, 1) if (32 * j - 96) % WID else v
                acc_l = to_l if acc_l is None else jnp.where(mine, to_l, acc_l)
                acc_r = to_r if acc_r is None else jnp.where(mine, to_r, acc_r)
            HLs[b, i] = acc_l
            HRs[b, i] = acc_r
        return remote(HLs.at[b], HRr.at[b], device(-1)), remote(HRs.at[b], HLr.at[b], device(1))

    @pl.loop(0, HEI // 8)
    def _(i):
        y0 = pl.multiple_of(i * 8, 8)
        self_energy(0, 1)(y0)
        self_energy(DEP - 1, DEP)(y0)

    c_xw.wait_recv()
    s["XH"][...] = unturned(s["XWr"], 72) * has_right
    pl.loop(0, DEP)(lambda z: xstage(w0, SDw, place_w, z))
    chunks(energies(0, DEP - 1))
    forms = lax.fori_loop(0, DEP - 1, per_density, (zero8,) * 4)
    sides = [send_sides(0)]

    c_xc.wait_recv()
    c_w.wait_recv()
    s["XWr"][pl.ds(64, 8)] = s["XCr"][...] * has_up
    s["XH"][...] = unturned(s["XWr"], 72) * has_right
    for c in range(3):
        w0[c, DEP] = w0[c, DEP] * has_up
    xstage(w0, SDw, place_w, DEP)
    chunks(energies(DEP - 1, DEP))
    forms = per_density(DEP - 1, forms)

    own, red = s["own"], s["red"]

    def reduce_start(stage, row):
        own[stage, pl.ds(0, 1)] = row
        n, me, target = axes[stage]
        return [remote(own.at[stage, pl.ds(0, 1)], red.at[stage, me, pl.ds(0, 1)], target(lax.rem(me + k, n)))
                for k in range(1, n)]

    def reduce_end(stage, copies):
        n, me, _ = axes[stage]
        for copy in copies:
            copy.wait_recv()
        red[stage, me, pl.ds(0, 1)] = own[stage, pl.ds(0, 1)]
        total = red[stage, 0, pl.ds(0, 1)]
        for k in range(1, n):
            total = total + red[stage, k, pl.ds(0, 1)]
        return total

    lane1 = lax.broadcasted_iota(jnp.int32, (1, WID), 1)
    mine = jnp.zeros((1, WID), F32)
    for k, v in enumerate((gamma, delta, eps, *forms)):
        mine = jnp.where(lane1 == k, jnp.sum(rows(v), axis=1, keepdims=True), mine)
    copies = reduce_start(0, mine)
    sides.append(send_sides(1))

    def smooth_y(v):
        hi, lo = split(v)
        return dot(s["Wy"][0], hi) + dot(s["Wy"][1], hi) + dot(s["Wy"][0], lo)

    def smooth_x(v, k):
        hi, lo = split(v)
        return dot(hi, s["Wx"][k, 0]) + dot(hi, s["Wx"][k, 1]) + dot(lo, s["Wx"][k, 0])

    @pl.loop(0, DEP)
    def _(z):
        for i in range(3):
            SE[i, z] = smooth_y(SE[i, z])

    copies = reduce_start(1, reduce_end(0, copies))

    for pair in sides:
        for copy in pair:
            copy.wait_recv()
    for b in range(2):
        @pl.loop(0, 3)
        def _(i, b=b):
            HLr[b, i] = smooth_y(HLr[b, i] * has_left)
            HRr[b, i] = smooth_y(HRr[b, i] * has_right)

    copies = reduce_start(2, reduce_end(1, copies))

    for b in range(2):
        @pl.loop(0, 4)
        def _(j, b=b):
            for i in range(3):
                SE[i, 4 * b + j] = (smooth_x(SE[i, 4 * b + j], 0) + smooth_x(HLr[b, i], 1 + j)
                                    + smooth_x(HRr[b, i], 5 + j))

    total = reduce_end(2, copies)
    g0, d0, ep, ze, t0, t1, t2 = (total[:, k:k + 1] for k in range(7))
    alpha = g0 / d0
    g1 = g0 - 2.0 * alpha * d0 + alpha * alpha * ep
    beta = g1 / g0
    d1 = (1.0 + beta) * (1.0 + beta) * d0 - 2.0 * alpha * (1.0 + beta) * ep + alpha * alpha * ze
    alpha1 = g1 / d1
    a1 = alpha + alpha1 * (1.0 + beta)
    b1 = -(alpha1 * alpha)
    ca = jnp.broadcast_to(a1, (HEI, WID))
    cb = jnp.broadcast_to(b1, (HEI, WID))
    caa, cab, cbb = a1 * a1, 2.0 * (a1 * b1), b1 * b1
    mean = (caa * t0 + cab * t1 + cbb * t2) / float(S * DEP * HEI * WID * GX)
    scale = NORMAL * jnp.broadcast_to(1.0 / (mean + EPSILON), (HEI, WID))
    caa, cab, cbb = (jnp.broadcast_to(v, (HEI, WID)) for v in (caa, cab, cbb))

    G, Gup, Gdn, F = s["G"], s["Gup"], s["Gdn"], s["F"]

    def planes(k):
        z = DEP - 1 - k
        return remote(G.at[k], Gup.at[k], device(0, -3)), remote(G.at[z], Gdn.at[z], device(0, 3))

    def combine(z):
        G[z] = caa * SE[0, z] + cab * SE[1, z] + cbb * SE[2, z]

    far = []
    for k in range(DEP // 2):
        combine(k)
        combine(DEP - 1 - k)
        far.append(planes(k))

    low = G[DEP - 1]
    high = G[0]
    for k in range(1, DEP):
        low = LAMBDA * low + G[DEP - 1 - k]
        high = LAMBDA * high + G[k]
    RU, RD = s["RU"], s["RD"]
    RU[0] = low
    RD[0] = high
    near = [remote(RU.at[0], RU.at[1], device(0, -1)), remote(RD.at[0], RD.at[1], device(0, 1)),
            remote(RU.at[0], RU.at[2], device(0, -2)), remote(RD.at[0], RD.at[2], device(0, 2))]
    far += [planes(k) for k in range(DEP // 2, DEP)]

    acc = None
    for z in range(DEP):
        acc = G[z] if z == 0 else LAMBDA * acc + G[z]
        F[z] = acc
    acc = jnp.zeros((HEI, WID), F32)
    for z in range(DEP - 2, -1, -1):
        acc = LAMBDA * (acc + G[z + 1])
        F[z] = F[z] + acc

    at1, at2, at3 = flag(slab + 1 < S), flag(slab + 2 < S), flag(slab + 3 < S)
    bt1, bt2, bt3 = flag(slab >= 1), flag(slab >= 2), flag(slab >= 3)

    @pl.loop(0, DEP)
    def _(z):
        for c in range(3):
            s["U"][c, 0, z] = ca * s0[c, z + 1] + cb * w0[c, z]

    stores = [pltpu.make_async_copy(s["U"], out_u, s["local"].at[4])]
    stores[0].start()

    for copy in near:
        copy.wait_recv()
    near_u = at1 * RU[1] + (LAMBDA**DEP * at2) * RU[2]
    near_d = bt1 * RD[1] + (LAMBDA**DEP * bt2) * RD[2]
    for z in range(DEP):
        F[z] = F[z] + LAMBDA ** (DEP - z) * near_u + LAMBDA ** (z + 1) * near_d

    up_scale, dn_scale = at3 * LAMBDA**RAD, bt3 * LAMBDA**RAD
    RR = s["RR"]

    def finish_plane(z, value):
        b = bone[0, z].astype(F32)
        new = dens[0, z] + REMODEL * b * (value * scale - 1.0)
        s["D"][0, z] = jnp.clip(new, FLOOR, CEILING)
        copy = pltpu.make_async_copy(s["D"].at[0, z], out_d.at[0, z], s["local"].at[5 + z])
        copy.start()
        stores.append(copy)

    for k in range(DEP):
        z = DEP - 1 - k
        far[k][0].wait_recv()
        far[k][1].wait_recv()
        up = up_scale * Gup[k]
        down = dn_scale * Gdn[z]
        if k:
            up = up + (1.0 / LAMBDA) * RR[0]
            down = down + (1.0 / LAMBDA) * RR[1]
        RR[0] = up
        RR[1] = down
        if k < DEP // 2:
            F[k] = F[k] + up
            F[z] = F[z] + down
        else:
            finish_plane(k, F[k] + up)
            finish_plane(z, F[z] + down)

    for copy in stores:
        copy.wait()
    for copy in sends:
        copy.wait_send()


def on_device(sizes, density, bone, fixed, load):
    GX, GY, GZ = sizes
    copies = 4 + 2 + 4 + 3 + 4 + (GX + 2 * GY + GZ // 2 - 3) + 4 + 16
    V = pltpu.VMEM
    plane, tall, thin = (HEI, WID), (HEI + 8, WID), (48, WID)
    scratch = {
        "send": pltpu.SemaphoreType.DMA((copies,)),
        "recv": pltpu.SemaphoreType.DMA((copies,)),
        "local": pltpu.SemaphoreType.DMA((13,)),
        "U": V(load.shape, F32), "D": V(density.shape, F32),
        "dens": V(density.shape, F32), "bone": V(bone.shape, jnp.int32), "fixed": V(fixed.shape, jnp.int32),
        "load": V(load.shape, F32),
        "E": V((9, *plane), F32), "R": V((3, DEP, *plane), F32), "R8": V((3, *plane), F32),
        "T": V((10, *plane), F32), "Q": V((DEP, *plane), F32),
        "s0": V((3, 10, *plane), F32), "w0": V((3, 9, *plane), F32),
        "SDs": V((6, 10, *tall), F32), "SDw": V((6, 10, *tall), F32),
        "A": V((6, 9, *plane), F32), "B": V((6, 10, *tall), F32),
        "XSD": V((6, *tall), F32), "XA": V((3, *plane), F32), "XB": V((3, *tall), F32),
        "EX": V(plane, F32), "XE": V(plane, F32), "X0": V(plane, F32), "XH": V(plane, F32), "XL1": V(plane, F32),
        "XEs": V((8, WID), F32), "XEr": V((8, WID), F32), "XDr": V((8, WID), F32),
        "XLs1": V(thin, F32), "XRs1": V(thin, F32), "XLr1": V(thin, F32), "XRr1": V(thin, F32),
        "XLs2": V(thin, F32), "XRs2": V(thin, F32), "XLr2": V(thin, F32), "XRr2": V(thin, F32),
        "XWs": V((64, WID), F32), "XWr": V((72, WID), F32), "XCr": V((8, WID), F32),
        "SE": V((3, DEP, *plane), F32), "own": V((3, 8, WID), F32), "red": V((3, max(GX, 2 * GY, GZ // 2), 8, WID), F32),
        "Wy": V((2, HEI, HEI), BF16), "Wx": V((9, 2, WID, WID), BF16), "W2": V(plane, F32), "WZ": V((DEP, WID), F32), "GD": V((DEP, *plane), F32),
        "G": V((DEP, *plane), F32), "Gup": V((DEP, *plane), F32), "Gdn": V((DEP, *plane), F32),
        "HLs": V((2, 3, *plane), F32), "HRs": V((2, 3, *plane), F32),
        "HLr": V((2, 3, *plane), F32), "HRr": V((2, 3, *plane), F32),
        "RU": V((3, *plane), F32), "RD": V((3, *plane), F32), "F": V((DEP, *plane), F32), "RR": V((2, *plane), F32),
    }
    names = list(scratch)

    def kernel(*refs):
        body(sizes, *refs[:6], dict(zip(names, refs[6:])))

    outer = pl.BlockSpec(memory_space=pltpu.HBM)
    results = pl.pallas_call(
        kernel,
        out_shape=(jax.ShapeDtypeStruct(density.shape, F32), jax.ShapeDtypeStruct(load.shape, F32)),
        in_specs=[outer] * 4,
        out_specs=(outer, outer),
        scratch_shapes=[scratch[n] for n in names],
        compiler_params=pltpu.CompilerParams(
            collective_id=0, has_side_effects=True, vmem_limit_bytes=56 * 1024 * 1024),
    )(density, bone, fixed, load)

    def hand_over(d, u, out_d, out_u, mid_d, mid_u, into, out):
        parts = []
        for k in range(PIECES):
            rows_z = pl.ds(k * (DEP // PIECES), DEP // PIECES)
            parts.append((d.at[0, rows_z], mid_d.at[0, rows_z], out_d.at[0, rows_z]))
            parts += [(u.at[c, 0, rows_z], mid_u.at[c, 0, rows_z], out_u.at[c, 0, rows_z]) for c in range(3)]
        reads = [pltpu.make_async_copy(a, b, into.at[n]) for n, (a, b, _) in enumerate(parts)]
        writes = [pltpu.make_async_copy(b, c, out.at[n]) for n, (_, b, c) in enumerate(parts)]
        for read in reads:
            read.start()
        for read, write in zip(reads, writes):
            read.wait()
            write.start()
        for write in writes:
            write.wait()

    return pl.pallas_call(
        hand_over,
        out_shape=tuple(jax.ShapeDtypeStruct(v.shape, F32) for v in results),
        in_specs=[outer] * 2,
        out_specs=(outer, outer),
        scratch_shapes=[V(density.shape, F32), V(load.shape, F32), pltpu.SemaphoreType.DMA((4 * PIECES,)),
                        pltpu.SemaphoreType.DMA((4 * PIECES,))],
        compiler_params=pltpu.CompilerParams(vmem_limit_bytes=56 * 1024 * 1024),
    )(*results)


def solution(mesh):
    sizes = tuple(mesh.shape[name] for name in ("gx", "gy", "gz"))
    placed = (P("gz", "gy", None, "gx"),) * 3 + (P(None, "gz", "gy", None, "gx"),)
    return jax.shard_map(
        functools.partial(on_device, sizes),
        mesh=mesh,
        in_specs=placed,
        out_specs=(P("gz", "gy", None, "gx"), P(None, "gz", "gy", None, "gx")),
        check_vma=False,
    )
```
